32 devices in a mesh: batch: 4 (over y, x), node: 8 (over z, core).
Axes of the slice: x: 2, y: 2, z: 4, core: 2. Of those that a mesh axis runs over, the one named last changes fastest.
Arguments:
- params: float32 [360448], P(('batch', 'node'))
- moment1: float32 [360448], P(('batch', 'node')), may hold values from -0.0234375 to 0.0234375
- moment2: float32 [360448], P(('batch', 'node')), may hold values from 1.9e-06 to 0.00015
- memory: float32 [4, 65536, 100], P('batch', 'node'), may hold values from -4 to 4
- mailbox: bfloat16 [4, 65536, 386], P('batch', 'node'), may hold values from -4 to 4
- mail_time: int32 [4, 65536], P('batch', 'node'), may hold values from 2048 to 4095
- update_time: int32 [4, 65536], P('batch', 'node'), may hold values from 0 to 2047
- node_feat: bfloat16 [65536, 413], P('node'), may hold values from -4 to 4
- req_rows: int32 [4, 8, 8, 1024], P('batch', 'node'), may hold values from 0 to 8191, as said below
- req_count: int32 [4, 8, 8], P('batch', 'node'), may hold values from 1 to 1024, 4096 in all within a row
- root_live: int32 [4, 8, 3, 512], P('batch', 'node'), may hold values from 0 to 4095, as said below
- nbr_live: int32 [4, 8, 1536, 10], P('batch', 'node'), may hold values from 0 to 4095
- nbr_dt: int32 [4, 8, 1536, 10], P('batch', 'node'), may hold values from 0 to 4095
- nbr_edge: bfloat16 [4, 8, 1536, 10, 186], P('batch', 'node'), may hold values from -4 to 4
- ev_edge: bfloat16 [4, 8, 512, 186], P('batch', 'node'), may hold values from -4 to 4
- ev_time: int32 [4, 8, 512], P('batch', 'node'), may hold values from 4096 to 8191
- neg_count: int32 [4, 8, 512], P('batch', 'node'), may hold values from 1 to 8
Outputs:
- loss_sum: float32 [], replicated
- loss_weight: float32 [], replicated
- grad_norm: float32 [], replicated
- params_new: float32 [360448], P(('batch', 'node'))
- moment1_new: float32 [360448], P(('batch', 'node'))
- moment2_new: float32 [360448], P(('batch', 'node'))
- params_low: bfloat16 [360448], P(('batch', 'node'))
- memory_new: float32 [4, 65536, 100], P('batch', 'node')
- mailbox_new: bfloat16 [4, 65536, 386], P('batch', 'node')
- mail_time_new: int32 [4, 65536], P('batch', 'node')
- update_time_new: int32 [4, 65536], P('batch', 'node')
- memory_grad: float32 [4, 65536, 100], P('batch', 'node')
The draws below stay inside these ranges and needn't reach their ends.
Inputs may be any that keep to these rules, and one draw needn't show every extreme that they name: `req_rows`: within one batch group, the rows that all devices and slots request of one owner are all distinct. `req_count`: live requests of a device to each owner; a device's counts sum to 4096. `root_live`: the 1536 entries of one device are distinct live request indices.
All inputs are finite; a program needn't handle non-finite values.
Results may differ from the reference program's by a relative error of at most 0.012.
The reference program's roundings to bfloat16 on the way count: a program that leaves them out, or rounds other values in their place, can miss the bound.
Values may be sent and summed in bfloat16 or wider, within the bound.
No kernel may reach another device: no remote copies, remote signals or barrier semaphores. Data moves between devices by JAX's collectives and lax.ppermute only.
A program may use at most 256 MiB of HBM per device.

```python
import math
import jax
import jax.numpy as jnp
import numpy as np
from jax import lax

MEM = 100
TENC = 100
EDGE = 186
NFEAT = 413
HEADS = 2
NBR = 10
STEP = 5
EV = 512
LIVE = 4096
CAP = 1024
NODE_DEV = 8192
NODES = 65536
GROUPS = 4
SHARDS = 8
MAIL = 386
FLAT = 360448


def pieces_drawn():
    return [('w_ih', (2 * MEM + EDGE + TENC, 3 * MEM)), ('w_hh', (MEM, 3 * MEM)), ('w_nf', (NFEAT, MEM)), ('w_q', (MEM + TENC, MEM)), ('w_kv', (MEM + EDGE + TENC, 2 * MEM)), ('w_o', (2 * MEM, MEM)), ('w_src', (MEM, MEM)), ('w_dst', (MEM, MEM)), ('w_out', (MEM, 1)), ('b_ih', (3 * MEM,)), ('b_hh', (3 * MEM,)), ('b_o', (MEM,)), ('ln_gain', (MEM,)), ('ln_bias', (MEM,)), ('b_pred', (MEM,)), ('b_out', (1,))]


def draw_params(key, part):
    key = jax.random.fold_in(key, 11)
    parts_list = []
    total = 0
    for number, entry in enumerate(pieces_drawn()):
        piece_name, shape_dims = entry
        sub = jax.random.fold_in(key, number)
        if len(shape_dims) == 2:
            value = jax.random.normal(sub, shape_dims, jnp.float32) * shape_dims[0] ** (-0.5)
        elif piece_name == 'ln_gain':
            value = 1.0 + 0.3 * jax.random.uniform(sub, shape_dims, jnp.float32, -1.0, 1.0)
        else:
            value = 0.3 * jax.random.normal(sub, shape_dims, jnp.float32)
        parts_list.append(value.reshape(-1))
        total = total + value.size
    filler = 0.05 * jax.random.normal(jax.random.fold_in(key, 99), (FLAT - total,), jnp.float32)
    return jnp.concatenate(parts_list + [filler])


def spread_log(key, lower, upper):
    ratio = jax.random.uniform(key, (FLAT,), jnp.float32)
    return jnp.exp(jnp.log(lower) + ratio * (jnp.log(upper) - jnp.log(lower)))


def draw_moment2(key, part):
    key = jax.random.fold_in(key, 14)
    return spread_log(key, 1.9e-06, 7.5e-06)


def draw_req_rows(key, part):
    key = jax.random.fold_in(key, 12)
    keys = jax.random.split(key, GROUPS * SHARDS)
    chosen = jax.vmap(lambda k: jax.random.permutation(k, NODE_DEV)[:SHARDS * CAP])(keys)
    chosen = chosen.reshape(GROUPS, SHARDS, SHARDS, CAP)
    return jnp.transpose(chosen, (0, 2, 1, 3)).astype(jnp.int32)


def draw_root_live(key, part):
    key = jax.random.fold_in(key, 13)
    keys = jax.random.split(key, GROUPS * SHARDS)
    chosen = jax.vmap(lambda k: jax.random.permutation(k, LIVE)[:3 * EV])(keys)
    return chosen.reshape(GROUPS, SHARDS, 3, EV).astype(jnp.int32)


def place_ends(entries, key, low, largest):
    longest = entries.shape.index(max(entries.shape))
    spots = []
    for shift in (0, 1):
        where = [jax.random.randint(jax.random.fold_in(key, axis), (), 0, length) for axis, length in enumerate(entries.shape)]
        where[longest] = (where[longest] + shift) % entries.shape[longest]
        spots.append(tuple(where))
    return entries.at[spots[0]].set(low).at[spots[1]].set(largest)


def level_of(own_key, shape, cuts, low, largest):
    loudness, own = 1.0, jax.random.fold_in(own_key, 6)
    for position, shards_of in cuts:
        steps = jnp.exp(jax.random.uniform(jax.random.fold_in(own, position), (shards_of,), jnp.float32, low / len(cuts), largest / len(cuts)))
        loudness = loudness * jnp.repeat(steps, shape[position] // shards_of).reshape([-1 if axis == position else 1 for axis in range(len(shape))])
    return loudness


def split_up(number_of, total, bound, skew):
    loads = [(1 << 20) // math.isqrt(standing ** skew) + 1 for standing in range(2, number_of + 1)]
    surplus, given = total - bound - (number_of - 1), [1] * (number_of - 1)
    while surplus > 0:
        free = [i for i in range(number_of - 1) if given[i] < bound]
        mass, left = sum([loads[i] for i in free]), surplus
        for i in free:
            addition = min(bound - given[i], max(1, left * loads[i] // mass), surplus)
            given[i] = given[i] + addition
            surplus = surplus - addition
    return np.array([bound] + given)


def ragged_sizes(stream_key, count, total, limit, slope):
    if count == 2:
        one = jax.random.randint(stream_key, (), max(1, total - limit), min(limit, total - 1) + 1)
        return jnp.stack([one, total - one])
    tallies = jnp.asarray(split_up(count, total, limit, slope), jnp.int32)
    couples = (count - 1) // 2
    source_of, taker = tallies[1:1 + 2 * couples:2], tallies[2:2 + 2 * couples:2]
    margin = jnp.minimum(source_of - 1, limit - taker)
    passed = jax.random.randint(jax.random.fold_in(stream_key, 1), (couples,), 0, 1 << 20) % (margin + 1)
    tallies = tallies.at[1:1 + 2 * couples:2].set(source_of - passed).at[2:2 + 2 * couples:2].set(taker + passed)
    return tallies[jax.random.permutation(jax.random.fold_in(stream_key, 2), count)]


def noise(own_key, shape, scale, most, cuts=(), kind=jnp.bfloat16):
    values = scale * jax.random.normal(own_key, shape, jnp.float32)
    if cuts:
        values = values * level_of(own_key, shape, cuts, -0.22, 0.18)
    return jnp.clip(values, -most, most).astype(kind)


def setup_inputs(seed: int = 0) -> dict:
    splits = jax.random.split(jax.random.key(seed), 18)
    params = draw_params(jax.random.fold_in(splits[17], 71), 0)
    moment1 = noise(splits[1], (FLAT,), 0.0017, 0.0234375, ((0, 32),), jnp.float32)
    moment2 = draw_moment2(jax.random.fold_in(splits[17], 71), 0)
    memory = noise(splits[3], (GROUPS, NODES, MEM), 1.0, 4.0, ((0, 4), (1, 8)), jnp.float32)
    mailbox = noise(splits[4], (GROUPS, NODES, MAIL), 1.0, 4.0, ((0, 4), (1, 8)))
    mail_time = place_ends(jax.random.randint(splits[5], (GROUPS, NODES), 2048, 4096), jax.random.fold_in(splits[5], 1), 2048, 4095).astype(jnp.int32)
    update_time = place_ends(jax.random.randint(splits[6], (GROUPS, NODES), 0, 2048), jax.random.fold_in(splits[6], 1), 0, 2047).astype(jnp.int32)
    node_feat = noise(splits[7], (NODES, NFEAT), 1.0, 4.0, ((0, 8),))
    req_rows = draw_req_rows(jax.random.fold_in(splits[17], 71), 0)
    req_count = jax.vmap(lambda own: ragged_sizes(own, SHARDS, LIVE, CAP, 2))(jax.random.split(splits[9], GROUPS * SHARDS)).reshape((GROUPS, SHARDS, SHARDS)).astype(jnp.int32)
    root_live = draw_root_live(jax.random.fold_in(splits[17], 71), 0)
    nbr_live = place_ends(jax.random.randint(splits[11], (GROUPS, SHARDS, 3 * EV, NBR), 0, LIVE), jax.random.fold_in(splits[11], 1), 0, LIVE - 1).astype(jnp.int32)
    nbr_dt = place_ends(jax.random.randint(splits[12], (GROUPS, SHARDS, 3 * EV, NBR), 0, 4096), jax.random.fold_in(splits[12], 1), 0, 4095).astype(jnp.int32)
    nbr_edge = noise(splits[13], (GROUPS, SHARDS, 3 * EV, NBR, EDGE), 1.0, 4.0, ((0, 4), (1, 8)))
    ev_edge = noise(splits[14], (GROUPS, SHARDS, EV, EDGE), 1.0, 4.0, ((0, 4), (1, 8)))
    ev_time = place_ends(jax.random.randint(splits[15], (GROUPS, SHARDS, EV), 4096, 8192), jax.random.fold_in(splits[15], 1), 4096, 8191).astype(jnp.int32)
    neg_count = place_ends(jax.random.randint(splits[16], (GROUPS, SHARDS, EV), 1, 9), jax.random.fold_in(splits[16], 1), 1, 8).astype(jnp.int32)
    return dict(params=params, moment1=moment1, moment2=moment2, memory=memory, mailbox=mailbox, mail_time=mail_time, update_time=update_time, node_feat=node_feat, req_rows=req_rows, req_count=req_count, root_live=root_live, nbr_live=nbr_live, nbr_dt=nbr_dt, nbr_edge=nbr_edge, ev_edge=ev_edge, ev_time=ev_time, neg_count=neg_count)


@jax.custom_vjp
def low(v):
    return lax.optimization_barrier(v.astype(jnp.bfloat16)).astype(jnp.float32)

@jax.custom_vjp
def low_back(v):
    return v

def low_keep(v):
    return (low(v), None)

def low_pass(kept, grad):
    return (grad,)

def back_keep(v):
    return (v, None)

def back_low(kept, grad):
    return (low(grad),)
low.defvjp(low_keep, low_pass)
low_back.defvjp(back_keep, back_low)
clip_limit = 1.0
learn_rate = 0.02
beta_first = 0.5
beta_second = 0.6
adam_floor = 1e-08
decay_rate = 0.01

def pieces():
    return [('w_ih', (2 * MEM + EDGE + TENC, 3 * MEM)), ('w_hh', (MEM, 3 * MEM)), ('w_nf', (NFEAT, MEM)), ('w_q', (MEM + TENC, MEM)), ('w_kv', (MEM + EDGE + TENC, 2 * MEM)), ('w_o', (2 * MEM, MEM)), ('w_src', (MEM, MEM)), ('w_dst', (MEM, MEM)), ('w_out', (MEM, 1)), ('b_ih', (3 * MEM,)), ('b_hh', (3 * MEM,)), ('b_o', (MEM,)), ('ln_gain', (MEM,)), ('ln_bias', (MEM,)), ('b_pred', (MEM,)), ('b_out', (1,))]

def unpack(flat):
    table = {}
    offset = 0
    for piece_name, shape_dims in pieces():
        amount = 1
        for extent in shape_dims:
            amount = amount * extent
        table[piece_name] = flat[offset:offset + amount].reshape(shape_dims)
        offset = offset + amount
    return table

def matmul(left, right):
    return jnp.dot(left, right, precision=lax.Precision.HIGHEST)

def encode(delta):
    freqs = 10.0 ** (-9.0 * jnp.arange(TENC, dtype=jnp.float32) / (TENC - 1))
    return jnp.cos(delta.astype(jnp.float32)[..., None] * freqs)

def gru_gates(gate_in, gate_hid, memory_rows):
    reset = jax.nn.sigmoid(gate_in[:, :MEM] + gate_hid[:, :MEM])
    update = jax.nn.sigmoid(gate_in[:, MEM:2 * MEM] + gate_hid[:, MEM:2 * MEM])
    candidate = jnp.tanh(gate_in[:, 2 * MEM:] + reset * gate_hid[:, 2 * MEM:])
    return (1.0 - update) * candidate + update * memory_rows

def attend(query, keyval):
    rows = query.shape[0]
    width = MEM // HEADS
    keys = keyval[..., :MEM].reshape(rows, NBR, HEADS, width)
    values = keyval[..., MEM:].reshape(rows, NBR, HEADS, width)
    scores = jnp.einsum('nhd,nkhd->nhk', query.reshape(rows, HEADS, width), keys, precision=lax.Precision.HIGHEST) * width ** (-0.5)
    scores = scores - lax.optimization_barrier(jnp.max(scores, -1, keepdims=True))
    weights = jnp.exp(scores)
    weights = weights / lax.optimization_barrier(jnp.sum(weights, -1, keepdims=True))
    return jnp.einsum('nhk,nkhd->nhd', weights, values, precision=lax.Precision.HIGHEST).reshape(rows, MEM)

def norm_act(pre, gain, shift):
    active = jax.nn.gelu(pre)
    centre = active - lax.optimization_barrier(jnp.mean(active, -1, keepdims=True))
    spread = lax.optimization_barrier(jnp.mean(centre * centre, -1, keepdims=True))
    return centre * lax.rsqrt(spread + 1e-05) * gain + shift

def link_loss(pos_logit, neg_logit, weight):
    return jnp.sum(jax.nn.softplus(-pos_logit)) + jnp.sum(weight * jax.nn.softplus(neg_logit))

def device_loss(wts, mem, mail, delta, feat, roots, neighbors, ndelta, nedge, weight):
    mem_low = low(mem)
    xin = jnp.concatenate([mail, low(encode(delta))], -1)
    gate_in = low_back(matmul(xin, wts['w_ih'])) + wts['b_ih']
    gate_hid = low_back(matmul(mem_low, wts['w_hh'])) + wts['b_hh']
    renewed = gru_gates(gate_in, gate_hid, mem_low)
    hidden = low(renewed + low_back(matmul(feat, wts['w_nf'])))
    count_rows = roots.shape[0]
    root_rows = hidden[roots]
    key_in = jnp.concatenate([hidden[neighbors], nedge, low(encode(ndelta))], -1)
    keyval = low_back(matmul(key_in.reshape(count_rows * NBR, -1), wts['w_kv'])).reshape(count_rows, NBR, 2 * MEM)
    query_in = jnp.concatenate([root_rows, jnp.ones((count_rows, TENC), jnp.float32)], -1)
    query = low_back(matmul(query_in, wts['w_q']))
    attended = jax.checkpoint(attend)(query, keyval)
    out_pre = low_back(matmul(jnp.concatenate([low(attended), root_rows], -1), wts['w_o'])) + wts['b_o']
    embed = low(norm_act(out_pre, wts['ln_gain'], wts['ln_bias']))
    src_proj = low_back(matmul(embed[:EV], wts['w_src']))
    dst_proj = low_back(matmul(embed[EV:2 * EV], wts['w_dst']))
    neg_proj = low_back(matmul(embed[2 * EV:], wts['w_dst']))
    pos_act = low(jax.nn.gelu(src_proj + dst_proj + wts['b_pred']))
    neg_act = low(jax.nn.gelu(src_proj + neg_proj + wts['b_pred']))
    pos_logit = low_back(matmul(pos_act, wts['w_out']))[:, 0] + wts['b_out'][0]
    neg_logit = low_back(matmul(neg_act, wts['w_out']))[:, 0] + wts['b_out'][0]
    return (link_loss(pos_logit, neg_logit, weight), renewed)

def reference(params, moment1, moment2, memory, mailbox, mail_time, update_time, node_feat, req_rows, req_count, root_live, nbr_live, nbr_dt, nbr_edge, ev_edge, ev_time, neg_count):
    devices = GROUPS * SHARDS
    index = jnp.arange(LIVE, dtype=jnp.int32)

    def locate(rows, counts):
        upper = jnp.cumsum(counts).astype(jnp.int32)
        lower = upper - counts
        owner = lax.optimization_barrier(jnp.sum((index[:, None] >= upper[None, :]).astype(jnp.int32), 1)).astype(jnp.int32)
        match = owner[:, None] == jnp.arange(SHARDS, dtype=jnp.int32)[None, :]
        start = lax.optimization_barrier(jnp.sum(jnp.where(match, lower[None, :], 0), 1)).astype(jnp.int32)
        return (owner * NODE_DEV + rows[owner, index - start]).astype(jnp.int32)
    node_ids = jax.vmap(locate)(req_rows.reshape(devices, SHARDS, CAP), req_count.reshape(devices, SHARDS))
    group_of = (jnp.arange(devices, dtype=jnp.int32) // SHARDS)[:, None]
    global_ids = (node_ids + group_of * NODES).astype(jnp.int32)
    mem_all = memory.reshape(GROUPS * NODES, MEM)
    mail_all = mailbox.reshape(GROUPS * NODES, MAIL)
    mtime = mail_time.reshape(-1)
    utime = update_time.reshape(-1)
    mem_live = mem_all[global_ids]
    mail_live = mail_all[global_ids].astype(jnp.float32)
    delta = mtime[global_ids] - utime[global_ids]
    feat_live = node_feat[node_ids].astype(jnp.float32)
    roots = root_live.reshape(devices, 3 * EV)
    neighbors = nbr_live.reshape(devices, 3 * EV, NBR)
    ndelta = nbr_dt.reshape(devices, 3 * EV, NBR)
    nedge = nbr_edge.reshape(devices, 3 * EV, NBR, EDGE).astype(jnp.float32)
    weights = neg_count.reshape(devices, EV).astype(jnp.float32)

    def total(flat, mems):
        wts = unpack(low(flat))

        def single(pack):
            return device_loss(wts, *pack)
        losses, renewed = lax.map(jax.checkpoint(single), (mems, mail_live, delta, feat_live, roots, neighbors, ndelta, nedge, weights))
        return (jnp.sum(losses), renewed)
    loss_sum, back_fn, renewed = jax.vjp(total, params, mem_live, has_aux=True)
    grad_flat, grad_mem = back_fn(jnp.ones_like(loss_sum))
    loss_weight = jnp.sum(1.0 + weights)
    grad_norm = jnp.sqrt(jnp.sum(grad_flat * grad_flat))
    clipped = grad_flat * jnp.minimum(1.0, clip_limit / (grad_norm + 1e-06))
    moment1_new = beta_first * moment1 + (1.0 - beta_first) * clipped
    moment2_new = beta_second * moment2 + (1.0 - beta_second) * clipped * clipped
    ratio = moment1_new / (1.0 - beta_first ** STEP) / (jnp.sqrt(moment2_new / (1.0 - beta_second ** STEP)) + adam_floor)
    params_new = params - learn_rate * (ratio + decay_rate * params)
    flat_ids = global_ids.reshape(-1)
    memory_new = mem_all.at[flat_ids].set(renewed.reshape(-1, MEM)).reshape(GROUPS, NODES, MEM)
    memory_grad = jnp.zeros_like(mem_all).at[flat_ids].add(grad_mem.reshape(-1, MEM)).reshape(GROUPS, NODES, MEM)
    src_ids = jnp.take_along_axis(global_ids, roots[:, :EV], 1).reshape(-1)
    dst_ids = jnp.take_along_axis(global_ids, roots[:, EV:2 * EV], 1).reshape(-1)
    src_mem = jnp.take_along_axis(renewed, roots[:, :EV, None], 1)
    dst_mem = jnp.take_along_axis(renewed, roots[:, EV:2 * EV, None], 1)
    edges = ev_edge.reshape(devices, EV, EDGE).astype(jnp.float32)
    mail_src = jnp.concatenate([src_mem, dst_mem, edges], -1).astype(jnp.bfloat16).reshape(-1, MAIL)
    mail_dst = jnp.concatenate([dst_mem, src_mem, edges], -1).astype(jnp.bfloat16).reshape(-1, MAIL)
    mailbox_new = mail_all.at[src_ids].set(mail_src).at[dst_ids].set(mail_dst).reshape(GROUPS, NODES, MAIL)
    stamps = ev_time.reshape(-1)
    mail_time_new = mtime.at[src_ids].set(stamps).at[dst_ids].set(stamps).reshape(GROUPS, NODES)
    update_time_new = utime.at[flat_ids].set(mtime[flat_ids]).reshape(GROUPS, NODES)
    return (loss_sum, loss_weight, grad_norm, params_new, moment1_new, moment2_new, params_new.astype(jnp.bfloat16), memory_new, mailbox_new, mail_time_new, update_time_new, memory_grad)
```

```python
import functools
import math

import jax
import jax.numpy as jnp
import numpy as np
from jax import lax
from jax.experimental import pallas as pl
from jax.experimental.pallas import tpu as pltpu
from jax.sharding import PartitionSpec as P

MEM = 100
TENC = 100
EDGE = 186
NFEAT = 413
NBR = 10
STEP = 5
EV = 512
MAIL = 386
FLAT = 360448

clip_limit = 1.0
learn_rate = 0.02
beta_first = 0.5
beta_second = 0.6
adam_floor = 1e-08
decay_rate = 0.01

F32 = jnp.float32
BF16 = jnp.bfloat16
LANES = 128
PAD = 112
HALF = 56
GATES = 3 * PAD
KV = 4 * HALF
EB = 128
SECT = 3 * EB
STREAMS = 8
VMEM_LIMIT = 60 * 2**20

ROW_HH = 1458
ROW_NF = 1758
ROW_Q = 2171
ROW_KV = 2371
ROW_O = 3143
ROW_SRC = 3343
ROW_DST = 3443
ROW_OUT = 3543
ROW_BIH = 3544
ROW_BHH = 3547
ROW_BO = 3550
ROW_GAIN = 3551
ROW_SHIFT = 3552
ROW_BPRED = 3553
ROW_BOUT = 3554
USED = 355401
FLAT_ROWS = FLAT // LANES
PERIODS = 113
WROWS = 32 * PERIODS
GRU_ROWS = 2176
ATT_BASE = 2168
ATT_ROWS = 1448

FREQS = np.float32(10.0 ** (-9.0 * np.arange(TENC) / (TENC - 1)))

VMEM = pl.BlockSpec(memory_space=pltpu.VMEM)
SMEM = pl.BlockSpec(memory_space=pltpu.SMEM)


def params_of(limit=VMEM_LIMIT):
    return pltpu.CompilerParams(vmem_limit_bytes=limit)


def dot(left, right, left_dim=1, right_dim=0):
    return lax.dot_general(
        left, right, (((left_dim,), (right_dim,)), ((), ())), preferred_element_type=F32
    )


def fit_cosine():
    u = np.cos(np.pi * (np.arange(4000) + 0.5) / 4000) * 0.5 + 0.5
    u = u * (np.pi**2 * 1.002)
    fit = np.polynomial.chebyshev.Chebyshev.fit(u, np.cos(np.sqrt(u)), 7, domain=[0, np.pi**2 * 1.002])
    return [float(np.float32(c)) for c in fit.convert(kind=np.polynomial.Polynomial).coef]


COSINE = fit_cosine()


def cosine(x):
    turns = jnp.floor(x * np.float32(0.5 / np.pi) + 0.5)
    x = x - turns * np.float32(6.28125)
    x = x - turns * np.float32(2 * np.pi - 6.28125)
    u = x * x
    total = jnp.full_like(u, COSINE[-1])
    for c in COSINE[-2::-1]:
        total = total * u + np.float32(c)
    return total


def sigmoid(x):
    return 0.5 * jnp.tanh(0.5 * x) + 0.5


GELU_C = math.sqrt(2.0 / math.pi)


def gelu(x):
    t = jnp.tanh(GELU_C * (x + 0.044715 * (x * x * x)))
    return 0.5 * x * (1.0 + t)


def gelu_slope(x):
    x2 = x * x
    t = jnp.tanh(GELU_C * (x + 0.044715 * (x2 * x)))
    return 0.5 * (1.0 + t) + 0.5 * x * (1.0 - t * t) * (GELU_C * (1.0 + 3 * 0.044715 * x2))


def lane_of(shape):
    return lax.broadcasted_iota(jnp.int32, shape, len(shape) - 1)


def row_of(shape):
    return lax.broadcasted_iota(jnp.int32, shape, len(shape) - 2)


def roll_left(x, amount):
    amount = amount % LANES
    return x if amount == 0 else pltpu.roll(x, LANES - amount, 1)


def spread_heads(x):
    lane = lane_of(x.shape)
    moved = roll_left(x, -6)
    return jnp.where(lane < 50, x, jnp.where((lane >= 56) & (lane < 106), moved, 0.0))


def join_heads(x):
    lane = lane_of(x.shape)
    return jnp.where(lane < 50, x, jnp.where(lane < 100, roll_left(x, 6), 0.0))


def codes_kernel(dt, delta, freq, phi_n, phi_m):
    freqs = freq[...]
    for k in range(NBR):

        def one(i, carry, k=k):
            at = pl.ds(pl.multiple_of(i * LANES, LANES), LANES)
            phi_n[k, :, at] = cosine(dt[k : k + 1, at].astype(F32) * freqs).astype(BF16)
            return carry

        lax.fori_loop(0, dt.shape[1] // LANES, one, 0)

    def other(i, carry):
        at = pl.ds(pl.multiple_of(i * LANES, LANES), LANES)
        phi_m[:, at] = cosine(delta[:, at].astype(F32) * freqs).astype(BF16)
        return carry

    lax.fori_loop(0, delta.shape[1] // LANES, other, 0)


def time_codes(dt, delta):
    freq = jnp.asarray(np.tile(FREQS[:, None], (1, LANES)))
    return pl.pallas_call(
        codes_kernel,
        out_shape=(
            jax.ShapeDtypeStruct((NBR, TENC, dt.shape[1]), BF16),
            jax.ShapeDtypeStruct((TENC, delta.shape[1]), BF16),
        ),
        in_specs=[VMEM] * 3,
        out_specs=(VMEM, VMEM),
        compiler_params=params_of(24 * 2**20),
        cost_estimate=pl.CostEstimate(flops=60_000_000, bytes_accessed=5_000_000, transcendentals=0),
    )(dt, delta, freq)


def weights_kernel(
    flat,
    w_mail,
    w_time,
    w_hid,
    w_feat,
    gate_bias,
    kv_h,
    kv_e,
    kv_t,
    q_h,
    q_one,
    o_att,
    o_att_n,
    o_h,
    src_t,
    src_n,
    dst_t,
    dst_n,
    cols,
    wide,
    rows,
):
    wide[0:FLAT_ROWS, :] = flat[...].astype(F32)
    wide[FLAT_ROWS:, :] = jnp.zeros((wide.shape[0] - FLAT_ROWS, LANES), F32)
    lane = lane_of((PERIODS, LANES))
    for j in range(32):
        first, shift = divmod(100 * j, LANES)
        out = roll_left(wide[pl.ds(first, PERIODS, stride=25), :], shift)
        if shift + 100 > LANES:
            after = roll_left(wide[pl.ds(first + 1, PERIODS, stride=25), :], shift)
            out = jnp.where(lane < LANES - shift, out, after)
        rows[pl.ds(j, PERIODS, stride=32), :] = jnp.where(lane < 100, out, 0.0)

    def turned(start, count, stride=1):
        size = -(-count // LANES) * LANES
        if stride == 1:
            block = rows[start : start + size, :]
        else:
            block = rows[pl.ds(start, size, stride=stride), :]
        return jnp.where(row_of((size, LANES)) < count, block, 0.0).T

    for g in range(3):
        to = slice(PAD * g, PAD * g + PAD)
        w_mail[to, :] = turned(g, MAIL, 3)[:PAD, :MAIL].astype(BF16)
        w_time[to, :] = turned(3 * MAIL + g, TENC, 3)[:PAD, :TENC].astype(BF16)
        w_hid[to, :] = turned(ROW_HH + g, MEM, 3)[:PAD, :MEM].astype(BF16)
    w_feat[...] = turned(ROW_NF, NFEAT)[:PAD, :NFEAT].astype(BF16)

    def column(r):
        return jnp.broadcast_to(rows[r : r + 1, :], (LANES, LANES)).T[:PAD, :]

    for g in range(3):
        gate_bias[0, PAD * g : PAD * g + PAD, :] = column(ROW_BIH + g)
        gate_bias[1, PAD * g : PAD * g + PAD, :] = column(ROW_BHH + g)
    for part in range(2):
        to = slice(PAD * part, PAD * part + PAD)

        def heads(start, count, part=part):
            size = -(-count // LANES) * LANES
            block = spread_heads(rows[pl.ds(ROW_KV + 2 * start + part, size, stride=2), :])
            return jnp.where(row_of((size, LANES)) < count, block, 0.0).T[:PAD]

        kv_h[to, :] = heads(0, MEM).astype(BF16)
        kv_e[to, :] = heads(MEM, EDGE)[:, :EDGE].astype(BF16)
        kv_t[to, :] = heads(MEM + EDGE, TENC)[:, :TENC].astype(BF16)
    q_rows = spread_heads(rows[ROW_Q : ROW_Q + LANES, :])
    keep = row_of((LANES, LANES)) < 100
    q_h[...] = jnp.where(keep, q_rows, 0.0).T[:PAD].astype(BF16)
    q_two = spread_heads(rows[ROW_Q + 100 : ROW_Q + 100 + LANES, :])
    q_sum = jnp.sum(jnp.where(keep, q_two, 0.0), 0, keepdims=True)
    q_one[...] = jnp.broadcast_to(q_sum, (LANES, LANES)).T[:PAD]
    att = spread_heads(turned(ROW_O, 100))
    o_att[...] = att[:PAD, :PAD].astype(BF16)
    o_att_n[...] = att.T[:PAD, :PAD].astype(BF16)
    o_h[...] = turned(ROW_O + 100, 100)[:PAD].astype(BF16)
    for start, out_t, out_n in ((ROW_SRC, src_t, src_n), (ROW_DST, dst_t, dst_n)):
        block = turned(start, 100)
        out_t[...] = block[:PAD, :PAD].astype(BF16)
        out_n[...] = block.T[:PAD, :PAD].astype(BF16)
    for i, r in enumerate((ROW_BO, ROW_GAIN, ROW_SHIFT, ROW_BPRED, ROW_OUT)):
        cols[i, :, :] = column(r)
    first = rows[ROW_BOUT : ROW_BOUT + 1, :]
    value = jnp.sum(jnp.where(lane_of((1, LANES)) == 0, first, 0.0), 1, keepdims=True)
    cols[5, :, :] = jnp.broadcast_to(value, (PAD, LANES))


def weights_of(flat):
    shapes = [
        ((GATES, MAIL), BF16),
        ((GATES, TENC), BF16),
        ((GATES, MEM), BF16),
        ((PAD, NFEAT), BF16),
        ((2, GATES, LANES), F32),
        ((KV, LANES), BF16),
        ((KV, EDGE), BF16),
        ((KV, TENC), BF16),
        ((PAD, LANES), BF16),
        ((PAD, LANES), F32),
        ((PAD, PAD), BF16),
        ((PAD, PAD), BF16),
        ((PAD, LANES), BF16),
        ((PAD, PAD), BF16),
        ((PAD, PAD), BF16),
        ((PAD, PAD), BF16),
        ((PAD, PAD), BF16),
        ((6, PAD, LANES), F32),
    ]
    return pl.pallas_call(
        weights_kernel,
        out_shape=[jax.ShapeDtypeStruct(s, d) for s, d in shapes],
        in_specs=[VMEM],
        out_specs=[VMEM] * len(shapes),
        scratch_shapes=[pltpu.VMEM((FLAT_ROWS + 16, LANES), F32), pltpu.VMEM((WROWS + 512, LANES), F32)],
        compiler_params=params_of(24 * 2**20),
        cost_estimate=pl.CostEstimate(flops=4_000_000, bytes_accessed=2_000_000, transcendentals=0),
    )(flat)


def gather_loop(index, table, out, count, base=0, to=0):
    group = 32

    def step(i, carry):
        for g in range(group // 16):
            at = pl.multiple_of(i * group + g * 16, 16)
            picked = [table[pl.ds(index[base + at + u], 1), :] for u in range(16)]
            out[pl.ds(to + at, 16), :] = jnp.concatenate(picked, 0).astype(out.dtype)
        return carry

    lax.fori_loop(0, count // group, step, 0)


def gru_products(mail, phi, feat, w_mail, w_time, w_hid, w_feat, low, gi, gh, nf):
    gi[...] = dot(w_mail[...], mail[...]) + dot(w_time[...], phi[...])
    gh[...] = dot(w_hid[...], low)
    if nf is not None:
        nf[...] = dot(w_feat[...], feat[...])


def gates_at(at, gi, gh, bias, kept):
    gr, gz, gn = (gi[PAD * g : PAD * g + PAD, at] + bias[0, PAD * g : PAD * g + PAD, :] for g in range(3))
    hr, hz, hn = (gh[PAD * g : PAD * g + PAD, at] + bias[1, PAD * g : PAD * g + PAD, :] for g in range(3))
    r = sigmoid(gr + hr)
    z = sigmoid(gz + hz)
    n = jnp.tanh(gn + r * hn)
    s = kept[:, at]
    return r, z, n, hn, s, (1.0 - z) * n + z * s


def to_rows(block):
    full = jnp.concatenate([block, jnp.zeros((LANES - PAD, LANES), F32)], 0)
    return full.T


def load_memory(mem, kept):
    low = mem[...].astype(BF16)
    kept[0:MEM, :] = low.astype(F32)
    kept[MEM:, :] = jnp.zeros((PAD - MEM, kept.shape[1]), F32)
    return low


def gru_kernel(
    index, mail, phi, mem, feat, w_mail, w_time, w_hid, w_feat, bias, sent, s_rows, s_cols, table, kept, gi, gh, nf
):
    block = mail.shape[1]
    step = pl.program_id(0)
    low = load_memory(mem, kept)
    gru_products(mail, phi, feat, w_mail, w_time, w_hid, w_feat, low, gi, gh, nf)

    def piece(i, carry):
        start = pl.multiple_of(i * LANES, LANES)
        at = pl.ds(start, LANES)
        _, _, _, _, _, renewed = gates_at(at, gi, gh, bias, kept)
        hidden = (renewed + nf[:, at]).astype(BF16).astype(F32)
        table[pl.ds(pl.multiple_of(step * block + start, LANES), LANES), :] = to_rows(hidden)
        s_rows[at, :] = to_rows(renewed)
        s_cols[:, at] = renewed[:MEM].astype(BF16)
        return carry

    lax.fori_loop(0, block // LANES, piece, 0)

    @pl.when(step == pl.num_programs(0) - 1)
    def _():
        gather_loop(index, table, sent, sent.shape[0])


def gru_specs(block):
    def cols(rows):
        return pl.BlockSpec((rows, block), lambda i: (0, i))

    return [cols(MAIL), cols(TENC), cols(MEM), cols(NFEAT)]


def gru_forward(index, mail, phi, mem, feat, wts, count):
    rows = mail.shape[1]
    block = 1024
    return pl.pallas_call(
        gru_kernel,
        grid=(rows // block,),
        out_shape=(
            jax.ShapeDtypeStruct((count, LANES), BF16),
            jax.ShapeDtypeStruct((rows, LANES), F32),
            jax.ShapeDtypeStruct((MEM, rows), BF16),
        ),
        in_specs=[SMEM] + gru_specs(block) + [VMEM] * 5,
        out_specs=(
            VMEM,
            pl.BlockSpec((block, LANES), lambda i: (i, 0)),
            pl.BlockSpec((MEM, block), lambda i: (0, i)),
        ),
        scratch_shapes=[
            pltpu.VMEM((rows, LANES), F32),
            pltpu.VMEM((PAD, block), F32),
            pltpu.VMEM((GATES, block), F32),
            pltpu.VMEM((GATES, block), F32),
            pltpu.VMEM((PAD, block), F32),
        ],
        compiler_params=params_of(48 * 2**20),
        cost_estimate=pl.CostEstimate(flops=4_000_000_000, bytes_accessed=24_000_000, transcendentals=3_000_000),
    )(index, mail, phi, mem, feat, *wts[:5])


def gather_kernel(index, table, out, wide):
    if table.dtype != F32:
        wide[...] = table[...].astype(F32)
        table = wide
    gather_loop(index, table, out, out.shape[0])


def gather_rows(table, index):
    return pl.pallas_call(
        gather_kernel,
        out_shape=jax.ShapeDtypeStruct((index.shape[0], LANES), BF16),
        in_specs=[SMEM, VMEM],
        out_specs=VMEM,
        scratch_shapes=[pltpu.VMEM(table.shape if table.dtype != F32 else (8, LANES), F32)],
        compiler_params=params_of(24 * 2**20),
        cost_estimate=pl.CostEstimate(
            flops=index.shape[0] * 1000, bytes_accessed=6_000_000, transcendentals=0
        ),
    )(index, table)


def gru_back_kernel(
    index,
    got,
    mail,
    phi,
    mem,
    feat,
    mail_time,
    update_time,
    w_mail,
    w_time,
    w_hid,
    bias,
    mem_new,
    mem_grad,
    time_new,
    grads,
    biases,
    wide,
    placed,
    kept,
    gi,
    gh,
    d_in,
    d_hid,
    d_low,
    direct,
    a_mail,
    a_time,
    a_hid,
    a_feat,
    a_bin,
    a_bhid,
):
    block = mail.shape[1]
    step = pl.program_id(0)

    @pl.when(step == 0)
    def _():
        wide[...] = got[...].astype(F32)
        if got.shape[0] != placed.shape[0]:
            placed[...] = jnp.zeros_like(placed)
        group = 32

        def move(i, carry):
            for u in range(group):
                at = i * group + u
                placed[pl.ds(index[at], 1), :] = wide[pl.ds(at, 1), :]
            return carry

        lax.fori_loop(0, got.shape[0] // group, move, 0)
        for ref in (a_mail, a_time, a_hid, a_feat, a_bin, a_bhid):
            ref[...] = jnp.zeros_like(ref)

    low = load_memory(mem, kept)
    gru_products(mail, phi, None, w_mail, w_time, w_hid, None, low, gi, gh, None)
    real = row_of((PAD, LANES)) < MEM

    def piece(i, carry):
        start = pl.multiple_of(i * LANES, LANES)
        at = pl.ds(start, LANES)
        r, z, n, hn, s, renewed = gates_at(at, gi, gh, bias, kept)
        turned = placed[pl.ds(pl.multiple_of(step * block + start, LANES), LANES), :].T
        live = turned[MEM : MEM + 1, :] > 0.5
        d = jnp.where(real, turned[:PAD], 0.0)
        d_low[:, at] = d.astype(BF16)
        dn = d * (1.0 - z) * (1.0 - n * n)
        dr = dn * hn * r * (1.0 - r)
        dz = d * (s - n) * z * (1.0 - z)
        dhn = dn * r
        direct[:, at] = d * z
        low_r, low_z = dr.astype(BF16), dz.astype(BF16)
        d_in[0:PAD, at] = low_r
        d_in[PAD : 2 * PAD, at] = low_z
        d_in[2 * PAD : 3 * PAD, at] = dn.astype(BF16)
        d_hid[0:PAD, at] = low_r
        d_hid[PAD : 2 * PAD, at] = low_z
        d_hid[2 * PAD : 3 * PAD, at] = dhn.astype(BF16)
        a_bin[0:PAD, :] += dr
        a_bin[PAD : 2 * PAD, :] += dz
        a_bin[2 * PAD : 3 * PAD, :] += dn
        a_bhid[...] += dhn
        mem_new[:, at] = jnp.where(live, renewed[:MEM], mem[:, at])
        time_new[:, at] = jnp.where(live, mail_time[:, at], update_time[:, at])
        return carry

    lax.fori_loop(0, block // LANES, piece, 0)
    din, dhid = d_in[...], d_hid[...]
    a_mail[:, :MAIL] += dot(din, mail[...], 1, 1)
    a_time[:, :TENC] += dot(din, phi[...], 1, 1)
    a_hid[:, :MEM] += dot(dhid, low, 1, 1)
    a_feat[:, :NFEAT] += dot(d_low[...], feat[...], 1, 1)
    mem_grad[...] = direct[0:MEM, :] + dot(w_hid[...], dhid, 0, 0)

    @pl.when(step == pl.num_programs(0) - 1)
    def _():
        def turned_back(ref, g):
            part = ref[PAD * g : PAD * g + PAD, :]
            return jnp.concatenate([part, jnp.zeros((LANES - PAD, part.shape[1]), F32)], 0).T

        grads[ROW_Q:GRU_ROWS, :] = jnp.zeros((GRU_ROWS - ROW_Q, LANES), F32)
        for g in range(3):
            grads[pl.ds(g, MAIL, stride=3), :] = turned_back(a_mail, g)[:MAIL]
            grads[pl.ds(3 * MAIL + g, TENC, stride=3), :] = turned_back(a_time, g)[:TENC]
            grads[pl.ds(ROW_HH + g, MEM, stride=3), :] = turned_back(a_hid, g)[:MEM]
        grads[ROW_NF:ROW_Q, :] = turned_back(a_feat, 0)[:NFEAT]
        sums = []
        for ref, g in ((a_bin, 0), (a_bin, 1), (a_bin, 2), (a_bin, 0), (a_bin, 1), (a_bhid, 0)):
            sums.append(jnp.sum(turned_back(ref, g), 0, keepdims=True))
        biases[...] = jnp.concatenate(sums + [jnp.zeros((2, LANES), F32)], 0)


def gru_backward(index, got, mail, phi, mem, feat, mail_time, update_time, wts):
    rows = mail.shape[1]
    block = 1024
    one = pl.BlockSpec((1, block), lambda i: (0, i))
    hundred = pl.BlockSpec((MEM, block), lambda i: (0, i))
    return pl.pallas_call(
        gru_back_kernel,
        grid=(rows // block,),
        out_shape=(
            jax.ShapeDtypeStruct((MEM, rows), F32),
            jax.ShapeDtypeStruct((MEM, rows), F32),
            jax.ShapeDtypeStruct((1, rows), jnp.int32),
            jax.ShapeDtypeStruct((GRU_ROWS, LANES), F32),
            jax.ShapeDtypeStruct((8, LANES), F32),
        ),
        in_specs=[SMEM, VMEM] + gru_specs(block) + [one, one] + [VMEM] * 4,
        out_specs=(hundred, hundred, one, VMEM, VMEM),
        scratch_shapes=[
            pltpu.VMEM(got.shape, F32),
            pltpu.VMEM((rows, LANES), F32),
            pltpu.VMEM((PAD, block), F32),
            pltpu.VMEM((GATES, block), F32),
            pltpu.VMEM((GATES, block), F32),
            pltpu.VMEM((GATES, block), BF16),
            pltpu.VMEM((GATES, block), BF16),
            pltpu.VMEM((PAD, block), BF16),
            pltpu.VMEM((PAD, block), F32),
            pltpu.VMEM((GATES, 512), F32),
            pltpu.VMEM((GATES, LANES), F32),
            pltpu.VMEM((GATES, LANES), F32),
            pltpu.VMEM((PAD, 512), F32),
            pltpu.VMEM((GATES, LANES), F32),
            pltpu.VMEM((PAD, LANES), F32),
        ],
        compiler_params=params_of(),
        cost_estimate=pl.CostEstimate(flops=7_000_000_000, bytes_accessed=28_000_000, transcendentals=3_000_000),
    )(index, got, mail, phi, mem, feat, mail_time, update_time, wts[0], wts[1], wts[2], wts[4])


def attention_kernel(
    index,
    counts,
    got,
    e0,
    e1,
    e2,
    p0,
    p1,
    p2,
    weight,
    kv_h,
    kv_e,
    kv_t,
    q_h,
    q_one,
    o_att,
    o_att_n,
    o_h,
    src_t,
    src_n,
    dst_t,
    dst_n,
    cols,
    sent,
    grads,
    losses,
    table,
    picked,
    kv,
    d_rows,
    a_kvh,
    a_kve,
    a_kvt,
    a_qh,
    a_q1,
    a_oa,
    a_oh,
    a_src,
    a_dst,
    a_col,
    a_one,
    *lanes,
):
    step = pl.program_id(0)
    near = NBR * SECT
    total = near + SECT
    scale = 50 ** (-0.5)
    sums = (a_kvh, a_kve, a_kvt, a_qh, a_q1, a_oa, a_oh, a_src, a_dst, a_col, a_one)

    @pl.when(step == 0)
    def _():
        table[...] = got[...].astype(F32)
        for ref in sums + lanes:
            ref[...] = jnp.zeros_like(ref)

    gather_loop(index, table, picked, total, step * total)
    roots = picked[near:total, :]

    def edge_of(k):
        return jnp.concatenate([e0[k], e1[k], e2[k]], 1)

    def code_of(k):
        return jnp.concatenate([p0[k], p1[k], p2[k]], 1)

    for k in range(NBR):
        kv[k] = (
            dot(kv_h[...], picked[k * SECT : k * SECT + SECT, :], 1, 1)
            + dot(kv_e[...], edge_of(k))
            + dot(kv_t[...], code_of(k))
        )
    query = dot(q_h[...], roots, 1, 1)
    o_root = dot(o_h[...], roots, 1, 1)
    bo, gain, shift, bpred, wout = (cols[i] for i in range(5))
    bout = cols[5, 0:1, :]
    real = row_of((PAD, LANES)) < MEM
    queries, probs, atts, pres, embs, norms = [], [], [], [], [], []
    for t in range(3):
        at = slice(t * EB, t * EB + EB)
        q = query[:, at] + q_one[...]
        scores = [[], []]
        for k in range(NBR):
            both = q * kv[k, 0:PAD, at]
            for h in range(2):
                scores[h].append(jnp.sum(both[h * HALF : h * HALF + HALF], 0, keepdims=True) * scale)
        weights = []
        for h in range(2):
            top = functools.reduce(jnp.maximum, scores[h])
            parts = [jnp.exp(x - top) for x in scores[h]]
            whole = functools.reduce(jnp.add, parts)
            weights.append([x / whole for x in parts])
        heads = []
        for h in range(2):
            rows = slice(PAD + h * HALF, PAD + h * HALF + HALF)
            heads.append(
                functools.reduce(jnp.add, [weights[h][k] * kv[k, rows, at] for k in range(NBR)])
            )
        att = jnp.concatenate(heads, 0).astype(BF16)
        pre = dot(o_att[...], att) + o_root[:, at] + bo
        active = gelu(pre)
        mean = jnp.sum(active, 0, keepdims=True) * (1.0 / MEM)
        centre = jnp.where(real, active - mean, 0.0)
        spread = jnp.sum(centre * centre, 0, keepdims=True) * (1.0 / MEM)
        inverse = lax.rsqrt(spread + 1e-05)
        hat = centre * inverse
        queries.append(q)
        probs.append(weights)
        atts.append(att)
        pres.append(pre)
        norms.append((hat, inverse))
        embs.append((hat * gain + shift).astype(BF16))

    src_proj = dot(src_t[...], embs[0]) + bpred
    tails = [src_proj + dot(dst_t[...], embs[1]), src_proj + dot(dst_t[...], embs[2])]
    acts = [gelu(x).astype(BF16) for x in tails]
    logits = [jnp.sum(x.astype(F32) * wout, 0, keepdims=True) + bout for x in acts]
    neg_weight = weight[...].astype(F32)

    def softplus(x):
        return jnp.maximum(x, 0.0) + jnp.log1p(jnp.exp(-jnp.abs(x)))

    d_pos = -sigmoid(-logits[0])
    d_neg = neg_weight * sigmoid(logits[1])
    a_one[0:1, :] += softplus(-logits[0]) + neg_weight * softplus(logits[1])
    a_one[1:2, :] += 1.0 + neg_weight
    a_one[2:3, :] += d_pos + d_neg
    d_logits = [x.astype(BF16).astype(F32) for x in (d_pos, d_neg)]
    a_col[4] += acts[0].astype(F32) * d_logits[0] + acts[1].astype(F32) * d_logits[1]
    d_tails = [wout * d * gelu_slope(x) for d, x in zip(d_logits, tails)]
    d_src = d_tails[0] + d_tails[1]
    a_col[3] += d_src
    d_low = [x.astype(BF16) for x in (d_src, d_tails[0], d_tails[1])]
    a_src[...] += dot(embs[0], d_low[0], 1, 1)
    a_dst[...] += dot(embs[1], d_low[1], 1, 1) + dot(embs[2], d_low[2], 1, 1)
    d_embs = [dot(src_n[...], d_low[0]), dot(dst_n[...], d_low[1]), dot(dst_n[...], d_low[2])]

    d_outs, d_queries = [], []
    for t in range(3):
        at = slice(t * EB, t * EB + EB)
        hat, inverse = norms[t]
        d_emb = d_embs[t]
        a_col[1] += d_emb * hat
        a_col[2] += d_emb
        d_hat = d_emb * gain
        mean = jnp.sum(d_hat, 0, keepdims=True) * (1.0 / MEM)
        mixed = jnp.sum(d_hat * hat, 0, keepdims=True) * (1.0 / MEM)
        d_active = jnp.where(real, inverse * (d_hat - mean - hat * mixed), 0.0)
        d_out = d_active * gelu_slope(pres[t])
        a_col[0] += d_out
        d_out_low = d_out.astype(BF16)
        d_outs.append(d_out_low)
        a_oa[...] += dot(d_out_low, atts[t], 1, 1)
        d_att = dot(o_att_n[...], d_out_low)
        q = queries[t]
        d_q = jnp.zeros((PAD, EB), F32)
        slopes = [[], []]
        for h in range(2):
            rows = slice(PAD + h * HALF, PAD + h * HALF + HALF)
            d_head = d_att[h * HALF : h * HALF + HALF]
            dp = [jnp.sum(d_head * kv[k, rows, at], 0, keepdims=True) for k in range(NBR)]
            mid = functools.reduce(jnp.add, [a * b for a, b in zip(dp, probs[t][h])])
            slopes[h] = [probs[t][h][k] * (dp[k] - mid) * scale for k in range(NBR)]
        for k in range(NBR):
            keys = kv[k, 0:PAD, at]
            factor = jnp.concatenate(
                [jnp.broadcast_to(slopes[h][k], (HALF, EB)) for h in range(2)], 0
            )
            share = jnp.concatenate(
                [jnp.broadcast_to(probs[t][h][k], (HALF, EB)) for h in range(2)], 0
            )
            d_q = d_q + factor * keys
            kv[k, 0:PAD, at] = factor * q
            kv[k, PAD:KV, at] = share * d_att
        d_queries.append(d_q)
        a_q1[...] += d_q.astype(BF16).astype(F32)

    d_out_all = jnp.concatenate(d_outs, 1)
    d_q_all = jnp.concatenate(d_queries, 1).astype(BF16)
    a_oh[...] += dot(d_out_all, roots)
    a_qh[...] += dot(d_q_all, roots)
    d_rows[near:total, :] = dot(d_out_all, o_h[...], 0, 0) + dot(d_q_all, q_h[...], 0, 0)
    for k in range(NBR):
        at = slice(k * SECT, k * SECT + SECT)
        d_kv = kv[k].astype(BF16)
        a_kvh[...] += dot(d_kv, picked[at, :])
        a_kve[:, :EDGE] += dot(d_kv, edge_of(k), 1, 1)
        a_kvt[:, :TENC] += dot(d_kv, code_of(k), 1, 1)
        d_rows[at, :] = dot(d_kv, kv_h[...], 0, 0)

    per = total // STREAMS
    base = step * total

    def add_rows(i, carry):
        for u in range(4):
            for s in range(STREAMS):
                at = s * per + i * 4 + u
                to = pl.ds(index[base + at], 1)
                lanes[s][to, :] += d_rows[pl.ds(at, 1), :]
        return carry

    lax.fori_loop(0, per // 4, add_rows, 0)

    @pl.when(step == pl.num_programs(0) - 1)
    def _():
        owners = counts.shape[0]
        slots = sent.shape[0] // owners
        piece = min(slots, LANES)

        def finish(i, carry):
            start = pl.multiple_of(i * piece, piece)
            at = pl.ds(start, piece)
            whole = functools.reduce(jnp.add, [ref[at, :] for ref in lanes])
            owner = start // slots
            slot = start - owner * slots + row_of((piece, LANES))
            lane = lane_of((piece, LANES))
            live = jnp.where((lane == MEM) & (slot < counts[owner]), 1.0, 0.0)
            sent[at, :] = jnp.where(lane < MEM, whole, live).astype(BF16)
            return carry

        lax.fori_loop(0, sent.shape[0] // piece, finish, 0)
        base_row = ATT_BASE

        def turned(block):
            short = -block.shape[0] % LANES
            if short:
                block = jnp.concatenate([block, jnp.zeros((short, block.shape[1]), F32)], 0)
            return block.T

        grads[...] = jnp.zeros_like(grads)
        q = ROW_Q - base_row
        grads[q : q + 100, :] = join_heads(turned(a_qh[...]))[:100]
        ones = jnp.sum(turned(a_q1[...]), 0, keepdims=True)
        grads[q + 100 : q + 200, :] = jnp.broadcast_to(join_heads(ones), (100, LANES))
        for part in range(2):
            rows = slice(PAD * part, PAD * part + PAD)
            start = ROW_KV - base_row + part
            grads[pl.ds(start, MEM, stride=2), :] = join_heads(turned(a_kvh[rows, :]))[:MEM]
            grads[pl.ds(start + 2 * MEM, EDGE, stride=2), :] = join_heads(turned(a_kve[rows, :]))[:EDGE]
            grads[pl.ds(start + 2 * (MEM + EDGE), TENC, stride=2), :] = join_heads(
                turned(a_kvt[rows, :])
            )[:TENC]
        o = ROW_O - base_row
        wide = jnp.concatenate([a_oa[...], jnp.zeros((PAD, LANES - PAD), F32)], 1)
        grads[o : o + 100, :] = turned(join_heads(wide))[:100]
        grads[o + 100 : o + 200, :] = turned(a_oh[...])[:100]
        for start, ref in ((ROW_SRC, a_src), (ROW_DST, a_dst)):
            wide = jnp.concatenate([ref[...], jnp.zeros((PAD, LANES - PAD), F32)], 1)
            grads[start - base_row : start - base_row + 100, :] = wide[:100]
        for i, r in enumerate((ROW_BO, ROW_GAIN, ROW_SHIFT, ROW_BPRED, ROW_OUT)):
            line = jnp.sum(turned(a_col[i]), 0, keepdims=True)
            grads[r - base_row : r - base_row + 1, :] = line
        line = jnp.where(
            lane_of((1, LANES)) == 0, jnp.sum(a_one[2:3, :], 1, keepdims=True), 0.0
        )
        grads[ROW_BOUT - base_row : ROW_BOUT - base_row + 1, :] = line
        losses[...] = jnp.broadcast_to(jnp.sum(a_one[...], 1, keepdims=True), (8, LANES))


def attention(index, counts, got, edges, codes, weight, wts):
    roots = edges.shape[2]
    blocks = roots // SECT

    def section(rows, t):
        return pl.BlockSpec((NBR, rows, EB), lambda b: (0, 0, t * blocks + b))

    slots = got.shape[0]
    total = (NBR + 1) * SECT
    return pl.pallas_call(
        attention_kernel,
        grid=(blocks,),
        out_shape=(
            jax.ShapeDtypeStruct((slots, LANES), BF16),
            jax.ShapeDtypeStruct((ATT_ROWS, LANES), F32),
            jax.ShapeDtypeStruct((8, LANES), F32),
        ),
        in_specs=[SMEM, SMEM, VMEM]
        + [section(EDGE, t) for t in range(3)]
        + [section(TENC, t) for t in range(3)]
        + [pl.BlockSpec((1, EB), lambda b: (0, b))]
        + [VMEM] * 13,
        out_specs=(VMEM, VMEM, VMEM),
        scratch_shapes=[
            pltpu.VMEM((slots, LANES), F32),
            pltpu.VMEM((total, LANES), BF16),
            pltpu.VMEM((NBR, KV, SECT), F32),
            pltpu.VMEM((total, LANES), F32),
            pltpu.VMEM((KV, LANES), F32),
            pltpu.VMEM((KV, 256), F32),
            pltpu.VMEM((KV, LANES), F32),
            pltpu.VMEM((PAD, LANES), F32),
            pltpu.VMEM((PAD, LANES), F32),
            pltpu.VMEM((PAD, PAD), F32),
            pltpu.VMEM((PAD, LANES), F32),
            pltpu.VMEM((PAD, PAD), F32),
            pltpu.VMEM((PAD, PAD), F32),
            pltpu.VMEM((5, PAD, LANES), F32),
            pltpu.VMEM((8, LANES), F32),
        ]
        + [pltpu.VMEM((slots, LANES), F32) for _ in range(STREAMS)],
        compiler_params=params_of(),
        cost_estimate=pl.CostEstimate(flops=9_000_000_000, bytes_accessed=20_000_000, transcendentals=1_000_000),
    )(index, counts, got, edges, edges, edges, codes, codes, codes, weight, *wts[5:])


def pack_kernel(gru, bias, att, losses, out, rows):
    rows[0:GRU_ROWS, :] = gru[...]
    rows[GRU_ROWS : ATT_BASE + ATT_ROWS, :] = att[8:, :]
    rows[ATT_BASE:GRU_ROWS, :] += att[0:8, :]
    rows[ROW_BIH : ROW_BIH + 8, :] += bias[...]
    rows[ATT_BASE + ATT_ROWS :, :] = jnp.zeros((rows.shape[0] - ATT_BASE - ATT_ROWS, LANES), F32)
    lane = lane_of((PERIODS, LANES))
    for m in range(25):
        first, shift = divmod(LANES * m, 100)
        value = None
        filled = 0
        source = first
        while filled < LANES:
            amount = shift if filled == 0 else -filled
            block = roll_left(rows[pl.ds(source, PERIODS, stride=32), :], amount)
            value = block if value is None else jnp.where(lane < filled, value, block)
            filled += 100 - (shift if filled == 0 else 0)
            source += 1
        out[pl.ds(m, PERIODS, stride=25), :] = value
    first, at = divmod(USED, LANES)
    tail = out.shape[0] - first
    where = row_of((tail, LANES)) * LANES + lane_of((tail, LANES))
    value = jnp.where(where < at, out[first:, :], 0.0)
    value = jnp.where(where == at, losses[0:1, :], value)
    value = jnp.where(where == at + 1, losses[1:2, :], value)
    out[first:, :] = value


def pack(gru, bias, att, losses):
    return pl.pallas_call(
        pack_kernel,
        out_shape=jax.ShapeDtypeStruct((25 * PERIODS + 7, LANES), F32),
        in_specs=[VMEM] * 4,
        out_specs=VMEM,
        scratch_shapes=[pltpu.VMEM((WROWS + 8, LANES), F32)],
        compiler_params=params_of(16 * 2**20),
        cost_estimate=pl.CostEstimate(flops=2_000_000, bytes_accessed=4_000_000, transcendentals=0),
    )(gru, bias, att, losses)


def mail_kernel(
    starts,
    rows,
    events,
    partner,
    edges,
    stamps,
    own,
    mailbox,
    mail_time,
    mail_new,
    time_new,
    near,
    far,
    kept,
    stage,
    lines,
):
    step = pl.program_id(0)
    senders = rows.shape[0] // (2 * EV)

    @pl.when(step == 0)
    def _():
        kept[...] = jnp.zeros_like(kept)
        stage[...] = jnp.zeros_like(stage)
        stage[EDGE + 1 : EDGE + 2, :] = jnp.ones((1, EV), F32)

    @pl.when(step < senders)
    def _():
        near[...] = partner[0].astype(F32)
        stage[0:EDGE, :] = edges[0].astype(F32)
        stage[EDGE : EDGE + 1, :] = stamps[0].astype(F32)
        for part in range(2):
            far[part] = stage[LANES * part : LANES * part + LANES, :].T

        def move(i, carry):
            place = step * 2 * EV + i
            to = pl.ds(rows[place], 1)
            event = pl.ds(events[place], 1)
            kept[0, to, :] = near[pl.ds(i, 1), :]
            kept[1, to, :] = far[0, event, :]
            kept[2, to, :] = far[1, event, :]
            return carry

        lax.fori_loop(starts[2 * step], starts[2 * step + 1], move, 0)

    @pl.when(step >= senders)
    def _():
        block = mailbox.shape[1]
        at = pl.ds(pl.multiple_of((step - senders) * block, LANES), block)
        last = kept[2, at, :].T
        stamp = EDGE - LANES
        has = last[stamp + 1 : stamp + 2, :] > 0.5
        lines[0:MEM, :] = own[...].astype(F32)
        lines[MEM : 2 * MEM, :] = kept[0, at, :].T[0:MEM]
        lines[2 * MEM : 2 * MEM + LANES, :] = kept[1, at, :].T
        lines[2 * MEM + LANES : MAIL, :] = last[0:stamp]
        mail_new[...] = jnp.where(has, lines[0:MAIL, :], mailbox[...].astype(F32)).astype(BF16)
        time_new[...] = jnp.where(has, last[stamp : stamp + 1, :].astype(jnp.int32), mail_time[...])


def deliver(starts, rows, events, partner, edges, stamps, own, mailbox, mail_time):
    senders = partner.shape[0]
    nodes = mailbox.shape[1]
    block = 1024

    def sender(i):
        return (jnp.minimum(i, senders - 1), 0, 0)

    def cols(count):
        return pl.BlockSpec((count, block), lambda i: (0, jnp.maximum(i - senders, 0)))

    return pl.pallas_call(
        mail_kernel,
        grid=(senders + nodes // block,),
        out_shape=(
            jax.ShapeDtypeStruct((MAIL, nodes), BF16),
            jax.ShapeDtypeStruct((1, nodes), jnp.int32),
        ),
        in_specs=[
            SMEM,
            SMEM,
            SMEM,
            pl.BlockSpec((1, 2 * EV, LANES), sender),
            pl.BlockSpec((1, EDGE, EV), sender),
            pl.BlockSpec((1, 1, EV), sender),
            cols(MEM),
            cols(MAIL),
            cols(1),
        ],
        out_specs=(cols(MAIL), cols(1)),
        scratch_shapes=[
            pltpu.VMEM((2 * EV, LANES), F32),
            pltpu.VMEM((2, EV, LANES), F32),
            pltpu.VMEM((3, nodes, LANES), F32),
            pltpu.VMEM((2 * LANES, EV), F32),
            pltpu.VMEM((MAIL + 6, block), F32),
        ],
        compiler_params=params_of(48 * 2**20),
        cost_estimate=pl.CostEstimate(flops=20_000_000, bytes_accessed=16_000_000, transcendentals=0),
    )(starts, rows, events, partner, edges, stamps, own, mailbox, mail_time)


def flip(x, axis, mask):
    return lax.ppermute(x, axis, [(i, i ^ mask) for i in range(lax.axis_size(axis))])


def axis_bits():
    table = []
    for axis in ("batch", "node"):
        count = lax.axis_size(axis).bit_length() - 1
        for b in reversed(range(count)):
            table.append((axis, 1 << b))
    return table


def bit_of(axis, mask):
    return (lax.axis_index(axis) & mask) != 0


def gather_params(x):
    table = axis_bits()
    order = [i for i, (a, m) in enumerate(table) if a == "node" and m > 1]
    order += [i for i, (a, m) in enumerate(table) if a == "batch"][::-1]
    order += [len(table) - 1]
    shape = x.shape
    x = x.reshape((1,) * len(table) + shape)
    for i in order:
        axis, mask = table[i]
        y = flip(x, axis, mask)
        bit = bit_of(axis, mask)
        x = jnp.concatenate([jnp.where(bit, y, x), jnp.where(bit, x, y)], i)
    return x.reshape((-1,) + shape[1:])


def scatter_sum(x):
    table = axis_bits()
    order = [len(table) - 1]
    order += [i for i, (a, m) in enumerate(table) if a == "batch"]
    order += [i for i, (a, m) in enumerate(table) if a == "node" and m > 1][::-1]
    x = x.reshape((2,) * len(table) + (-1, LANES))
    for i in order:
        axis, mask = table[i]
        bit = bit_of(axis, mask).astype(jnp.int32)
        away = lax.dynamic_slice_in_dim(x, 1 - bit, 1, i)
        x = lax.dynamic_slice_in_dim(x, bit, 1, i) + flip(away, axis, mask)
    return x.reshape(-1, LANES)


def sum_all(x):
    for axis, mask in axis_bits()[::-1]:
        x = x + flip(x, axis, mask)
    return x


def swap(x):
    return lax.all_to_all(x, "node", split_axis=0, concat_axis=0, tiled=True)


def to_slot(live, counts, slots):
    upper = jnp.cumsum(counts)
    shape = (-1,) + (1,) * live.ndim
    passed = live[None] >= upper.reshape(shape)
    return live + jnp.sum(jnp.where(passed, (slots - counts).reshape(shape), 0), 0)


def body(
    params,
    moment1,
    moment2,
    memory,
    mailbox,
    mail_time,
    update_time,
    node_feat,
    req_rows,
    req_count,
    root_live,
    nbr_live,
    nbr_dt,
    nbr_edge,
    ev_edge,
    ev_time,
    neg_count,
):
    shards = lax.axis_size("node")
    me = lax.axis_index("node")
    slots = req_rows.shape[3]
    wanted = req_rows[0, 0]
    counts = req_count[0, 0]
    mem_cols = memory[0].T
    mail_cols = mailbox[0].T
    feat_cols = node_feat.T
    edge_cols = jnp.transpose(nbr_edge[0, 0], (1, 2, 0))

    flat = gather_params(params.astype(BF16).reshape(1, -1, LANES)).reshape(-1, LANES)
    wts = weights_of(flat)
    asked = swap(wanted).reshape(-1)

    dt = nbr_dt[0, 0].T
    codes_n, codes_m = time_codes(dt, mail_time - update_time)

    near_slot = to_slot(nbr_live[0, 0].T, counts, slots)
    root_slot = to_slot(root_live[0, 0], counts, slots)
    blocks = EV // EB
    near_index = jnp.transpose(near_slot.reshape(NBR, 3, blocks, EB), (2, 0, 1, 3))
    root_index = jnp.transpose(root_slot.reshape(3, blocks, EB), (1, 0, 2))
    index = jnp.concatenate(
        [near_index.reshape(blocks, -1), root_index.reshape(blocks, -1)], 1
    ).reshape(-1)

    ends = root_slot[:2].reshape(-1)
    ordered = lax.sort(ends * (2 * EV) + jnp.arange(2 * EV, dtype=jnp.int32))
    end_id = ordered % (2 * EV)
    end_slot = ordered // (2 * EV)
    partner_slot = ends[(end_id + EV) % (2 * EV)]
    end_row = wanted.reshape(-1)[end_slot]
    first = jnp.sum(
        (end_slot[None, :] < (jnp.arange(LANES, dtype=jnp.int32) * slots)[:, None]).astype(jnp.int32), 1
    )
    notes = jnp.concatenate([end_row, end_id % EV, ev_time[0, 0], first]).reshape(-1, LANES)
    notes = lax.all_gather(notes, "node", axis=0, tiled=False)
    edges_all = lax.all_gather(ev_edge[0, 0].T, "node", axis=0, tiled=False)
    notes = notes.reshape(shards, -1)

    h_sent, s_rows, s_cols = gru_forward(asked, mail_cols, codes_m, mem_cols, feat_cols, wts, shards * slots)
    h_got = swap(h_sent.reshape(shards, slots, LANES))
    s_sent = gather_rows(s_rows, asked)
    h_got, s_sent = lax.optimization_barrier((h_got, s_sent))
    s_got = swap(s_sent.reshape(shards, slots, LANES)).reshape(-1, LANES)

    d_sent, att_grads, losses = attention(
        index, counts, h_got.reshape(-1, LANES), edge_cols, codes_n, neg_count[0], wts
    )
    d_got = swap(d_sent.reshape(shards, slots, LANES)).reshape(-1, LANES)

    partner = gather_rows(s_got, partner_slot)
    partner = lax.all_gather(partner, "node", axis=0, tiled=False)

    mem_new, mem_grad, upd_new, gru_grads, bias_grads = gru_backward(
        asked, d_got, mail_cols, codes_m, mem_cols, feat_cols, mail_time, update_time, wts
    )
    packed = pack(gru_grads, bias_grads, att_grads, losses)[:FLAT_ROWS]
    shard = scatter_sum(packed)

    events_of = notes[:, 2 * EV : 4 * EV].reshape(-1)
    rows_of = notes[:, : 2 * EV].reshape(-1)
    stamps = notes[:, 4 * EV : 5 * EV].reshape(shards, 1, EV)
    starts = lax.dynamic_slice_in_dim(notes[:, 5 * EV :], me, 2, 1).reshape(-1)
    mail_new, stamp_new = deliver(
        starts, rows_of, events_of, partner, edges_all, stamps, s_cols, mail_cols, mail_time
    )

    number = lax.axis_index("batch") * shards + me
    size = shard.shape[0] * LANES
    place = number * size + jnp.arange(size, dtype=jnp.int32).reshape(-1, LANES)
    grad = jnp.where(place < USED, shard, 0.0)
    values = jnp.stack(
        [
            jnp.sum(grad * grad),
            jnp.sum(jnp.where(place == USED, shard, 0.0)),
            jnp.sum(jnp.where(place == USED + 1, shard, 0.0)),
        ]
    )
    values = sum_all(jnp.zeros((8, LANES), F32).at[0, :3].set(values))
    grad_norm = jnp.sqrt(values[0, 0])
    clipped = grad.reshape(-1) * jnp.minimum(1.0, clip_limit / (grad_norm + 1e-06))
    moment1_new = beta_first * moment1 + (1.0 - beta_first) * clipped
    moment2_new = beta_second * moment2 + (1.0 - beta_second) * clipped * clipped
    ratio = (
        moment1_new
        / (1.0 - beta_first**STEP)
        / (jnp.sqrt(moment2_new / (1.0 - beta_second**STEP)) + adam_floor)
    )
    params_new = params - learn_rate * (ratio + decay_rate * params)
    return (
        values[0, 1],
        values[0, 2],
        grad_norm,
        params_new,
        moment1_new,
        moment2_new,
        params_new.astype(BF16),
        mem_new.T[None],
        mail_new.T[None],
        stamp_new,
        upd_new,
        mem_grad.T[None],
    )


def solution(mesh):
    both, split = P(("batch", "node")), P("batch", "node")
    in_specs = (both, both, both, split, split, split, split, P("node")) + (split,) * 9
    out_specs = (P(), P(), P()) + (both,) * 4 + (split,) * 5
    return jax.shard_map(body, mesh=mesh, in_specs=in_specs, out_specs=out_specs, check_vma=False)
```

```python
import functools
import math

import jax
import jax.numpy as jnp
import numpy as np
from jax import lax
from jax.experimental import pallas as pl
from jax.experimental.pallas import tpu as pltpu
from jax.sharding import PartitionSpec as P

MEM = 100
TENC = 100
EDGE = 186
NFEAT = 413
NBR = 10
STEP = 5
EV = 512
MAIL = 386
FLAT = 360448

clip_limit = 1.0
learn_rate = 0.02
beta_first = 0.5
beta_second = 0.6
adam_floor = 1e-08
decay_rate = 0.01

F32 = jnp.float32
BF16 = jnp.bfloat16
LANES = 128
PAD = 112
HALF = 56
WIRE = 104
GATES = 3 * PAD
KV = 4 * HALF
EB = 128
SECT = 3 * EB
STREAMS = 8
VMEM_LIMIT = 63_000_000

ROW_HH = 1458
ROW_NF = 1758
ROW_Q = 2171
ROW_KV = 2371
ROW_O = 3143
ROW_SRC = 3343
ROW_DST = 3443
ROW_OUT = 3543
ROW_BIH = 3544
ROW_BHH = 3547
ROW_BO = 3550
ROW_GAIN = 3551
ROW_SHIFT = 3552
ROW_BPRED = 3553
ROW_BOUT = 3554
USED = 355401
FLAT_ROWS = FLAT // LANES
PERIODS = 113
WROWS = 32 * PERIODS
GRU_ROWS = 2176
ATT_BASE = 2168
ATT_ROWS = 1448

FREQS = np.float32(10.0 ** (-9.0 * np.arange(TENC) / (TENC - 1)))

VMEM = pl.BlockSpec(memory_space=pltpu.VMEM)
SMEM = pl.BlockSpec(memory_space=pltpu.SMEM)


def params_of(limit=VMEM_LIMIT):
    return pltpu.CompilerParams(vmem_limit_bytes=limit)


def dot(left, right, left_dim=1, right_dim=0):
    return lax.dot_general(
        left, right, (((left_dim,), (right_dim,)), ((), ())), preferred_element_type=F32
    )


def fit_cosine():
    u = np.cos(np.pi * (np.arange(4000) + 0.5) / 4000) * 0.5 + 0.5
    u = u * (np.pi**2 * 1.002)
    fit = np.polynomial.chebyshev.Chebyshev.fit(u, np.cos(np.sqrt(u)), 7, domain=[0, np.pi**2 * 1.002])
    return [float(np.float32(c)) for c in fit.convert(kind=np.polynomial.Polynomial).coef]


COSINE = fit_cosine()


def cosine(x):
    turns = jnp.floor(x * np.float32(0.5 / np.pi) + 0.5)
    x = x - turns * np.float32(6.28125)
    x = x - turns * np.float32(2 * np.pi - 6.28125)
    u = x * x
    total = jnp.full_like(u, COSINE[-1])
    for c in COSINE[-2::-1]:
        total = total * u + np.float32(c)
    return total


def sigmoid(x):
    return 0.5 * jnp.tanh(0.5 * x) + 0.5


GELU_C = math.sqrt(2.0 / math.pi)


def gelu(x):
    t = jnp.tanh(GELU_C * (x + 0.044715 * (x * x * x)))
    return 0.5 * x * (1.0 + t)


def gelu_slope(x):
    x2 = x * x
    t = jnp.tanh(GELU_C * (x + 0.044715 * (x2 * x)))
    return 0.5 * (1.0 + t) + 0.5 * x * (1.0 - t * t) * (GELU_C * (1.0 + 3 * 0.044715 * x2))


def lane_of(shape):
    return lax.broadcasted_iota(jnp.int32, shape, len(shape) - 1)


def row_of(shape):
    return lax.broadcasted_iota(jnp.int32, shape, len(shape) - 2)


def roll_left(x, amount):
    amount = amount % LANES
    return x if amount == 0 else pltpu.roll(x, LANES - amount, 1)


def spread_heads(x):
    lane = lane_of(x.shape)
    moved = roll_left(x, -6)
    return jnp.where(lane < 50, x, jnp.where((lane >= 56) & (lane < 106), moved, 0.0))


def join_heads(x):
    lane = lane_of(x.shape)
    return jnp.where(lane < 50, x, jnp.where(lane < 100, roll_left(x, 6), 0.0))


def codes_kernel(delta, freq, out):
    freqs = freq[...]
    for k in range(out.shape[0]):

        def one(i, carry, k=k):
            at = pl.ds(pl.multiple_of(i * LANES, LANES), LANES)
            out[k, :, at] = cosine(delta[k : k + 1, at].astype(F32) * freqs).astype(BF16)
            return carry

        lax.fori_loop(0, delta.shape[1] // LANES, one, 0)


def time_codes(delta):
    freq = jnp.asarray(np.tile(FREQS[:, None], (1, LANES)))
    rows, count = delta.shape
    return pl.pallas_call(
        codes_kernel,
        out_shape=jax.ShapeDtypeStruct((rows, TENC, count), BF16),
        in_specs=[VMEM] * 2,
        out_specs=VMEM,
        compiler_params=params_of(16 * 2**20),
        cost_estimate=pl.CostEstimate(
            flops=rows * count * 3000, bytes_accessed=rows * count * 200, transcendentals=0
        ),
    )(delta, freq)


def weights_kernel(
    flat,
    w_mail,
    w_time,
    w_hid,
    w_feat,
    gate_bias,
    kv_h,
    kv_e,
    kv_t,
    q_h,
    q_one,
    o_att,
    o_att_n,
    o_h,
    src_t,
    src_n,
    dst_t,
    dst_n,
    cols,
    wide,
    rows,
):
    wide[0:FLAT_ROWS, :] = flat[...].astype(F32)
    wide[FLAT_ROWS:, :] = jnp.zeros((wide.shape[0] - FLAT_ROWS, LANES), F32)
    lane = lane_of((PERIODS, LANES))
    for j in range(32):
        first, shift = divmod(100 * j, LANES)
        out = roll_left(wide[pl.ds(first, PERIODS, stride=25), :], shift)
        if shift + 100 > LANES:
            after = roll_left(wide[pl.ds(first + 1, PERIODS, stride=25), :], shift)
            out = jnp.where(lane < LANES - shift, out, after)
        rows[pl.ds(j, PERIODS, stride=32), :] = jnp.where(lane < 100, out, 0.0)

    def turned(start, count, stride=1):
        size = -(-count // LANES) * LANES
        if stride == 1:
            block = rows[start : start + size, :]
        else:
            block = rows[pl.ds(start, size, stride=stride), :]
        return jnp.where(row_of((size, LANES)) < count, block, 0.0).T

    for g in range(3):
        to = slice(PAD * g, PAD * g + PAD)
        w_mail[to, :] = turned(g, MAIL, 3)[:PAD, :MAIL].astype(BF16)
        w_time[to, :] = turned(3 * MAIL + g, TENC, 3)[:PAD, :TENC].astype(BF16)
        w_hid[to, :] = turned(ROW_HH + g, MEM, 3)[:PAD, :MEM].astype(BF16)
    w_feat[...] = turned(ROW_NF, NFEAT)[:PAD, :NFEAT].astype(BF16)

    def column(r):
        return jnp.broadcast_to(rows[r : r + 1, :], (LANES, LANES)).T[:PAD, :]

    for g in range(3):
        gate_bias[0, PAD * g : PAD * g + PAD, :] = column(ROW_BIH + g)
        gate_bias[1, PAD * g : PAD * g + PAD, :] = column(ROW_BHH + g)
    for part in range(2):
        to = slice(PAD * part, PAD * part + PAD)

        def heads(start, count, part=part):
            size = -(-count // LANES) * LANES
            block = spread_heads(rows[pl.ds(ROW_KV + 2 * start + part, size, stride=2), :])
            return jnp.where(row_of((size, LANES)) < count, block, 0.0).T[:PAD]

        kv_h[to, :] = heads(0, MEM).astype(BF16)
        kv_e[to, :] = heads(MEM, EDGE)[:, :EDGE].astype(BF16)
        kv_t[to, :] = heads(MEM + EDGE, TENC)[:, :TENC].astype(BF16)
    q_rows = spread_heads(rows[ROW_Q : ROW_Q + LANES, :])
    keep = row_of((LANES, LANES)) < 100
    q_h[...] = jnp.where(keep, q_rows, 0.0).T[:PAD].astype(BF16)
    q_two = spread_heads(rows[ROW_Q + 100 : ROW_Q + 100 + LANES, :])
    q_sum = jnp.sum(jnp.where(keep, q_two, 0.0), 0, keepdims=True)
    q_one[...] = jnp.broadcast_to(q_sum, (LANES, LANES)).T[:PAD]
    att = spread_heads(turned(ROW_O, 100))
    o_att[...] = att[:PAD, :PAD].astype(BF16)
    o_att_n[...] = att.T[:PAD, :PAD].astype(BF16)
    o_h[...] = turned(ROW_O + 100, 100)[:PAD].astype(BF16)
    for start, out_t, out_n in ((ROW_SRC, src_t, src_n), (ROW_DST, dst_t, dst_n)):
        block = turned(start, 100)
        out_t[...] = block[:PAD, :PAD].astype(BF16)
        out_n[...] = block.T[:PAD, :PAD].astype(BF16)
    for i, r in enumerate((ROW_BO, ROW_GAIN, ROW_SHIFT, ROW_BPRED, ROW_OUT)):
        cols[i, :, :] = column(r)
    first = rows[ROW_BOUT : ROW_BOUT + 1, :]
    value = jnp.sum(jnp.where(lane_of((1, LANES)) == 0, first, 0.0), 1, keepdims=True)
    cols[5, :, :] = jnp.broadcast_to(value, (PAD, LANES))


def weights_of(flat):
    shapes = [
        ((GATES, MAIL), BF16),
        ((GATES, TENC), BF16),
        ((GATES, MEM), BF16),
        ((PAD, NFEAT), BF16),
        ((2, GATES, LANES), F32),
        ((KV, LANES), BF16),
        ((KV, EDGE), BF16),
        ((KV, TENC), BF16),
        ((PAD, LANES), BF16),
        ((PAD, LANES), F32),
        ((PAD, PAD), BF16),
        ((PAD, PAD), BF16),
        ((PAD, LANES), BF16),
        ((PAD, PAD), BF16),
        ((PAD, PAD), BF16),
        ((PAD, PAD), BF16),
        ((PAD, PAD), BF16),
        ((6, PAD, LANES), F32),
    ]
    return pl.pallas_call(
        weights_kernel,
        out_shape=[jax.ShapeDtypeStruct(s, d) for s, d in shapes],
        in_specs=[VMEM],
        out_specs=[VMEM] * len(shapes),
        scratch_shapes=[pltpu.VMEM((FLAT_ROWS + 16, LANES), F32), pltpu.VMEM((WROWS + 512, LANES), F32)],
        compiler_params=params_of(),
        cost_estimate=pl.CostEstimate(flops=4_000_000, bytes_accessed=2_000_000, transcendentals=0),
    )(flat)


def gather_loop(index, table, out, count, base=0, to=0):
    group = 32

    def step(i, carry):
        for g in range(group // 16):
            at = pl.multiple_of(i * group + g * 16, 16)
            picked = [table[pl.ds(index[base + at + u], 1), :] for u in range(16)]
            out[pl.ds(to + at, 16), :] = jnp.concatenate(picked, 0).astype(out.dtype)
        return carry

    lax.fori_loop(0, count // group, step, 0)


def gather_turned(index, table, out):
    slots = out.shape[2]
    pieces = slots // LANES

    def step(j, carry):
        owner = j // pieces
        at = pl.ds(pl.multiple_of((j - owner * pieces) * LANES, LANES), LANES)
        groups = []
        for g in range(LANES // 8):
            picked = [table[pl.ds(index[j * LANES + g * 8 + u], 1), :] for u in range(8)]
            groups.append(jnp.concatenate(picked, 0))
        out[owner, 0:WIRE, at] = jnp.concatenate(groups, 0).T[:WIRE].astype(BF16)
        return carry

    lax.fori_loop(0, out.shape[0] * pieces, step, 0, unroll=2)


def turn_into(got, table):
    slots = got.shape[2]
    pieces = slots // LANES
    short = jnp.zeros((LANES - WIRE, LANES), F32)

    def step(j, carry):
        owner = j // pieces
        at = pl.ds(pl.multiple_of((j - owner * pieces) * LANES, LANES), LANES)
        block = jnp.concatenate([got[owner, 0:WIRE, at].astype(F32), short], 0)
        table[pl.ds(pl.multiple_of(j * LANES, LANES), LANES), :] = block.T
        return carry

    lax.fori_loop(0, got.shape[0] * pieces, step, 0, unroll=8)


def to_rows(block):
    full = jnp.concatenate([block, jnp.zeros((LANES - PAD, LANES), F32)], 0)
    return full.T


def mem_piece(mem, i):
    return mem.reshape(MEM * 8, LANES)[pl.ds(i, MEM, stride=8), :]


def gru_products(mail, phi, low, w_mail, w_time, w_hid, gi, gh):
    gi[...] = dot(w_mail[...], mail[...]) + dot(w_time[...], phi[...])
    gh[...] = dot(w_hid[...], low[...])


def gates_at(at, gi, gh, bias, low):
    gr, gz, gn = (gi[PAD * g : PAD * g + PAD, at] + bias[0, PAD * g : PAD * g + PAD, :] for g in range(3))
    hr, hz, hn = (gh[PAD * g : PAD * g + PAD, at] + bias[1, PAD * g : PAD * g + PAD, :] for g in range(3))
    r = sigmoid(gr + hr)
    z = sigmoid(gz + hz)
    n = jnp.tanh(gn + r * hn)
    s = jnp.concatenate([low[:, at].astype(F32), jnp.zeros((PAD - MEM, LANES), F32)], 0)
    return r, z, n, hn, s, (1.0 - z) * n + z * s


def gru_kernel(
    index, mail, phi, mem, feat, w_mail, w_time, w_hid, w_feat, bias, sent, s_rows, low, table, gi, gh, nf
):
    block = mail.shape[1]
    step = pl.program_id(0)
    for i in range(block // LANES):
        low[:, i * LANES : i * LANES + LANES] = mem_piece(mem, i).astype(BF16)
    gru_products(mail, phi, low, w_mail, w_time, w_hid, gi, gh)
    nf[...] = dot(w_feat[...], feat[...])

    def piece(i, carry):
        start = pl.multiple_of(i * LANES, LANES)
        at = pl.ds(start, LANES)
        _, _, _, _, _, renewed = gates_at(at, gi, gh, bias, low)
        hidden = (renewed + nf[:, at]).astype(BF16).astype(F32)
        table[pl.ds(pl.multiple_of(step * block + start, LANES), LANES), :] = to_rows(hidden)
        s_rows[at, :] = to_rows(renewed)
        return carry

    lax.fori_loop(0, block // LANES, piece, 0)

    @pl.when(step == pl.num_programs(0) - 1)
    def _():
        gather_turned(index, table, sent)


BLOCK = 1024


def cols_spec(rows):
    return pl.BlockSpec((rows, BLOCK), lambda i: (0, i))


def mem_spec():
    return pl.BlockSpec((MEM, BLOCK // LANES, LANES), lambda i: (0, i, 0))


def gru_forward(index, mail, phi, mem, feat, wts, shards, slots):
    rows = mail.shape[1]
    return pl.pallas_call(
        gru_kernel,
        grid=(rows // BLOCK,),
        out_shape=(
            jax.ShapeDtypeStruct((shards, WIRE, slots), BF16),
            jax.ShapeDtypeStruct((rows, LANES), F32),
            jax.ShapeDtypeStruct((MEM, rows), BF16),
        ),
        in_specs=[SMEM, cols_spec(MAIL), cols_spec(TENC), mem_spec(), cols_spec(NFEAT)] + [VMEM] * 5,
        out_specs=(VMEM, pl.BlockSpec((BLOCK, LANES), lambda i: (i, 0)), cols_spec(MEM)),
        scratch_shapes=[
            pltpu.VMEM((rows, LANES), F32),
            pltpu.VMEM((GATES, BLOCK), F32),
            pltpu.VMEM((GATES, BLOCK), F32),
            pltpu.VMEM((PAD, BLOCK), F32),
        ],
        compiler_params=params_of(),
        cost_estimate=pl.CostEstimate(flops=4_000_000_000, bytes_accessed=24_000_000, transcendentals=3_000_000),
    )(index, mail, phi, mem, feat, *wts[:5])


def send_kernel(index, table, notes, out):
    for owner in range(out.shape[0]):
        out[owner, WIRE:, :] = notes[...]
    gather_turned(index, table, out)


def send_rows(table, index, notes, shards, slots):
    return pl.pallas_call(
        send_kernel,
        out_shape=jax.ShapeDtypeStruct((shards, WIRE + notes.shape[0], slots), BF16),
        in_specs=[SMEM, VMEM, VMEM],
        out_specs=VMEM,
        compiler_params=params_of(24 * 2**20),
        cost_estimate=pl.CostEstimate(flops=8_000_000, bytes_accessed=6_000_000, transcendentals=0),
    )(index, table, notes)


def partner_kernel(index, got, out, table):
    turn_into(got, table)
    gather_loop(index, table, out, index.shape[0])


def partner_rows(got, index):
    return pl.pallas_call(
        partner_kernel,
        out_shape=jax.ShapeDtypeStruct((index.shape[0], LANES), BF16),
        in_specs=[SMEM, VMEM],
        out_specs=VMEM,
        scratch_shapes=[pltpu.VMEM((got.shape[0] * got.shape[2], LANES), F32)],
        compiler_params=params_of(24 * 2**20),
        cost_estimate=pl.CostEstimate(flops=2_000_000, bytes_accessed=2_000_000, transcendentals=0),
    )(index, got)


def book_kernel(ordered, ends, wanted, row, partner, event):
    count = ordered.shape[0]

    def step(i, carry):
        for u in range(8):
            at = i * 8 + u
            key = ordered[at]
            end = jnp.bitwise_and(key, count - 1)
            row[at] = wanted[lax.shift_right_logical(key, count.bit_length() - 1)]
            partner[at] = ends[jnp.bitwise_xor(end, count // 2)]
            event[at] = jnp.bitwise_and(end, count // 2 - 1)
        return carry

    lax.fori_loop(0, count // 8, step, 0)


def bookkeeping(ordered, ends, wanted):
    shape = jax.ShapeDtypeStruct(ordered.shape, jnp.int32)
    return pl.pallas_call(
        book_kernel,
        out_shape=(shape, shape, shape),
        in_specs=[SMEM] * 3,
        out_specs=(SMEM,) * 3,
        compiler_params=params_of(),
        cost_estimate=pl.CostEstimate(flops=4_000_000, bytes_accessed=60_000, transcendentals=0),
    )(ordered, ends, wanted)


def factor_kernel(
    index,
    flags,
    mail,
    phi,
    low,
    mem,
    mail_time,
    update_time,
    w_mail,
    w_time,
    w_hid,
    bias,
    factors,
    s_cols,
    mem_new,
    time_new,
    placed,
    gi,
    gh,
):
    step = pl.program_id(0)

    @pl.when(step == 0)
    def _():
        count = index.shape[0]
        if count != placed.shape[0]:
            placed[...] = jnp.zeros_like(placed)
        group = 32

        def move(i, carry):
            for u in range(group):
                at = i * group + u
                placed[pl.ds(index[at], 1), :] = jnp.full((1, LANES), flags[at], jnp.int32)
            return carry

        lax.fori_loop(0, count // group, move, 0)

    gru_products(mail, phi, low, w_mail, w_time, w_hid, gi, gh)
    for i in range(BLOCK // LANES):
        at = slice(i * LANES, i * LANES + LANES)
        r, z, n, hn, s, renewed = gates_at(at, gi, gh, bias, low)
        live = placed[pl.ds(pl.multiple_of(step * BLOCK + i * LANES, LANES), LANES), :].T[0:1, :] > 0
        an = (1.0 - z) * (1.0 - n * n)
        factors[0, :, at] = (an * hn * (r * (1.0 - r)))[:MEM]
        factors[1, :, at] = ((s - n) * (z * (1.0 - z)))[:MEM]
        factors[2, :, at] = an[:MEM]
        factors[3, :, at] = r[:MEM]
        factors[4, :, at] = z[:MEM]
        s_cols[:, at] = renewed[:MEM].astype(BF16)
        value = jnp.where(live, renewed[:MEM], mem_piece(mem, i))
        mem_new.reshape(MEM * 8, LANES)[pl.ds(i, MEM, stride=8), :] = value
        time_new[:, at] = jnp.where(live, mail_time[:, at], update_time[:, at])


def gru_factors(index, flags, mail, phi, low, mem, mail_time, update_time, wts):
    rows = mail.shape[1]
    return pl.pallas_call(
        factor_kernel,
        grid=(rows // BLOCK,),
        out_shape=(
            jax.ShapeDtypeStruct((5, MEM, rows), F32),
            jax.ShapeDtypeStruct((MEM, rows), BF16),
            jax.ShapeDtypeStruct((MEM, rows // LANES, LANES), F32),
            jax.ShapeDtypeStruct((1, rows), jnp.int32),
        ),
        in_specs=[SMEM, SMEM, cols_spec(MAIL), cols_spec(TENC), cols_spec(MEM), mem_spec()]
        + [cols_spec(1)] * 2
        + [VMEM] * 4,
        out_specs=(
            pl.BlockSpec((5, MEM, BLOCK), lambda i: (0, 0, i)),
            cols_spec(MEM),
            mem_spec(),
            cols_spec(1),
        ),
        scratch_shapes=[
            pltpu.VMEM((rows, LANES), jnp.int32),
            pltpu.VMEM((GATES, BLOCK), F32),
            pltpu.VMEM((GATES, BLOCK), F32),
        ],
        compiler_params=params_of(),
        cost_estimate=pl.CostEstimate(flops=3_000_000_000, bytes_accessed=34_000_000, transcendentals=3_000_000),
    )(index, flags, mail, phi, low, mem, mail_time, update_time, wts[0], wts[1], wts[2], wts[4])


def gru_back_kernel(
    index,
    got,
    factors,
    mail,
    phi,
    low,
    feat,
    w_hid,
    mem_grad,
    grads,
    biases,
    wide,
    placed,
    d_in,
    d_hid,
    d_low,
    direct,
    a_mail,
    a_time,
    a_hid,
    a_feat,
    a_bin,
    a_bhid,
):
    step = pl.program_id(0)

    @pl.when(step == 0)
    def _():
        turn_into(got, wide)
        count = wide.shape[0]
        if count != placed.shape[0]:
            placed[...] = jnp.zeros_like(placed)
        group = 32

        def move(i, carry):
            for u in range(group):
                at = i * group + u
                placed[pl.ds(index[at], 1), :] = wide[pl.ds(at, 1), :]
            return carry

        lax.fori_loop(0, count // group, move, 0)
        for ref in (d_in, d_hid, d_low, a_mail, a_time, a_hid, a_feat, a_bin, a_bhid):
            ref[...] = jnp.zeros_like(ref)

    for i in range(BLOCK // LANES):
        at = slice(i * LANES, i * LANES + LANES)
        d = placed[pl.ds(pl.multiple_of(step * BLOCK + i * LANES, LANES), LANES), :].T[:MEM]
        dr = d * factors[0, :, at]
        dz = d * factors[1, :, at]
        dn = d * factors[2, :, at]
        dhn = dn * factors[3, :, at]
        direct[:, at] = d * factors[4, :, at]
        low_r, low_z = dr.astype(BF16), dz.astype(BF16)
        d_low[0:MEM, at] = d.astype(BF16)
        d_in[0:MEM, at] = low_r
        d_in[PAD : PAD + MEM, at] = low_z
        d_in[2 * PAD : 2 * PAD + MEM, at] = dn.astype(BF16)
        d_hid[0:MEM, at] = low_r
        d_hid[PAD : PAD + MEM, at] = low_z
        d_hid[2 * PAD : 2 * PAD + MEM, at] = dhn.astype(BF16)
        a_bin[0:MEM, :] += dr
        a_bin[PAD : PAD + MEM, :] += dz
        a_bin[2 * PAD : 2 * PAD + MEM, :] += dn
        a_bhid[0:MEM, :] += dhn
    din, dhid = d_in[...], d_hid[...]
    a_mail[:, :MAIL] += dot(din, mail[...], 1, 1)
    a_time[:, :TENC] += dot(din, phi[...], 1, 1)
    a_hid[:, :MEM] += dot(dhid, low[...], 1, 1)
    a_feat[:, :NFEAT] += dot(d_low[...], feat[...], 1, 1)
    direct[...] += dot(w_hid[...], dhid, 0, 0)
    for i in range(BLOCK // LANES):
        at = slice(i * LANES, i * LANES + LANES)
        mem_grad.reshape(MEM * 8, LANES)[pl.ds(i, MEM, stride=8), :] = direct[:, at]

    @pl.when(step == pl.num_programs(0) - 1)
    def _():
        def turned_back(ref, g):
            part = ref[PAD * g : PAD * g + PAD, :]
            return jnp.concatenate([part, jnp.zeros((LANES - PAD, part.shape[1]), F32)], 0).T

        grads[ROW_Q:GRU_ROWS, :] = jnp.zeros((GRU_ROWS - ROW_Q, LANES), F32)
        for g in range(3):
            grads[pl.ds(g, MAIL, stride=3), :] = turned_back(a_mail, g)[:MAIL]
            grads[pl.ds(3 * MAIL + g, TENC, stride=3), :] = turned_back(a_time, g)[:TENC]
            grads[pl.ds(ROW_HH + g, MEM, stride=3), :] = turned_back(a_hid, g)[:MEM]
        grads[ROW_NF:ROW_Q, :] = turned_back(a_feat, 0)[:NFEAT]
        sums = []
        for ref, g in ((a_bin, 0), (a_bin, 1), (a_bin, 2), (a_bin, 0), (a_bin, 1), (a_bhid, 0)):
            sums.append(jnp.sum(turned_back(ref, g), 0, keepdims=True))
        biases[...] = jnp.concatenate(sums + [jnp.zeros((2, LANES), F32)], 0)


def gru_backward(index, got, factors, mail, phi, low, feat, wts):
    rows = mail.shape[1]
    return pl.pallas_call(
        gru_back_kernel,
        grid=(rows // BLOCK,),
        out_shape=(
            jax.ShapeDtypeStruct((MEM, rows // LANES, LANES), F32),
            jax.ShapeDtypeStruct((GRU_ROWS, LANES), F32),
            jax.ShapeDtypeStruct((8, LANES), F32),
        ),
        in_specs=[SMEM, VMEM, pl.BlockSpec((5, MEM, BLOCK), lambda i: (0, 0, i))]
        + [cols_spec(r) for r in (MAIL, TENC, MEM, NFEAT)]
        + [VMEM],
        out_specs=(mem_spec(), VMEM, VMEM),
        scratch_shapes=[
            pltpu.VMEM((got.shape[0] * got.shape[2], LANES), F32),
            pltpu.VMEM((rows, LANES), F32),
            pltpu.VMEM((GATES, BLOCK), BF16),
            pltpu.VMEM((GATES, BLOCK), BF16),
            pltpu.VMEM((PAD, BLOCK), BF16),
            pltpu.VMEM((MEM, BLOCK), F32),
            pltpu.VMEM((GATES, 512), F32),
            pltpu.VMEM((GATES, LANES), F32),
            pltpu.VMEM((GATES, LANES), F32),
            pltpu.VMEM((PAD, 512), F32),
            pltpu.VMEM((GATES, LANES), F32),
            pltpu.VMEM((PAD, LANES), F32),
        ],
        compiler_params=params_of(),
        cost_estimate=pl.CostEstimate(flops=5_000_000_000, bytes_accessed=36_000_000, transcendentals=0),
    )(index, got, factors, mail, phi, low, feat, wts[2])


def attention_kernel(
    index,
    got,
    e0,
    e1,
    e2,
    p0,
    p1,
    p2,
    weight,
    kv_h,
    kv_e,
    kv_t,
    q_h,
    q_one,
    o_att,
    o_att_n,
    o_h,
    src_t,
    src_n,
    dst_t,
    dst_n,
    cols,
    sent,
    grads,
    losses,
    table,
    kv,
    d_rows,
    d_two,
    a_kvh,
    a_kve,
    a_kvt,
    a_qh,
    a_q1,
    a_oa,
    a_oh,
    a_src,
    a_dst,
    a_col,
    a_one,
    *rest,
):
    lanes, picks = rest[:STREAMS], rest[STREAMS:]
    step = pl.program_id(0)
    near = NBR * SECT
    total = near + SECT
    scale = 50 ** (-0.5)
    sums = (a_kvh, a_kve, a_kvt, a_qh, a_q1, a_oa, a_oh, a_src, a_dst, a_col, a_one)

    @pl.when(step == 0)
    def _():
        turn_into(got, table)
        for ref in sums + lanes:
            ref[...] = jnp.zeros_like(ref)

    at_block = step * total
    gather_loop(index, table, picks[NBR], SECT, at_block + near)
    gather_loop(index, table, picks[0], SECT, at_block)
    roots = picks[NBR][...]

    def edge_of(k):
        return jnp.concatenate([e0[k], e1[k], e2[k]], 1)

    def code_of(k):
        return jnp.concatenate([p0[k], p1[k], p2[k]], 1)

    for k in range(NBR):
        kv[k] = (
            dot(kv_h[...], picks[k][...], 1, 1)
            + dot(kv_e[...], edge_of(k))
            + dot(kv_t[...], code_of(k))
        )
        if k + 1 < NBR:
            for g in range(SECT // 16):
                first = (k + 1) * SECT + g * 16
                rows = [table[pl.ds(index[at_block + first + u], 1), :] for u in range(16)]
                picks[k + 1][g * 16 : g * 16 + 16, :] = jnp.concatenate(rows, 0).astype(BF16)
    query = dot(q_h[...], roots, 1, 1)
    o_root = dot(o_h[...], roots, 1, 1)
    bo, gain, shift, bpred, wout = (cols[i] for i in range(5))
    bout = cols[5, 0:1, :]
    real = row_of((PAD, LANES)) < MEM
    queries, probs, atts, pres, embs, norms = [], [], [], [], [], []
    for t in range(3):
        at = slice(t * EB, t * EB + EB)
        q = query[:, at] + q_one[...]
        scores = [[], []]
        for k in range(NBR):
            both = q * kv[k, 0:PAD, at]
            for h in range(2):
                scores[h].append(jnp.sum(both[h * HALF : h * HALF + HALF], 0, keepdims=True) * scale)
        weights = []
        for h in range(2):
            top = functools.reduce(jnp.maximum, scores[h])
            parts = [jnp.exp(x - top) for x in scores[h]]
            whole = functools.reduce(jnp.add, parts)
            weights.append([x / whole for x in parts])
        heads = []
        for h in range(2):
            rows = slice(PAD + h * HALF, PAD + h * HALF + HALF)
            heads.append(
                functools.reduce(jnp.add, [weights[h][k] * kv[k, rows, at] for k in range(NBR)])
            )
        att = jnp.concatenate(heads, 0).astype(BF16)
        pre = dot(o_att[...], att) + o_root[:, at] + bo
        active = gelu(pre)
        mean = jnp.sum(active, 0, keepdims=True) * (1.0 / MEM)
        centre = jnp.where(real, active - mean, 0.0)
        spread = jnp.sum(centre * centre, 0, keepdims=True) * (1.0 / MEM)
        inverse = lax.rsqrt(spread + 1e-05)
        hat = centre * inverse
        queries.append(q)
        probs.append(weights)
        atts.append(att)
        pres.append(pre)
        norms.append((hat, inverse))
        embs.append((hat * gain + shift).astype(BF16))

    src_proj = dot(src_t[...], embs[0]) + bpred
    tails = [src_proj + dot(dst_t[...], embs[1]), src_proj + dot(dst_t[...], embs[2])]
    acts = [gelu(x).astype(BF16) for x in tails]
    logits = [jnp.sum(x.astype(F32) * wout, 0, keepdims=True) + bout for x in acts]
    neg_weight = weight[...].astype(F32)

    def softplus(x):
        return jnp.maximum(x, 0.0) + jnp.log1p(jnp.exp(-jnp.abs(x)))

    d_pos = -sigmoid(-logits[0])
    d_neg = neg_weight * sigmoid(logits[1])
    a_one[0:1, :] += softplus(-logits[0]) + neg_weight * softplus(logits[1])
    a_one[1:2, :] += 1.0 + neg_weight
    a_one[2:3, :] += d_pos + d_neg
    d_logits = [x.astype(BF16).astype(F32) for x in (d_pos, d_neg)]
    a_col[4] += acts[0].astype(F32) * d_logits[0] + acts[1].astype(F32) * d_logits[1]
    d_tails = [wout * d * gelu_slope(x) for d, x in zip(d_logits, tails)]
    d_src = d_tails[0] + d_tails[1]
    a_col[3] += d_src
    d_low = [x.astype(BF16) for x in (d_src, d_tails[0], d_tails[1])]
    a_src[...] += dot(embs[0], d_low[0], 1, 1)
    a_dst[...] += dot(embs[1], d_low[1], 1, 1) + dot(embs[2], d_low[2], 1, 1)
    d_embs = [dot(src_n[...], d_low[0]), dot(dst_n[...], d_low[1]), dot(dst_n[...], d_low[2])]

    d_outs, d_queries = [], []
    for t in range(3):
        at = slice(t * EB, t * EB + EB)
        hat, inverse = norms[t]
        d_emb = d_embs[t]
        a_col[1] += d_emb * hat
        a_col[2] += d_emb
        d_hat = d_emb * gain
        mean = jnp.sum(d_hat, 0, keepdims=True) * (1.0 / MEM)
        mixed = jnp.sum(d_hat * hat, 0, keepdims=True) * (1.0 / MEM)
        d_active = jnp.where(real, inverse * (d_hat - mean - hat * mixed), 0.0)
        d_out = d_active * gelu_slope(pres[t])
        a_col[0] += d_out
        d_out_low = d_out.astype(BF16)
        d_outs.append(d_out_low)
        a_oa[...] += dot(d_out_low, atts[t], 1, 1)
        d_att = dot(o_att_n[...], d_out_low)
        q = queries[t]
        d_q = jnp.zeros((PAD, EB), F32)
        slopes = [[], []]
        for h in range(2):
            rows = slice(PAD + h * HALF, PAD + h * HALF + HALF)
            d_head = d_att[h * HALF : h * HALF + HALF]
            dp = [jnp.sum(d_head * kv[k, rows, at], 0, keepdims=True) for k in range(NBR)]
            mid = functools.reduce(jnp.add, [a * b for a, b in zip(dp, probs[t][h])])
            slopes[h] = [probs[t][h][k] * (dp[k] - mid) * scale for k in range(NBR)]
        for k in range(NBR):
            keys = kv[k, 0:PAD, at]
            factor = jnp.concatenate(
                [jnp.broadcast_to(slopes[h][k], (HALF, EB)) for h in range(2)], 0
            )
            share = jnp.concatenate(
                [jnp.broadcast_to(probs[t][h][k], (HALF, EB)) for h in range(2)], 0
            )
            d_q = d_q + factor * keys
            kv[k, 0:PAD, at] = factor * q
            kv[k, PAD:KV, at] = share * d_att
        d_queries.append(d_q)
        a_q1[...] += d_q.astype(BF16).astype(F32)

    d_out_all = jnp.concatenate(d_outs, 1)
    d_q_all = jnp.concatenate(d_queries, 1).astype(BF16)
    a_oh[...] += dot(d_out_all, roots)
    a_qh[...] += dot(d_q_all, roots)
    d_rows[...] = dot(d_out_all, o_h[...], 0, 0) + dot(d_q_all, q_h[...], 0, 0)
    base = step * total
    each = SECT // STREAMS

    def add_rows(first, ref):
        for u in range(each):
            for s in range(STREAMS):
                at = s * each + u
                to = pl.ds(index[first + at], 1)
                lanes[s][to, :] += ref[at : at + 1, :]

    for k in range(NBR):
        mine, other = (d_two, d_rows) if k % 2 == 0 else (d_rows, d_two)
        d_kv = kv[k].astype(BF16)
        a_kvh[...] += dot(d_kv, picks[k][...])
        a_kve[:, :EDGE] += dot(d_kv, edge_of(k), 1, 1)
        a_kvt[:, :TENC] += dot(d_kv, code_of(k), 1, 1)
        mine[...] = dot(d_kv, kv_h[...], 0, 0)
        add_rows(base + (NBR if k == 0 else k - 1) * SECT, other)
    add_rows(base + (NBR - 1) * SECT, d_rows)

    @pl.when(step == pl.num_programs(0) - 1)
    def _():
        slots = sent.shape[2]
        pieces = slots // LANES

        def finish(j, carry):
            owner = j // pieces
            to = pl.ds(pl.multiple_of((j - owner * pieces) * LANES, LANES), LANES)
            at = pl.ds(pl.multiple_of(j * LANES, LANES), LANES)
            whole = functools.reduce(jnp.add, [ref[at, :] for ref in lanes])
            sent[owner, :, to] = jnp.where(lane_of((LANES, LANES)) < MEM, whole, 0.0).T[:WIRE].astype(BF16)
            return carry

        lax.fori_loop(0, sent.shape[0] * pieces, finish, 0, unroll=4)
        base_row = ATT_BASE

        def turned(block):
            short = -block.shape[0] % LANES
            if short:
                block = jnp.concatenate([block, jnp.zeros((short, block.shape[1]), F32)], 0)
            return block.T

        grads[...] = jnp.zeros_like(grads)
        q = ROW_Q - base_row
        grads[q : q + 100, :] = join_heads(turned(a_qh[...]))[:100]
        ones = jnp.sum(turned(a_q1[...]), 0, keepdims=True)
        grads[q + 100 : q + 200, :] = jnp.broadcast_to(join_heads(ones), (100, LANES))
        for part in range(2):
            rows = slice(PAD * part, PAD * part + PAD)
            start = ROW_KV - base_row + part
            grads[pl.ds(start, MEM, stride=2), :] = join_heads(turned(a_kvh[rows, :]))[:MEM]
            grads[pl.ds(start + 2 * MEM, EDGE, stride=2), :] = join_heads(turned(a_kve[rows, :]))[:EDGE]
            grads[pl.ds(start + 2 * (MEM + EDGE), TENC, stride=2), :] = join_heads(
                turned(a_kvt[rows, :])
            )[:TENC]
        o = ROW_O - base_row
        wide = jnp.concatenate([a_oa[...], jnp.zeros((PAD, LANES - PAD), F32)], 1)
        grads[o : o + 100, :] = turned(join_heads(wide))[:100]
        grads[o + 100 : o + 200, :] = turned(a_oh[...])[:100]
        for start, ref in ((ROW_SRC, a_src), (ROW_DST, a_dst)):
            wide = jnp.concatenate([ref[...], jnp.zeros((PAD, LANES - PAD), F32)], 1)
            grads[start - base_row : start - base_row + 100, :] = wide[:100]
        for i, r in enumerate((ROW_BO, ROW_GAIN, ROW_SHIFT, ROW_BPRED, ROW_OUT)):
            line = jnp.sum(turned(a_col[i]), 0, keepdims=True)
            grads[r - base_row : r - base_row + 1, :] = line
        line = jnp.where(
            lane_of((1, LANES)) == 0, jnp.sum(a_one[2:3, :], 1, keepdims=True), 0.0
        )
        grads[ROW_BOUT - base_row : ROW_BOUT - base_row + 1, :] = line
        losses[...] = jnp.broadcast_to(jnp.sum(a_one[...], 1, keepdims=True), (8, LANES))


def attention(index, got, edges, codes, weight, wts):
    roots = edges.shape[2]
    blocks = roots // SECT

    def section(rows, t):
        return pl.BlockSpec((NBR, rows, EB), lambda b: (0, 0, t * blocks + b))

    slots = got.shape[0] * got.shape[2]
    total = (NBR + 1) * SECT
    return pl.pallas_call(
        attention_kernel,
        grid=(blocks,),
        out_shape=(
            jax.ShapeDtypeStruct(got.shape, BF16),
            jax.ShapeDtypeStruct((ATT_ROWS, LANES), F32),
            jax.ShapeDtypeStruct((8, LANES), F32),
        ),
        in_specs=[SMEM, VMEM]
        + [section(EDGE, t) for t in range(3)]
        + [section(TENC, t) for t in range(3)]
        + [pl.BlockSpec((1, EB), lambda b: (0, b))]
        + [VMEM] * 13,
        out_specs=(VMEM, VMEM, VMEM),
        scratch_shapes=[
            pltpu.VMEM((slots, LANES), F32),
            pltpu.VMEM((NBR, KV, SECT), F32),
            pltpu.VMEM((SECT, LANES), F32),
            pltpu.VMEM((SECT, LANES), F32),
            pltpu.VMEM((KV, LANES), F32),
            pltpu.VMEM((KV, 256), F32),
            pltpu.VMEM((KV, LANES), F32),
            pltpu.VMEM((PAD, LANES), F32),
            pltpu.VMEM((PAD, LANES), F32),
            pltpu.VMEM((PAD, PAD), F32),
            pltpu.VMEM((PAD, LANES), F32),
            pltpu.VMEM((PAD, PAD), F32),
            pltpu.VMEM((PAD, PAD), F32),
            pltpu.VMEM((5, PAD, LANES), F32),
            pltpu.VMEM((8, LANES), F32),
        ]
        + [pltpu.VMEM((slots, LANES), F32) for _ in range(STREAMS)]
        + [pltpu.VMEM((SECT, LANES), BF16) for _ in range(NBR + 1)],
        compiler_params=params_of(),
        cost_estimate=pl.CostEstimate(flops=9_000_000_000, bytes_accessed=20_000_000, transcendentals=1_000_000),
    )(index, got, edges, edges, edges, codes, codes, codes, weight, *wts[5:])


def pack_kernel(gru, bias, att, losses, out, rows):
    rows[0:GRU_ROWS, :] = gru[...]
    rows[GRU_ROWS : ATT_BASE + ATT_ROWS, :] = att[8:, :]
    rows[ATT_BASE:GRU_ROWS, :] += att[0:8, :]
    rows[ROW_BIH : ROW_BIH + 8, :] += bias[...]
    rows[ATT_BASE + ATT_ROWS :, :] = jnp.zeros((rows.shape[0] - ATT_BASE - ATT_ROWS, LANES), F32)
    lane = lane_of((PERIODS, LANES))
    for m in range(25):
        first, shift = divmod(LANES * m, 100)
        value = None
        filled = 0
        source = first
        while filled < LANES:
            amount = shift if filled == 0 else -filled
            block = roll_left(rows[pl.ds(source, PERIODS, stride=32), :], amount)
            value = block if value is None else jnp.where(lane < filled, value, block)
            filled += 100 - (shift if filled == 0 else 0)
            source += 1
        out[pl.ds(m, PERIODS, stride=25), :] = value
    first, at = divmod(USED, LANES)
    tail = out.shape[0] - first
    where = row_of((tail, LANES)) * LANES + lane_of((tail, LANES))
    value = jnp.where(where < at, out[first:, :], 0.0)
    value = jnp.where(where == at, losses[0:1, :], value)
    value = jnp.where(where == at + 1, losses[1:2, :], value)
    out[first:, :] = value


def pack(gru, bias, att, losses):
    return pl.pallas_call(
        pack_kernel,
        out_shape=jax.ShapeDtypeStruct((25 * PERIODS + 7, LANES), F32),
        in_specs=[VMEM] * 4,
        out_specs=VMEM,
        scratch_shapes=[pltpu.VMEM((WROWS + 8, LANES), F32)],
        compiler_params=params_of(16 * 2**20),
        cost_estimate=pl.CostEstimate(flops=2_000_000, bytes_accessed=4_000_000, transcendentals=0),
    )(gru, bias, att, losses)


def edge_kernel(edges, stamps, out, stage):
    stage[...] = jnp.zeros_like(stage)
    stage[EDGE + 1 : EDGE + 2, :] = jnp.ones((1, EV), F32)
    stage[0:EDGE, :] = edges[0].astype(F32)
    stage[EDGE : EDGE + 1, :] = stamps[0].astype(F32)
    for part in range(2):
        out[0, part] = stage[LANES * part : LANES * part + LANES, :].T


def edge_tables(edges, stamps):
    senders = edges.shape[0]
    return pl.pallas_call(
        edge_kernel,
        grid=(senders,),
        out_shape=jax.ShapeDtypeStruct((senders, 2, EV, LANES), F32),
        in_specs=[
            pl.BlockSpec((1, EDGE, EV), lambda i: (i, 0, 0)),
            pl.BlockSpec((1, 1, EV), lambda i: (i, 0, 0)),
        ],
        out_specs=pl.BlockSpec((1, 2, EV, LANES), lambda i: (i, 0, 0, 0)),
        scratch_shapes=[pltpu.VMEM((2 * LANES, EV), F32)],
        compiler_params=params_of(16 * 2**20),
        cost_estimate=pl.CostEstimate(flops=3_000_000, bytes_accessed=6_000_000, transcendentals=0),
    )(edges, stamps)


def mail_kernel(
    starts, rows, events, partner, far, own, mailbox, mail_time, mail_new, time_new, near, kept, lines
):
    step = pl.program_id(0)
    senders = rows.shape[0] // (2 * EV)

    @pl.when(step == 0)
    def _():
        kept[2] = jnp.zeros(kept.shape[1:], F32)

    @pl.when(step < senders)
    def _():
        near[...] = partner[0].astype(F32)

        def move(i, carry):
            place = step * 2 * EV + i
            to = pl.ds(rows[place], 1)
            event = pl.ds(events[place], 1)
            kept[0, to, :] = near[pl.ds(i, 1), :]
            kept[1, to, :] = far[0, 0, event, :]
            kept[2, to, :] = far[0, 1, event, :]
            return carry

        lax.fori_loop(starts[2 * step], starts[2 * step + 1], move, 0)

    @pl.when(step >= senders)
    def _():
        block = mailbox.shape[1]
        at = pl.ds(pl.multiple_of((step - senders) * block, LANES), block)
        last = kept[2, at, :].T
        stamp = EDGE - LANES
        has = last[stamp + 1 : stamp + 2, :] > 0.5
        lines[0:MEM, :] = own[...].astype(F32)
        lines[MEM : 2 * MEM, :] = kept[0, at, :].T[0:MEM]
        lines[2 * MEM : 2 * MEM + LANES, :] = kept[1, at, :].T
        lines[2 * MEM + LANES : MAIL, :] = last[0:stamp]
        mail_new[...] = jnp.where(has, lines[0:MAIL, :], mailbox[...].astype(F32)).astype(BF16)
        time_new[...] = jnp.where(has, last[stamp : stamp + 1, :].astype(jnp.int32), mail_time[...])


def deliver(starts, rows, events, partner, far, own, mailbox, mail_time):
    senders = partner.shape[0]
    nodes = mailbox.shape[1]
    block = 1024

    def sender(i):
        return (jnp.minimum(i, senders - 1), 0, 0)

    def cols(count):
        return pl.BlockSpec((count, block), lambda i: (0, jnp.maximum(i - senders, 0)))

    return pl.pallas_call(
        mail_kernel,
        grid=(senders + nodes // block,),
        out_shape=(
            jax.ShapeDtypeStruct((MAIL, nodes), BF16),
            jax.ShapeDtypeStruct((1, nodes), jnp.int32),
        ),
        in_specs=[
            SMEM,
            SMEM,
            SMEM,
            pl.BlockSpec((1, 2 * EV, LANES), sender),
            pl.BlockSpec((1, 2, EV, LANES), lambda i: (jnp.minimum(i, senders - 1), 0, 0, 0)),
            cols(MEM),
            cols(MAIL),
            cols(1),
        ],
        out_specs=(cols(MAIL), cols(1)),
        scratch_shapes=[
            pltpu.VMEM((2 * EV, LANES), F32),
            pltpu.VMEM((3, nodes, LANES), F32),
            pltpu.VMEM((MAIL + 6, block), F32),
        ],
        compiler_params=params_of(44 * 2**20),
        cost_estimate=pl.CostEstimate(flops=20_000_000, bytes_accessed=16_000_000, transcendentals=0),
    )(starts, rows, events, partner, far, own, mailbox, mail_time)


def flip(x, axis, mask):
    return lax.ppermute(x, axis, [(i, i ^ mask) for i in range(lax.axis_size(axis))])


def rounds():
    table = []
    low, count = 2, lax.axis_size("node")
    while low < count:
        size = min(4, count // low)
        table.append(("node", low, size))
        low *= size
    table.append(("batch", 1, lax.axis_size("batch")))
    table.append(("node", 1, 2))
    return table


def place_in(axis, low, size):
    return (lax.axis_index(axis) // low) % size


def tree_sum(parts):
    while len(parts) > 1:
        parts = [a + b for a, b in zip(parts[::2], parts[1::2])]
    return parts[0]


def gather_params(x, between):
    shape = x.shape
    axes = []
    for number, (axis, low, size) in enumerate(rounds()):
        parts = [x] + [flip(x, axis, low * m) for m in range(1, size)]
        parts = between(number, x, parts)
        here = place_in(axis, low, size)
        key = (axis == "node", -low)
        at = sum(1 for k in axes if k < key)
        axes.append(key)
        axes.sort()
        out = jnp.zeros(x.shape[:at] + (size,) + x.shape[at:], x.dtype)
        for m, part in enumerate(parts):
            to = jnp.bitwise_xor(here, m)
            out = lax.dynamic_update_slice_in_dim(out, jnp.expand_dims(part, at), to, at)
        x = out
    return x.reshape((-1,) + shape[1:])


def scatter_sum(x, between):
    table = rounds()
    dims = sorted(((axis == "node", -low), size) for axis, low, size in table)
    keys = [k for k, _ in dims]
    x = x.reshape(tuple(n for _, n in dims) + (-1, LANES))
    for number, (axis, low, size) in enumerate(table[::-1]):
        at = keys.index((axis == "node", -low))
        here = place_in(axis, low, size)

        def part(m, x=x, at=at, here=here):
            return lax.dynamic_slice_in_dim(x, jnp.bitwise_xor(here, m), 1, at)

        away = [flip(part(m), axis, low * m) for m in range(1, size)]
        away = between(number, x, away)
        x = tree_sum([part(0)] + list(away))
    return x.reshape(-1, LANES)


def sum_all(x):
    for axis, low, size in rounds()[::-1]:
        x = tree_sum([x] + [flip(x, axis, low * m) for m in range(1, size)])
    return x


def after(x, *others):
    return lax.optimization_barrier((x,) + others)[0]


def swap(x):
    return lax.all_to_all(x, "node", split_axis=0, concat_axis=0, tiled=True)


def to_slot(live, counts, slots):
    upper = jnp.cumsum(counts)
    shape = (-1,) + (1,) * live.ndim
    passed = live[None] >= upper.reshape(shape)
    return live + jnp.sum(jnp.where(passed, (slots - counts).reshape(shape), 0), 0)


def body(
    params,
    moment1,
    moment2,
    memory,
    mailbox,
    mail_time,
    update_time,
    node_feat,
    req_rows,
    req_count,
    root_live,
    nbr_live,
    nbr_dt,
    nbr_edge,
    ev_edge,
    ev_time,
    neg_count,
):
    shards = lax.axis_size("node")
    me = lax.axis_index("node")
    slots = req_rows.shape[3]
    wanted = req_rows[0, 0]
    counts = req_count[0, 0]
    rows = memory.shape[1]
    mem_cols = jnp.transpose(memory.reshape(rows // LANES, LANES, MEM), (2, 0, 1))
    mail_cols = mailbox[0].T
    feat_cols = node_feat.T
    edge_cols = jnp.transpose(nbr_edge[0, 0], (1, 2, 0))

    dead = jnp.arange(slots, dtype=jnp.int32)[None, :] >= counts[:, None]
    wanted_or_dead = wanted + rows * dead.astype(jnp.int32)

    near_slot = to_slot(nbr_live[0, 0].T, counts, slots)
    root_slot = to_slot(root_live[0, 0], counts, slots)
    blocks = EV // EB
    near_index = jnp.transpose(near_slot.reshape(NBR, 3, blocks, EB), (2, 0, 1, 3))
    root_index = jnp.transpose(root_slot.reshape(3, blocks, EB), (1, 0, 2))
    index = jnp.concatenate(
        [near_index.reshape(blocks, -1), root_index.reshape(blocks, -1)], 1
    ).reshape(-1)

    edge_sent = ev_edge[0, 0].T
    early = {}

    last = len(rounds()) - 1

    def between(number, x, parts):
        if number == last - 1:
            early["asked"] = swap(after(wanted_or_dead, x))
            early["codes"] = time_codes(after(mail_time - update_time, x))
            *parts, early["asked"], early["codes"] = lax.optimization_barrier(
                (*parts, early["asked"], early["codes"])
            )
        if number == last:
            early["edges"] = swap(jnp.broadcast_to(after(edge_sent, x), (shards,) + edge_sent.shape))
        return parts

    flat = gather_params(params.astype(BF16).reshape(1, -1, LANES), between).reshape(-1, LANES)
    asked = early["asked"].reshape(-1)
    flags = (asked < rows).astype(jnp.int32)
    asked = asked % rows
    codes_m = early["codes"][0]
    wts = weights_of(flat)
    h_sent, s_rows, low = gru_forward(asked, mail_cols, codes_m, mem_cols, feat_cols, wts, shards, slots)
    h_got = swap(h_sent)

    codes_n = time_codes(nbr_dt[0, 0].T)
    edges_all = early["edges"]
    ends = root_slot[:2].reshape(-1)
    ordered = lax.sort(ends * (2 * EV) + jnp.arange(2 * EV, dtype=jnp.int32))
    end_row, partner_slot, event = bookkeeping(ordered, ends, wanted.reshape(-1))
    first = jnp.sum(
        (ordered[None, :] < (jnp.arange(LANES, dtype=jnp.int32) * (slots * 2 * EV))[:, None]).astype(jnp.int32),
        1,
    )
    notes = jnp.concatenate([end_row, event, ev_time[0, 0], first])
    digits = jnp.concatenate([notes // 128, notes % 128]).astype(BF16)
    lines = -(-digits.shape[0] // (8 * slots)) * 8
    digits = jnp.pad(digits, (0, lines * slots - digits.shape[0])).reshape(lines, slots)
    s_sent = send_rows(s_rows, asked, digits, shards, slots)
    h_got, s_sent, codes_n, edges_all, partner_slot, index = lax.optimization_barrier(
        (h_got, s_sent, codes_n, edges_all, partner_slot, index)
    )
    s_got = swap(s_sent)
    d_sent, att_grads, losses = attention(index, h_got, edge_cols, codes_n, neg_count[0], wts)
    d_sent, s_got, low = lax.optimization_barrier((d_sent, s_got, low))
    d_got = swap(d_sent)

    factors, s_cols, mem_new, upd_new = gru_factors(
        asked, flags, mail_cols, codes_m, low, mem_cols, mail_time, update_time, wts
    )
    partner = partner_rows(s_got, partner_slot)
    digits = s_got[:, WIRE:, :].reshape(shards, -1)[:, : 2 * notes.shape[0]].astype(F32).astype(jnp.int32)
    notes = digits[:, : notes.shape[0]] * 128 + digits[:, notes.shape[0] :]
    stamps = notes[:, 4 * EV : 5 * EV].reshape(shards, 1, EV)
    far = edge_tables(edges_all, stamps)
    partner = jnp.broadcast_to(partner[None], (shards,) + partner.shape)
    d_got, factors, partner, far = lax.optimization_barrier((d_got, factors, partner, far))
    partner_got = swap(partner)
    mem_grad, gru_grads, bias_grads = gru_backward(
        asked, d_got, factors, mail_cols, codes_m, low, feat_cols, wts
    )
    packed = pack(gru_grads, bias_grads, att_grads, losses)[:FLAT_ROWS]
    late = {}

    def during(number, x, parts):
        if number == 1:
            events_of = notes[:, 2 * EV : 4 * EV].reshape(-1)
            rows_of = notes[:, : 2 * EV].reshape(-1)
            starts = lax.dynamic_slice_in_dim(notes[:, 5 * EV :], me, 2, 1).reshape(-1)
            mail = deliver(
                starts, rows_of, events_of, after(partner_got, x), far, s_cols, mail_cols, mail_time
            )
            *parts, late["mail"], late["stamp"] = lax.optimization_barrier((*parts, *mail))
        return parts

    shard = scatter_sum(packed, during)
    mail_new, stamp_new = late["mail"], late["stamp"]

    number = lax.axis_index("batch") * shards + me
    size = shard.shape[0] * LANES
    place = number * size + jnp.arange(size, dtype=jnp.int32).reshape(-1, LANES)
    grad = jnp.where(place < USED, shard, 0.0)
    lines = [
        jnp.sum(grad * grad, 0, keepdims=True),
        jnp.sum(jnp.where(place == USED, shard, 0.0), 0, keepdims=True),
        jnp.sum(jnp.where(place == USED + 1, shard, 0.0), 0, keepdims=True),
        jnp.zeros((5, LANES), F32),
    ]
    values = jnp.sum(sum_all(jnp.concatenate(lines, 0)), 1)
    grad_norm = jnp.sqrt(values[0])
    clipped = grad.reshape(-1) * jnp.minimum(1.0, clip_limit / (grad_norm + 1e-06))
    moment1_new = beta_first * moment1 + (1.0 - beta_first) * clipped
    moment2_new = beta_second * moment2 + (1.0 - beta_second) * clipped * clipped
    ratio = (
        moment1_new
        / (1.0 - beta_first**STEP)
        / (jnp.sqrt(moment2_new / (1.0 - beta_second**STEP)) + adam_floor)
    )
    params_new = params - learn_rate * (ratio + decay_rate * params)
    return (
        values[1],
        values[2],
        grad_norm,
        params_new,
        moment1_new,
        moment2_new,
        params_new.astype(BF16),
        jnp.transpose(mem_new, (1, 2, 0)).reshape(memory.shape),
        mail_new.T[None],
        stamp_new,
        upd_new,
        jnp.transpose(mem_grad, (1, 2, 0)).reshape(memory.shape),
    )


def solution(mesh):
    both, split = P(("batch", "node")), P("batch", "node")
    in_specs = (both, both, both, split, split, split, split, P("node")) + (split,) * 9
    out_specs = (P(), P(), P()) + (both,) * 4 + (split,) * 5
    return jax.shard_map(body, mesh=mesh, in_specs=in_specs, out_specs=out_specs, check_vma=False)
```

```python
import functools
import math

import jax
import jax.numpy as jnp
import numpy as np
from jax import lax
from jax.experimental import pallas as pl
from jax.experimental.pallas import tpu as pltpu
from jax.sharding import PartitionSpec as P

MEM = 100
TENC = 100
EDGE = 186
NFEAT = 413
NBR = 10
STEP = 5
EV = 512
MAIL = 386
FLAT = 360448

clip_limit = 1.0
learn_rate = 0.02
beta_first = 0.5
beta_second = 0.6
adam_floor = 1e-08
decay_rate = 0.01

F32 = jnp.float32
BF16 = jnp.bfloat16
LANES = 128
PAD = 112
HALF = 56
WIRE = 104
GATES = 3 * PAD
KV = 4 * HALF
EB = 128
SECT = 3 * EB
STREAMS = 8
VMEM_LIMIT = 63_000_000

ROW_HH = 1458
ROW_NF = 1758
ROW_Q = 2171
ROW_KV = 2371
ROW_O = 3143
ROW_SRC = 3343
ROW_DST = 3443
ROW_OUT = 3543
ROW_BIH = 3544
ROW_BHH = 3547
ROW_BO = 3550
ROW_GAIN = 3551
ROW_SHIFT = 3552
ROW_BPRED = 3553
ROW_BOUT = 3554
USED = 355401
FLAT_ROWS = FLAT // LANES
PERIODS = 113
WROWS = 32 * PERIODS
GRU_ROWS = 2176
ATT_BASE = 2168
ATT_ROWS = 1448

FREQS = np.float32(10.0 ** (-9.0 * np.arange(TENC) / (TENC - 1)))

VMEM = pl.BlockSpec(memory_space=pltpu.VMEM)
SMEM = pl.BlockSpec(memory_space=pltpu.SMEM)


def params_of(limit=VMEM_LIMIT):
    return pltpu.CompilerParams(vmem_limit_bytes=limit)


def dot(left, right, left_dim=1, right_dim=0):
    return lax.dot_general(
        left, right, (((left_dim,), (right_dim,)), ((), ())), preferred_element_type=F32
    )


def fit_cosine():
    u = np.cos(np.pi * (np.arange(4000) + 0.5) / 4000) * 0.5 + 0.5
    u = u * (np.pi**2 * 1.002)
    fit = np.polynomial.chebyshev.Chebyshev.fit(u, np.cos(np.sqrt(u)), 7, domain=[0, np.pi**2 * 1.002])
    return [float(np.float32(c)) for c in fit.convert(kind=np.polynomial.Polynomial).coef]


COSINE = fit_cosine()


def cosine(x):
    turns = jnp.floor(x * np.float32(0.5 / np.pi) + 0.5)
    x = x - turns * np.float32(6.28125)
    x = x - turns * np.float32(2 * np.pi - 6.28125)
    u = x * x
    total = jnp.full_like(u, COSINE[-1])
    for c in COSINE[-2::-1]:
        total = total * u + np.float32(c)
    return total


def sigmoid(x):
    return 0.5 * jnp.tanh(0.5 * x) + 0.5


GELU_C = math.sqrt(2.0 / math.pi)


def gelu(x):
    t = jnp.tanh(GELU_C * (x + 0.044715 * (x * x * x)))
    return 0.5 * x * (1.0 + t)


def gelu_slope(x):
    x2 = x * x
    t = jnp.tanh(GELU_C * (x + 0.044715 * (x2 * x)))
    return 0.5 * (1.0 + t) + 0.5 * x * (1.0 - t * t) * (GELU_C * (1.0 + 3 * 0.044715 * x2))


def lane_of(shape):
    return lax.broadcasted_iota(jnp.int32, shape, len(shape) - 1)


def row_of(shape):
    return lax.broadcasted_iota(jnp.int32, shape, len(shape) - 2)


def roll_left(x, amount):
    amount = amount % LANES
    return x if amount == 0 else pltpu.roll(x, LANES - amount, 1)


def spread_heads(x):
    lane = lane_of(x.shape)
    moved = roll_left(x, -6)
    return jnp.where(lane < 50, x, jnp.where((lane >= 56) & (lane < 106), moved, 0.0))


def join_heads(x):
    lane = lane_of(x.shape)
    return jnp.where(lane < 50, x, jnp.where(lane < 100, roll_left(x, 6), 0.0))


def codes_kernel(delta, freq, out):
    freqs = freq[...]
    extra = out.shape[1] - TENC
    if extra:
        tail = (row_of((extra, LANES)) == 0).astype(F32)
    for k in range(out.shape[0]):

        def one(i, carry, k=k):
            at = pl.ds(pl.multiple_of(i * LANES, LANES), LANES)
            value = cosine(delta[k : k + 1, at].astype(F32) * freqs)
            if extra:
                value = jnp.concatenate([value, tail], 0)
            out[k, :, at] = value.astype(BF16)
            return carry

        lax.fori_loop(0, delta.shape[1] // LANES, one, 0)


def time_codes(delta, lines=TENC):
    freq = jnp.asarray(np.tile(FREQS[:, None], (1, LANES)))
    rows, count = delta.shape
    return pl.pallas_call(
        codes_kernel,
        out_shape=jax.ShapeDtypeStruct((rows, lines, count), BF16),
        in_specs=[VMEM] * 2,
        out_specs=VMEM,
        compiler_params=params_of(16 * 2**20),
        cost_estimate=pl.CostEstimate(
            flops=rows * count * 3000, bytes_accessed=rows * count * 200, transcendentals=0
        ),
    )(delta, freq)


def unpack_weights(
    flat,
    w_mail,
    w_two,
    w_hid,
    w_feat,
    kv_h,
    kv_e,
    kv_t,
    q_h,
    q_one,
    o_att,
    o_att_n,
    o_h,
    src_t,
    src_n,
    dst_t,
    dst_n,
    cols,
    wide,
    rows,
):
    wide[0:FLAT_ROWS, :] = flat[...].astype(F32)
    wide[FLAT_ROWS:, :] = jnp.zeros((wide.shape[0] - FLAT_ROWS, LANES), F32)
    lane = lane_of((PERIODS, LANES))
    for j in range(32):
        first, shift = divmod(100 * j, LANES)
        out = roll_left(wide[pl.ds(first, PERIODS, stride=25), :], shift)
        if shift + 100 > LANES:
            after = roll_left(wide[pl.ds(first + 1, PERIODS, stride=25), :], shift)
            out = jnp.where(lane < LANES - shift, out, after)
        rows[pl.ds(j, PERIODS, stride=32), :] = jnp.where(lane < 100, out, 0.0)

    def turned(start, count, stride=1):
        size = -(-count // LANES) * LANES
        if stride == 1:
            block = rows[start : start + size, :]
        else:
            block = rows[pl.ds(start, size, stride=stride), :]
        return jnp.where(row_of((size, LANES)) < count, block, 0.0).T

    def column(r):
        return jnp.broadcast_to(rows[r : r + 1, :], (LANES, LANES)).T[:PAD, :]

    at_bias = lane_of((PAD, LANES)) == MEM
    for g in range(3):
        to = slice(PAD * g, PAD * g + PAD)
        w_mail[to, :] = turned(g, MAIL, 3)[:PAD, :MAIL].astype(BF16)
        time = jnp.where(at_bias, column(ROW_BIH + g), turned(3 * MAIL + g, TENC, 3)[:PAD])
        hid = jnp.where(at_bias, column(ROW_BHH + g), turned(ROW_HH + g, MEM, 3)[:PAD])
        time, hid = time[:, :PAD].astype(BF16), hid[:, :PAD].astype(BF16)
        none = jnp.zeros((PAD, PAD), BF16)
        if g < 2:
            w_two[to, :] = jnp.concatenate([time, hid], 1)
            w_hid[to, :] = hid
        else:
            w_two[to, :] = jnp.concatenate([time, none], 1)
            w_hid[to, :] = none
            last = slice(PAD * 3, PAD * 4)
            w_two[last, :] = jnp.concatenate([none, hid], 1)
            w_hid[last, :] = hid
    w_feat[...] = turned(ROW_NF, NFEAT)[:PAD, :NFEAT].astype(BF16)
    for part in range(2):
        to = slice(PAD * part, PAD * part + PAD)

        def heads(start, count, part=part):
            size = -(-count // LANES) * LANES
            block = spread_heads(rows[pl.ds(ROW_KV + 2 * start + part, size, stride=2), :])
            return jnp.where(row_of((size, LANES)) < count, block, 0.0).T[:PAD]

        kv_h[to, :] = heads(0, MEM).astype(BF16)
        kv_e[to, :] = heads(MEM, EDGE)[:, :EDGE].astype(BF16)
        kv_t[to, :] = heads(MEM + EDGE, TENC)[:, :TENC].astype(BF16)
    q_rows = spread_heads(rows[ROW_Q : ROW_Q + LANES, :])
    keep = row_of((LANES, LANES)) < 100
    q_h[...] = jnp.where(keep, q_rows, 0.0).T[:PAD].astype(BF16)
    q_two = spread_heads(rows[ROW_Q + 100 : ROW_Q + 100 + LANES, :])
    q_sum = jnp.sum(jnp.where(keep, q_two, 0.0), 0, keepdims=True)
    q_one[...] = jnp.broadcast_to(q_sum, (LANES, LANES)).T[:PAD]
    att = spread_heads(turned(ROW_O, 100))
    o_att[...] = att[:PAD, :PAD].astype(BF16)
    o_att_n[...] = att.T[:PAD, :PAD].astype(BF16)
    o_h[...] = turned(ROW_O + 100, 100)[:PAD].astype(BF16)
    for start, out_t, out_n in ((ROW_SRC, src_t, src_n), (ROW_DST, dst_t, dst_n)):
        block = turned(start, 100)
        out_t[...] = block[:PAD, :PAD].astype(BF16)
        out_n[...] = block.T[:PAD, :PAD].astype(BF16)
    for i, r in enumerate((ROW_BO, ROW_GAIN, ROW_SHIFT, ROW_BPRED, ROW_OUT)):
        cols[i, :, :] = column(r)
    first = rows[ROW_BOUT : ROW_BOUT + 1, :]
    value = jnp.sum(jnp.where(lane_of((1, LANES)) == 0, first, 0.0), 1, keepdims=True)
    cols[5, :, :] = jnp.broadcast_to(value, (PAD, LANES))


WEIGHTS = [
    ((GATES, MAIL), BF16),
    ((4 * PAD, 2 * PAD), BF16),
    ((4 * PAD, PAD), BF16),
    ((PAD, NFEAT), BF16),
    ((KV, LANES), BF16),
    ((KV, EDGE), BF16),
    ((KV, TENC), BF16),
    ((PAD, LANES), BF16),
    ((PAD, LANES), F32),
    ((PAD, PAD), BF16),
    ((PAD, PAD), BF16),
    ((PAD, LANES), BF16),
    ((PAD, PAD), BF16),
    ((PAD, PAD), BF16),
    ((PAD, PAD), BF16),
    ((PAD, PAD), BF16),
    ((6, PAD, LANES), F32),
]


def gather_loop(index, table, out, count, base=0, to=0):
    group = 32

    def step(i, carry):
        for g in range(group // 16):
            at = pl.multiple_of(i * group + g * 16, 16)
            picked = [table[pl.ds(index[base + at + u], 1), :] for u in range(16)]
            out[pl.ds(to + at, 16), :] = jnp.concatenate(picked, 0).astype(out.dtype)
        return carry

    lax.fori_loop(0, count // group, step, 0)


def gather_turned(index, table, out, finished=None):
    slots = out.shape[2]
    pieces = slots // LANES

    def one(owner, carry):
        def step(j, inner):
            at = pl.ds(pl.multiple_of(j * LANES, LANES), LANES)
            base = owner * slots + j * LANES
            groups = []
            for g in range(LANES // 8):
                picked = [table[pl.ds(index[base + g * 8 + u], 1), :] for u in range(8)]
                groups.append(jnp.concatenate(picked, 0))
            out[owner, 0:WIRE, at] = jnp.concatenate(groups, 0).T[:WIRE].astype(BF16)
            return inner

        lax.fori_loop(0, pieces, step, 0, unroll=min(2, pieces))
        if finished is not None:
            finished(owner)
        return carry

    lax.fori_loop(0, out.shape[0], one, 0)


def turn_into(got, table):
    slots = got.shape[2]
    pieces = slots // LANES
    short = jnp.zeros((LANES - WIRE, LANES), F32)

    def step(j, carry):
        owner = j // pieces
        at = pl.ds(pl.multiple_of((j - owner * pieces) * LANES, LANES), LANES)
        block = jnp.concatenate([got[owner, 0:WIRE, at].astype(F32), short], 0)
        table[pl.ds(pl.multiple_of(j * LANES, LANES), LANES), :] = block.T
        return carry

    lax.fori_loop(0, got.shape[0] * pieces, step, 0, unroll=8)


def to_rows(block):
    full = jnp.concatenate([block, jnp.zeros((LANES - PAD, LANES), F32)], 0)
    return full.T


def mem_piece(mem, i):
    return mem.reshape(MEM * 8, LANES)[pl.ds(i, MEM, stride=8), :]


def gate_products(mail, two, w_mail, w_two):
    both = dot(w_two[...], two)
    first = both[:GATES] + dot(w_mail[...], mail)
    return first[:PAD], first[PAD : 2 * PAD], first[2 * PAD :], both[GATES:]


def gates_at(at, sums, low, s=None):
    gr, gz, gn, hn = (x[:, at] for x in sums)
    r = sigmoid(gr)
    z = sigmoid(gz)
    n = jnp.tanh(gn + r * hn)
    if s is None:
        s = low[:, at].astype(F32)
    return r, z, n, hn, s, (1.0 - z) * n + z * s


def gru_kernel(index, flat, mail_in, phi_in, mem_in, feat_in, *refs):
    wts, rest = refs[: len(WEIGHTS)], refs[len(WEIGHTS) :]
    sent_out, low_out, s_out = rest[:3]
    wide, rows, mail, two, mem, feat, s_cols, table, sent, in_sems, out_sems, sent_sems = rest[3:]
    w_mail, w_two, w_hid, w_feat = wts[:4]
    nodes = mail.shape[1]
    half = nodes // 2
    copies = []
    for part in range(2):
        cols = slice(part * half, part * half + half)
        lines = slice(part * half // LANES, (part + 1) * half // LANES)
        pairs = [(r.at[:, cols], v.at[:, cols]) for r, v in ((mail_in, mail), (feat_in, feat))]
        pairs.append((phi_in.at[:, cols], two.at[0:PAD, cols]))
        pairs.append((mem_in.at[:, lines, :], mem.at[:, lines, :]))
        copies.append([pltpu.make_async_copy(r, v, in_sems.at[part, i]) for i, (r, v) in enumerate(pairs)])
        for copy in copies[-1]:
            copy.start()
    unpack_weights(flat, *wts, wide, rows)
    sub = 256
    real = row_of((PAD, sub)) < MEM
    ones = (row_of((PAD, sub)) == MEM).astype(F32)
    short = jnp.zeros((PAD - MEM, sub), F32)
    for part in range(2):
        for copy in copies[part]:
            copy.wait()

        def piece(j, carry):
            start = pl.multiple_of(j * sub, sub)
            at = pl.ds(start, sub)
            lows = []
            for i in range(sub // LANES):
                line = j * (sub // LANES) + i
                lows.append(mem.reshape(MEM * (nodes // LANES), LANES)[pl.ds(line, MEM, stride=nodes // LANES), :])
            full = jnp.concatenate([jnp.concatenate(lows, 1), short], 0)
            low_now = full.astype(BF16)
            two[PAD : 2 * PAD, at] = jnp.where(real, full, ones).astype(BF16)
            sums = gate_products(mail[:, at], two[:, at], w_mail, w_two)
            nf = dot(w_feat[...], feat[:, at])
            for i in range(sub // LANES):
                here = slice(i * LANES, i * LANES + LANES)
                _, _, _, _, _, renewed = gates_at(here, sums, low_now)
                hidden = (renewed + nf[:, here]).astype(BF16).astype(F32)
                to = pl.ds(pl.multiple_of(start + i * LANES, LANES), LANES)
                table[to, :] = to_rows(hidden)
                s_cols[:, to] = renewed[:MEM].astype(BF16)
            return carry

        lax.fori_loop(part * half // sub, (part + 1) * half // sub, piece, 0, unroll=4)
    outs = [
        pltpu.make_async_copy(two.at[PAD : 2 * PAD, :], low_out, out_sems.at[0]),
        pltpu.make_async_copy(s_cols, s_out, out_sems.at[1]),
    ]
    for copy in outs:
        copy.start()

    def done(owner):
        return pltpu.make_async_copy(sent.at[owner], sent_out.at[owner], sent_sems.at[owner])

    gather_turned(index, table, sent, lambda owner: done(owner).start())

    def settle(owner, carry):
        done(owner).wait()
        return carry

    lax.fori_loop(0, sent.shape[0], settle, 0)
    for copy in outs:
        copy.wait()


BLOCK = 1024


def cols_spec(rows):
    return pl.BlockSpec((rows, BLOCK), lambda i: (0, i))


def mem_spec():
    return pl.BlockSpec((MEM, BLOCK // LANES, LANES), lambda i: (0, i, 0))


HBM = pl.BlockSpec(memory_space=pl.ANY)


def gru_forward(index, flat, mail, phi, mem, feat, shards, slots):
    rows = mail.shape[1]
    shapes = [jax.ShapeDtypeStruct(s, d) for s, d in WEIGHTS]
    shapes += [
        jax.ShapeDtypeStruct((shards, WIRE, slots), BF16),
        jax.ShapeDtypeStruct((PAD, rows), BF16),
        jax.ShapeDtypeStruct((MEM, rows), BF16),
    ]
    got = pl.pallas_call(
        gru_kernel,
        out_shape=shapes,
        in_specs=[SMEM, VMEM] + [HBM] * 4,
        out_specs=[VMEM] * len(WEIGHTS) + [HBM] * 3,
        scratch_shapes=[
            pltpu.VMEM((FLAT_ROWS + 16, LANES), F32),
            pltpu.VMEM((WROWS + 512, LANES), F32),
            pltpu.VMEM((MAIL, rows), BF16),
            pltpu.VMEM((2 * PAD, rows), BF16),
            pltpu.VMEM((MEM, rows // LANES, LANES), F32),
            pltpu.VMEM((NFEAT, rows), BF16),
            pltpu.VMEM((MEM, rows), BF16),
            pltpu.VMEM((rows, LANES), F32),
            pltpu.VMEM((shards, WIRE, slots), BF16),
            pltpu.SemaphoreType.DMA((2, 4)),
            pltpu.SemaphoreType.DMA((2,)),
            pltpu.SemaphoreType.DMA((shards,)),
        ],
        compiler_params=params_of(),
        cost_estimate=pl.CostEstimate(flops=4_000_000_000, bytes_accessed=24_000_000, transcendentals=3_000_000),
    )(index, flat, mail, phi, mem, feat)
    return got[: len(WEIGHTS)], *got[len(WEIGHTS) :]


def send_kernel(index, s_cols, notes, out, table):
    for owner in range(out.shape[0]):
        out[owner, WIRE:, :] = notes[...]
    short = jnp.zeros((LANES - MEM, LANES), F32)

    def step(j, carry):
        at = pl.ds(pl.multiple_of(j * LANES, LANES), LANES)
        table[at, :] = jnp.concatenate([s_cols[:, at].astype(F32), short], 0).T
        return carry

    lax.fori_loop(0, table.shape[0] // LANES, step, 0, unroll=8)
    gather_turned(index, table, out)


def send_rows(s_cols, index, notes, shards, slots):
    return pl.pallas_call(
        send_kernel,
        out_shape=jax.ShapeDtypeStruct((shards, WIRE + notes.shape[0], slots), BF16),
        in_specs=[SMEM, VMEM, VMEM],
        out_specs=VMEM,
        scratch_shapes=[pltpu.VMEM((s_cols.shape[1], LANES), F32)],
        compiler_params=params_of(24 * 2**20),
        cost_estimate=pl.CostEstimate(flops=8_000_000, bytes_accessed=6_000_000, transcendentals=0),
    )(index, s_cols, notes)


def partner_kernel(index, got, out, table, rows):
    turn_into(got, table)
    gather_loop(index, table, rows, index.shape[0])
    flag = lane_of((LANES, LANES)) == MEM
    for i in range(index.shape[0] // LANES):
        at = slice(i * LANES, i * LANES + LANES)
        block = jnp.where(flag, 1.0, rows[at, :]).T[:WIRE].astype(BF16)

        def copy(owner, carry, at=at, block=block):
            out[owner, :, at] = block
            return carry

        lax.fori_loop(0, out.shape[0], copy, 0)


def partner_rows(got, index, shards):
    return pl.pallas_call(
        partner_kernel,
        out_shape=jax.ShapeDtypeStruct((shards, WIRE, index.shape[0]), BF16),
        in_specs=[SMEM, VMEM],
        out_specs=VMEM,
        scratch_shapes=[
            pltpu.VMEM((got.shape[0] * got.shape[2], LANES), F32),
            pltpu.VMEM((index.shape[0], LANES), F32),
        ],
        compiler_params=params_of(44 * 2**20),
        cost_estimate=pl.CostEstimate(flops=2_000_000, bytes_accessed=2_000_000, transcendentals=0),
    )(index, got)


def book_kernel(ordered, ends, wanted, row, partner, event):
    count = ordered.shape[0]

    def step(i, carry):
        for u in range(8):
            at = i * 8 + u
            key = ordered[at]
            end = jnp.bitwise_and(key, count - 1)
            row[at] = wanted[lax.shift_right_logical(key, count.bit_length() - 1)]
            partner[at] = ends[jnp.bitwise_xor(end, count // 2)]
            event[at] = jnp.bitwise_and(end, count // 2 - 1)
        return carry

    lax.fori_loop(0, count // 8, step, 0)


def bookkeeping(ordered, ends, wanted):
    shape = jax.ShapeDtypeStruct(ordered.shape, jnp.int32)
    return pl.pallas_call(
        book_kernel,
        out_shape=(shape, shape, shape),
        in_specs=[SMEM] * 3,
        out_specs=(SMEM,) * 3,
        compiler_params=params_of(),
        cost_estimate=pl.CostEstimate(flops=4_000_000, bytes_accessed=60_000, transcendentals=0),
    )(ordered, ends, wanted)


def factor_kernel(
    mail, phi, low, mem, live_in, mail_time, update_time, w_mail, w_two, factors, mem_new, time_new
):
    sub = 256
    for j in range(BLOCK // sub):
        part = slice(j * sub, j * sub + sub)
        sums = gate_products(mail[:, part], jnp.concatenate([phi[:, part], low[:, part]], 0), w_mail, w_two)
        for i in range(sub // LANES):
            there = slice(i * LANES, i * LANES + LANES)
            at = slice(j * sub + i * LANES, j * sub + i * LANES + LANES)
            s_low = jnp.where(row_of((PAD, LANES)) < MEM, low[:, at].astype(F32), 0.0)
            r, z, n, hn, s, renewed = gates_at(there, sums, None, s_low)
            live = live_in[:, at] > 0.5
            an = (1.0 - z) * (1.0 - n * n)
            factors[0, :, at] = (an * hn * (r * (1.0 - r))).astype(BF16)
            factors[1, :, at] = ((s - n) * (z * (1.0 - z))).astype(BF16)
            factors[2, :, at] = an.astype(BF16)
            factors[3, :, at] = r.astype(BF16)
            factors[4, :, at] = z.astype(BF16)
            line = (j * sub) // LANES + i
            value = jnp.where(live, renewed[:MEM], mem_piece(mem, line))
            mem_new.reshape(MEM * 8, LANES)[pl.ds(line, MEM, stride=8), :] = value
            time_new[:, at] = jnp.where(live, mail_time[:, at], update_time[:, at])


def gru_factors(mail, phi, low, mem, live, mail_time, update_time, wts):
    rows = mail.shape[1]
    return pl.pallas_call(
        factor_kernel,
        grid=(rows // BLOCK,),
        out_shape=(
            jax.ShapeDtypeStruct((5, PAD, rows), BF16),
            jax.ShapeDtypeStruct((MEM, rows // LANES, LANES), F32),
            jax.ShapeDtypeStruct((1, rows), jnp.int32),
        ),
        in_specs=[cols_spec(MAIL), cols_spec(PAD), cols_spec(PAD), mem_spec()]
        + [cols_spec(1)] * 3
        + [VMEM] * 2,
        out_specs=(
            pl.BlockSpec((5, PAD, BLOCK), lambda i: (0, 0, i)),
            mem_spec(),
            cols_spec(1),
        ),
        compiler_params=params_of(),
        cost_estimate=pl.CostEstimate(flops=3_000_000_000, bytes_accessed=34_000_000, transcendentals=3_000_000),
    )(mail, phi, low, mem, live, mail_time, update_time, wts[0], wts[1])


def gru_back_kernel(
    index,
    got,
    w_hid,
    factors_in,
    mail_in,
    phi_in,
    low_in,
    feat_in,
    grads,
    biases,
    grad_out,
    factors,
    mail,
    two,
    feat,
    mem_grad,
    wide,
    placed,
    d_one,
    d_two,
    a_mail,
    a_two,
    a_feat,
    in_sems,
    out_sems,
):
    pairs = ((factors_in, factors), (mail_in, mail), (phi_in, two.at[0:PAD, :]), (low_in, two.at[PAD : 2 * PAD, :]), (feat_in, feat))
    copies = [pltpu.make_async_copy(r, v, in_sems.at[i]) for i, (r, v) in enumerate(pairs)]
    for copy in copies:
        copy.start()
    turn_into(got, wide)
    count = wide.shape[0]
    if count != placed.shape[0]:
        placed[...] = jnp.zeros_like(placed)
    group = 32

    def move(i, carry):
        for u in range(group):
            at = i * group + u
            placed[pl.ds(index[at], 1), :] = wide[pl.ds(at, 1), :]
        return carry

    lax.fori_loop(0, count // group, move, 0)
    for ref in (a_mail, a_two, a_feat):
        ref[...] = jnp.zeros_like(ref)
    for copy in copies:
        copy.wait()
    nodes = mail.shape[1]
    lines = nodes // LANES

    def out_copy(step):
        part = pl.ds(step * (BLOCK // LANES), BLOCK // LANES)
        return pltpu.make_async_copy(mem_grad.at[:, part, :], grad_out.at[:, part, :], out_sems.at[step])

    def block(step, d_all):
        start = pl.multiple_of(step * BLOCK, BLOCK)
        for i in range(BLOCK // LANES):
            at = slice(i * LANES, i * LANES + LANES)
            there = pl.ds(pl.multiple_of(start + i * LANES, LANES), LANES)
            d = placed[there, :].T[:PAD]
            dn = d * factors[2, :, there]
            for part, value in enumerate(
                (d * factors[0, :, there], d * factors[1, :, there], dn, dn * factors[3, :, there], d)
            ):
                d_all[PAD * part : PAD * part + PAD, at] = value.astype(BF16)
        gates, dlow = d_all[0 : 4 * PAD, :], d_all[4 * PAD :, :]
        there = pl.ds(start, BLOCK)
        a_mail[:, :MAIL] += dot(gates[:GATES], mail[:, there], 1, 1)
        a_two[:, : 2 * PAD] += dot(gates, two[:, there], 1, 1)
        a_feat[:, :NFEAT] += dot(dlow, feat[:, there], 1, 1)
        direct = dlow.astype(F32) * factors[4, :, there].astype(F32) + dot(w_hid[...], gates, 0, 0)
        for i in range(BLOCK // LANES):
            line = pl.ds(step * (BLOCK // LANES) + i, MEM, stride=lines)
            mem_grad.reshape(MEM * lines, LANES)[line, :] = direct[:MEM, i * LANES : i * LANES + LANES]
        out_copy(step).start()

    def two_blocks(i, carry):
        block(2 * i, d_one)
        block(2 * i + 1, d_two)
        return carry

    lax.fori_loop(0, nodes // BLOCK // 2, two_blocks, 0)

    def turned_back(block):
        return jnp.concatenate([block, jnp.zeros((LANES - PAD, block.shape[1]), F32)], 0).T

    grads[ROW_Q:GRU_ROWS, :] = jnp.zeros((GRU_ROWS - ROW_Q, LANES), F32)
    lines_of = []
    for g in range(3):
        rows = slice(PAD * g, PAD * g + PAD)
        grads[pl.ds(g, MAIL, stride=3), :] = turned_back(a_mail[rows, :])[:MAIL]
        both = turned_back(a_two[rows, :])
        grads[pl.ds(3 * MAIL + g, TENC, stride=3), :] = both[:TENC]
        lines_of.append(both[MEM : MEM + 1])
        if g == 2:
            both = turned_back(a_two[GATES:, :])
        wide[0 : 2 * LANES, :] = both
        grads[pl.ds(ROW_HH + g, MEM, stride=3), :] = wide[PAD : PAD + MEM, :]
    hidden_bias = wide[PAD + MEM : PAD + MEM + 1, :]
    grads[ROW_NF:ROW_Q, :] = turned_back(a_feat[...])[:NFEAT]
    sums = lines_of + lines_of[:2] + [hidden_bias]
    biases[...] = jnp.concatenate(sums + [jnp.zeros((2, LANES), F32)], 0)

    def settle(step, carry):
        out_copy(step).wait()
        return carry

    lax.fori_loop(0, nodes // BLOCK, settle, 0)


def gru_backward(index, got, factors, mail, phi, low, feat, wts):
    rows = mail.shape[1]
    return pl.pallas_call(
        gru_back_kernel,
        out_shape=(
            jax.ShapeDtypeStruct((GRU_ROWS, LANES), F32),
            jax.ShapeDtypeStruct((8, LANES), F32),
            jax.ShapeDtypeStruct((MEM, rows // LANES, LANES), F32),
        ),
        in_specs=[SMEM, VMEM, VMEM] + [HBM] * 5,
        out_specs=(VMEM, VMEM, HBM),
        scratch_shapes=[
            pltpu.VMEM((5, PAD, rows), BF16),
            pltpu.VMEM((MAIL, rows), BF16),
            pltpu.VMEM((2 * PAD, rows), BF16),
            pltpu.VMEM((NFEAT, rows), BF16),
            pltpu.VMEM((MEM, rows // LANES, LANES), F32),
            pltpu.VMEM((got.shape[0] * got.shape[2], LANES), F32),
            pltpu.VMEM((rows, LANES), F32),
            pltpu.VMEM((5 * PAD, BLOCK), BF16),
            pltpu.VMEM((5 * PAD, BLOCK), BF16),
            pltpu.VMEM((GATES, 512), F32),
            pltpu.VMEM((4 * PAD, 256), F32),
            pltpu.VMEM((PAD, 512), F32),
            pltpu.SemaphoreType.DMA((5,)),
            pltpu.SemaphoreType.DMA((rows // BLOCK,)),
        ],
        compiler_params=params_of(),
        cost_estimate=pl.CostEstimate(flops=5_000_000_000, bytes_accessed=36_000_000, transcendentals=0),
    )(index, got, wts[2], factors, mail, phi, low, feat)


def attention_kernel(
    index,
    got,
    e0,
    e1,
    e2,
    p0,
    p1,
    p2,
    weight,
    kv_h,
    kv_e,
    kv_t,
    q_h,
    q_one,
    o_att,
    o_att_n,
    o_h,
    src_t,
    src_n,
    dst_t,
    dst_n,
    cols,
    sent,
    grads,
    losses,
    table,
    kv,
    d_rows,
    d_two,
    a_kvh,
    a_kve,
    a_kvt,
    a_qh,
    a_q1,
    a_oa,
    a_oh,
    a_src,
    a_dst,
    a_col,
    a_one,
    *rest,
):
    lanes, picks = rest[:STREAMS], rest[STREAMS:]
    step = pl.program_id(0)
    near = NBR * SECT
    total = near + SECT
    scale = 50 ** (-0.5)
    sums = (a_kvh, a_kve, a_kvt, a_qh, a_q1, a_oa, a_oh, a_src, a_dst, a_col, a_one)

    @pl.when(step == 0)
    def _():
        turn_into(got, table)
        for ref in sums + lanes:
            ref[...] = jnp.zeros_like(ref)

    at_block = step * total
    gather_loop(index, table, picks[NBR], SECT, at_block + near)
    gather_loop(index, table, picks[0], SECT, at_block)
    roots = picks[NBR][...]

    def edge_of(k):
        return jnp.concatenate([e0[k], e1[k], e2[k]], 1)

    def code_of(k):
        return jnp.concatenate([p0[k], p1[k], p2[k]], 1)

    for k in range(NBR):
        kv[k] = (
            dot(kv_h[...], picks[k][...], 1, 1)
            + dot(kv_e[...], edge_of(k))
            + dot(kv_t[...], code_of(k))
        )
        if k + 1 < NBR:
            for g in range(SECT // 16):
                first = (k + 1) * SECT + g * 16
                rows = [table[pl.ds(index[at_block + first + u], 1), :] for u in range(16)]
                picks[k + 1][g * 16 : g * 16 + 16, :] = jnp.concatenate(rows, 0).astype(BF16)
    query = dot(q_h[...], roots, 1, 1)
    o_root = dot(o_h[...], roots, 1, 1)
    bo, gain, shift, bpred, wout = (cols[i] for i in range(5))
    bout = cols[5, 0:1, :]
    real = row_of((PAD, LANES)) < MEM
    queries, probs, atts, pres, embs, norms = [], [], [], [], [], []
    for t in range(3):
        at = slice(t * EB, t * EB + EB)
        q = query[:, at] + q_one[...]
        scores = [[], []]
        for k in range(NBR):
            both = q * kv[k, 0:PAD, at]
            for h in range(2):
                scores[h].append(jnp.sum(both[h * HALF : h * HALF + HALF], 0, keepdims=True) * scale)
        weights = []
        for h in range(2):
            top = functools.reduce(jnp.maximum, scores[h])
            parts = [jnp.exp(x - top) for x in scores[h]]
            whole = functools.reduce(jnp.add, parts)
            weights.append([x / whole for x in parts])
        heads = []
        for h in range(2):
            rows = slice(PAD + h * HALF, PAD + h * HALF + HALF)
            heads.append(
                functools.reduce(jnp.add, [weights[h][k] * kv[k, rows, at] for k in range(NBR)])
            )
        att = jnp.concatenate(heads, 0).astype(BF16)
        pre = dot(o_att[...], att) + o_root[:, at] + bo
        active = gelu(pre)
        mean = jnp.sum(active, 0, keepdims=True) * (1.0 / MEM)
        centre = jnp.where(real, active - mean, 0.0)
        spread = jnp.sum(centre * centre, 0, keepdims=True) * (1.0 / MEM)
        inverse = lax.rsqrt(spread + 1e-05)
        hat = centre * inverse
        queries.append(q)
        probs.append(weights)
        atts.append(att)
        pres.append(pre)
        norms.append((hat, inverse))
        embs.append((hat * gain + shift).astype(BF16))

    src_proj = dot(src_t[...], embs[0]) + bpred
    tails = [src_proj + dot(dst_t[...], embs[1]), src_proj + dot(dst_t[...], embs[2])]
    acts = [gelu(x).astype(BF16) for x in tails]
    logits = [jnp.sum(x.astype(F32) * wout, 0, keepdims=True) + bout for x in acts]
    neg_weight = weight[...].astype(F32)

    def softplus(x):
        return jnp.maximum(x, 0.0) + jnp.log1p(jnp.exp(-jnp.abs(x)))

    d_pos = -sigmoid(-logits[0])
    d_neg = neg_weight * sigmoid(logits[1])
    a_one[0:1, :] += softplus(-logits[0]) + neg_weight * softplus(logits[1])
    a_one[1:2, :] += 1.0 + neg_weight
    a_one[2:3, :] += d_pos + d_neg
    d_logits = [x.astype(BF16).astype(F32) for x in (d_pos, d_neg)]
    a_col[4] += acts[0].astype(F32) * d_logits[0] + acts[1].astype(F32) * d_logits[1]
    d_tails = [wout * d * gelu_slope(x) for d, x in zip(d_logits, tails)]
    d_src = d_tails[0] + d_tails[1]
    a_col[3] += d_src
    d_low = [x.astype(BF16) for x in (d_src, d_tails[0], d_tails[1])]
    a_src[...] += dot(embs[0], d_low[0], 1, 1)
    a_dst[...] += dot(embs[1], d_low[1], 1, 1) + dot(embs[2], d_low[2], 1, 1)
    d_embs = [dot(src_n[...], d_low[0]), dot(dst_n[...], d_low[1]), dot(dst_n[...], d_low[2])]

    d_outs, d_queries = [], []
    for t in range(3):
        at = slice(t * EB, t * EB + EB)
        hat, inverse = norms[t]
        d_emb = d_embs[t]
        a_col[1] += d_emb * hat
        a_col[2] += d_emb
        d_hat = d_emb * gain
        mean = jnp.sum(d_hat, 0, keepdims=True) * (1.0 / MEM)
        mixed = jnp.sum(d_hat * hat, 0, keepdims=True) * (1.0 / MEM)
        d_active = jnp.where(real, inverse * (d_hat - mean - hat * mixed), 0.0)
        d_out = d_active * gelu_slope(pres[t])
        a_col[0] += d_out
        d_out_low = d_out.astype(BF16)
        d_outs.append(d_out_low)
        a_oa[...] += dot(d_out_low, atts[t], 1, 1)
        d_att = dot(o_att_n[...], d_out_low)
        q = queries[t]
        d_q = jnp.zeros((PAD, EB), F32)
        slopes = [[], []]
        for h in range(2):
            rows = slice(PAD + h * HALF, PAD + h * HALF + HALF)
            d_head = d_att[h * HALF : h * HALF + HALF]
            dp = [jnp.sum(d_head * kv[k, rows, at], 0, keepdims=True) for k in range(NBR)]
            mid = functools.reduce(jnp.add, [a * b for a, b in zip(dp, probs[t][h])])
            slopes[h] = [probs[t][h][k] * (dp[k] - mid) * scale for k in range(NBR)]
        for k in range(NBR):
            keys = kv[k, 0:PAD, at]
            factor = jnp.concatenate(
                [jnp.broadcast_to(slopes[h][k], (HALF, EB)) for h in range(2)], 0
            )
            share = jnp.concatenate(
                [jnp.broadcast_to(probs[t][h][k], (HALF, EB)) for h in range(2)], 0
            )
            d_q = d_q + factor * keys
            kv[k, 0:PAD, at] = factor * q
            kv[k, PAD:KV, at] = share * d_att
        d_queries.append(d_q)
        a_q1[...] += d_q.astype(BF16).astype(F32)

    d_out_all = jnp.concatenate(d_outs, 1)
    d_q_all = jnp.concatenate(d_queries, 1).astype(BF16)
    a_oh[...] += dot(d_out_all, roots)
    a_qh[...] += dot(d_q_all, roots)
    d_rows[...] = dot(d_out_all, o_h[...], 0, 0) + dot(d_q_all, q_h[...], 0, 0)
    base = step * total
    each = SECT // STREAMS

    def add_rows(first, ref):
        for u in range(each):
            for s in range(STREAMS):
                at = s * each + u
                to = pl.ds(index[first + at], 1)
                lanes[s][to, :] += ref[at : at + 1, :]

    for k in range(NBR):
        mine, other = (d_two, d_rows) if k % 2 == 0 else (d_rows, d_two)
        d_kv = kv[k].astype(BF16)
        a_kvh[...] += dot(d_kv, picks[k][...])
        a_kve[:, :EDGE] += dot(d_kv, edge_of(k), 1, 1)
        a_kvt[:, :TENC] += dot(d_kv, code_of(k), 1, 1)
        mine[...] = dot(d_kv, kv_h[...], 0, 0)
        add_rows(base + (NBR if k == 0 else k - 1) * SECT, other)
    add_rows(base + (NBR - 1) * SECT, d_rows)

    @pl.when(step == pl.num_programs(0) - 1)
    def _():
        slots = sent.shape[2]
        pieces = slots // LANES

        def finish(j, carry):
            owner = j // pieces
            to = pl.ds(pl.multiple_of((j - owner * pieces) * LANES, LANES), LANES)
            at = pl.ds(pl.multiple_of(j * LANES, LANES), LANES)
            whole = functools.reduce(jnp.add, [ref[at, :] for ref in lanes])
            sent[owner, :, to] = jnp.where(lane_of((LANES, LANES)) < MEM, whole, 0.0).T[:WIRE].astype(BF16)
            return carry

        lax.fori_loop(0, sent.shape[0] * pieces, finish, 0, unroll=4)
        base_row = ATT_BASE

        def turned(block):
            short = -block.shape[0] % LANES
            if short:
                block = jnp.concatenate([block, jnp.zeros((short, block.shape[1]), F32)], 0)
            return block.T

        grads[...] = jnp.zeros_like(grads)
        q = ROW_Q - base_row
        grads[q : q + 100, :] = join_heads(turned(a_qh[...]))[:100]
        ones = jnp.sum(turned(a_q1[...]), 0, keepdims=True)
        grads[q + 100 : q + 200, :] = jnp.broadcast_to(join_heads(ones), (100, LANES))
        for part in range(2):
            rows = slice(PAD * part, PAD * part + PAD)
            start = ROW_KV - base_row + part
            grads[pl.ds(start, MEM, stride=2), :] = join_heads(turned(a_kvh[rows, :]))[:MEM]
            grads[pl.ds(start + 2 * MEM, EDGE, stride=2), :] = join_heads(turned(a_kve[rows, :]))[:EDGE]
            grads[pl.ds(start + 2 * (MEM + EDGE), TENC, stride=2), :] = join_heads(
                turned(a_kvt[rows, :])
            )[:TENC]
        o = ROW_O - base_row
        wide = jnp.concatenate([a_oa[...], jnp.zeros((PAD, LANES - PAD), F32)], 1)
        grads[o : o + 100, :] = turned(join_heads(wide))[:100]
        grads[o + 100 : o + 200, :] = turned(a_oh[...])[:100]
        for start, ref in ((ROW_SRC, a_src), (ROW_DST, a_dst)):
            wide = jnp.concatenate([ref[...], jnp.zeros((PAD, LANES - PAD), F32)], 1)
            grads[start - base_row : start - base_row + 100, :] = wide[:100]
        for i, r in enumerate((ROW_BO, ROW_GAIN, ROW_SHIFT, ROW_BPRED, ROW_OUT)):
            line = jnp.sum(turned(a_col[i]), 0, keepdims=True)
            grads[r - base_row : r - base_row + 1, :] = line
        line = jnp.where(
            lane_of((1, LANES)) == 0, jnp.sum(a_one[2:3, :], 1, keepdims=True), 0.0
        )
        grads[ROW_BOUT - base_row : ROW_BOUT - base_row + 1, :] = line
        losses[...] = jnp.broadcast_to(jnp.sum(a_one[...], 1, keepdims=True), (8, LANES))


def attention(index, got, edges, codes, weight, wts):
    roots = edges.shape[2]
    blocks = roots // SECT

    def section(rows, t):
        return pl.BlockSpec((NBR, rows, EB), lambda b: (0, 0, t * blocks + b))

    slots = got.shape[0] * got.shape[2]
    total = (NBR + 1) * SECT
    return pl.pallas_call(
        attention_kernel,
        grid=(blocks,),
        out_shape=(
            jax.ShapeDtypeStruct(got.shape, BF16),
            jax.ShapeDtypeStruct((ATT_ROWS, LANES), F32),
            jax.ShapeDtypeStruct((8, LANES), F32),
        ),
        in_specs=[SMEM, VMEM]
        + [section(EDGE, t) for t in range(3)]
        + [section(TENC, t) for t in range(3)]
        + [pl.BlockSpec((1, EB), lambda b: (0, b))]
        + [VMEM] * 13,
        out_specs=(VMEM, VMEM, VMEM),
        scratch_shapes=[
            pltpu.VMEM((slots, LANES), F32),
            pltpu.VMEM((NBR, KV, SECT), F32),
            pltpu.VMEM((SECT, LANES), F32),
            pltpu.VMEM((SECT, LANES), F32),
            pltpu.VMEM((KV, LANES), F32),
            pltpu.VMEM((KV, 256), F32),
            pltpu.VMEM((KV, LANES), F32),
            pltpu.VMEM((PAD, LANES), F32),
            pltpu.VMEM((PAD, LANES), F32),
            pltpu.VMEM((PAD, PAD), F32),
            pltpu.VMEM((PAD, LANES), F32),
            pltpu.VMEM((PAD, PAD), F32),
            pltpu.VMEM((PAD, PAD), F32),
            pltpu.VMEM((5, PAD, LANES), F32),
            pltpu.VMEM((8, LANES), F32),
        ]
        + [pltpu.VMEM((slots, LANES), F32) for _ in range(STREAMS)]
        + [pltpu.VMEM((SECT, LANES), BF16) for _ in range(NBR + 1)],
        compiler_params=params_of(),
        cost_estimate=pl.CostEstimate(flops=9_000_000_000, bytes_accessed=20_000_000, transcendentals=1_000_000),
    )(index, got, edges, edges, edges, codes, codes, codes, weight, *wts[4:])


def pack_kernel(gru, bias, att, losses, out, rows):
    rows[0:GRU_ROWS, :] = gru[...]
    rows[GRU_ROWS : ATT_BASE + ATT_ROWS, :] = att[8:, :]
    rows[ATT_BASE:GRU_ROWS, :] += att[0:8, :]
    rows[ROW_BIH : ROW_BIH + 8, :] += bias[...]
    rows[ATT_BASE + ATT_ROWS :, :] = jnp.zeros((rows.shape[0] - ATT_BASE - ATT_ROWS, LANES), F32)
    lane = lane_of((PERIODS, LANES))
    for m in range(25):
        first, shift = divmod(LANES * m, 100)
        value = None
        filled = 0
        source = first
        while filled < LANES:
            amount = shift if filled == 0 else -filled
            block = roll_left(rows[pl.ds(source, PERIODS, stride=32), :], amount)
            value = block if value is None else jnp.where(lane < filled, value, block)
            filled += 100 - (shift if filled == 0 else 0)
            source += 1
        out[pl.ds(m, PERIODS, stride=25), :] = value
    first, at = divmod(USED, LANES)
    tail = out.shape[0] - first
    where = row_of((tail, LANES)) * LANES + lane_of((tail, LANES))
    value = jnp.where(where < at, out[first:, :], 0.0)
    value = jnp.where(where == at, losses[0:1, :], value)
    value = jnp.where(where == at + 1, losses[1:2, :], value)
    out[first:, :] = value


def pack(gru, bias, att, losses):
    return pl.pallas_call(
        pack_kernel,
        out_shape=jax.ShapeDtypeStruct((25 * PERIODS + 7, LANES), F32),
        in_specs=[VMEM] * 4,
        out_specs=VMEM,
        scratch_shapes=[pltpu.VMEM((WROWS + 8, LANES), F32)],
        compiler_params=params_of(16 * 2**20),
        cost_estimate=pl.CostEstimate(flops=2_000_000, bytes_accessed=4_000_000, transcendentals=0),
    )(gru, bias, att, losses)


NODES = 2048


def each_message(starts, sender, body_of):
    first, end = starts[2 * sender], starts[2 * sender + 1]

    def move(i, carry):
        for u in range(8):
            body_of(jnp.minimum(first + i * 8 + u, end - 1))
        return carry

    lax.fori_loop(0, (end - first + 7) // 8, move, 0)


def after_first(count):
    return pl.BlockSpec((count, NODES), lambda i: (0, jnp.maximum(i - 1, 0)))


def edge_kernel(
    starts, rows, events, edges, stamps, own, mailbox, mail_time, mail_new, time_new, stage, far, kept, lines
):
    step = pl.program_id(0)

    @pl.when(step == 0)
    def _():
        kept[1] = jnp.zeros(kept.shape[1:], F32)
        stage[...] = jnp.zeros_like(stage)
        stage[EDGE + 1 : EDGE + 2, :] = jnp.ones((1, EV), F32)

        def sender(s, carry):
            stage[0:EDGE, :] = edges[s].astype(F32)
            stage[EDGE : EDGE + 1, :] = stamps[s].astype(F32)
            for part in range(2):
                far[part] = stage[LANES * part : LANES * part + LANES, :].T

            def one(i):
                place = s * 2 * EV + i
                to = pl.ds(rows[place], 1)
                event = pl.ds(events[place], 1)
                kept[0, to, :] = far[0, event, :]
                kept[1, to, :] = far[1, event, :]

            each_message(starts, s, one)
            return carry

        lax.fori_loop(0, edges.shape[0], sender, 0)

    @pl.when(step > 0)
    def _():
        at = pl.ds(pl.multiple_of((step - 1) * NODES, LANES), NODES)
        last = kept[1, at, :].T
        stamp = EDGE - LANES
        has = last[stamp + 1 : stamp + 2, :] > 0.5
        lines[0:MEM, :] = own[...].astype(F32)
        lines[2 * MEM : 2 * MEM + LANES, :] = kept[0, at, :].T
        lines[2 * MEM + LANES : MAIL, :] = last[0:stamp]
        mail_new[...] = jnp.where(has, lines[0:MAIL, :], mailbox[...].astype(F32)).astype(BF16)
        time_new[...] = jnp.where(has, last[stamp : stamp + 1, :].astype(jnp.int32), mail_time[...])


def deliver_edges(starts, rows, events, edges, stamps, own, mailbox, mail_time):
    nodes = mailbox.shape[1]
    return pl.pallas_call(
        edge_kernel,
        grid=(1 + nodes // NODES,),
        out_shape=(
            jax.ShapeDtypeStruct((MAIL, nodes), BF16),
            jax.ShapeDtypeStruct((1, nodes), jnp.int32),
        ),
        in_specs=[SMEM, SMEM, SMEM, VMEM, VMEM]
        + [after_first(MEM), after_first(MAIL), after_first(1)],
        out_specs=(after_first(MAIL), after_first(1)),
        scratch_shapes=[
            pltpu.VMEM((2 * LANES, EV), F32),
            pltpu.VMEM((2, EV, LANES), F32),
            pltpu.VMEM((2, nodes, LANES), F32),
            pltpu.VMEM((MAIL + 6, NODES), F32),
        ],
        compiler_params=params_of(),
        cost_estimate=pl.CostEstimate(flops=20_000_000, bytes_accessed=16_000_000, transcendentals=0),
    )(starts, rows, events, edges, stamps, own, mailbox, mail_time)


def partner_into_kernel(starts, rows, partner, mailbox, mail_new, near, kept, lines):
    step = pl.program_id(0)

    @pl.when(step == 0)
    def _():
        kept[...] = jnp.zeros_like(kept)
        short = jnp.zeros((LANES - WIRE, LANES), F32)

        def sender(s, carry):
            for i in range(2 * EV // LANES):
                at = slice(i * LANES, i * LANES + LANES)
                near[at, :] = jnp.concatenate([partner[s, :, at].astype(F32), short], 0).T

            def one(i):
                kept[pl.ds(rows[s * 2 * EV + i], 1), :] = near[pl.ds(i, 1), :]

            each_message(starts, s, one)
            return carry

        lax.fori_loop(0, partner.shape[0], sender, 0)

    @pl.when(step > 0)
    def _():
        at = pl.ds(pl.multiple_of((step - 1) * NODES, LANES), NODES)
        turned = kept[at, :].T
        has = turned[MEM : MEM + 1, :] > 0.5
        lines[...] = mailbox[...].astype(F32)
        lines[MEM : 2 * MEM, :] = jnp.where(has, turned[0:MEM], lines[MEM : 2 * MEM, :])
        mail_new[...] = lines[...].astype(BF16)


def deliver_partners(starts, rows, partner, mailbox):
    nodes = mailbox.shape[1]
    upper = 208
    return pl.pallas_call(
        partner_into_kernel,
        grid=(1 + nodes // NODES,),
        out_shape=jax.ShapeDtypeStruct((MAIL, nodes), BF16),
        in_specs=[SMEM, SMEM, VMEM, after_first(upper)],
        out_specs=after_first(upper),
        scratch_shapes=[
            pltpu.VMEM((2 * EV, LANES), F32),
            pltpu.VMEM((nodes, LANES), F32),
            pltpu.VMEM((upper, NODES), F32),
        ],
        input_output_aliases={3: 0},
        compiler_params=params_of(),
        cost_estimate=pl.CostEstimate(flops=10_000_000, bytes_accessed=8_000_000, transcendentals=0),
    )(starts, rows, partner, mailbox)


def flip(x, axis, mask):
    return lax.ppermute(x, axis, [(i, i ^ mask) for i in range(lax.axis_size(axis))])


def rounds():
    table = []
    low, count = 2, lax.axis_size("node")
    while low < count:
        size = min(4, count // low)
        table.append(("node", low, size))
        low *= size
    table.append(("batch", 1, lax.axis_size("batch")))
    table.append(("node", 1, 2))
    return table


def place_in(axis, low, size):
    return (lax.axis_index(axis) // low) % size


def tree_sum(parts):
    while len(parts) > 1:
        parts = [a + b for a, b in zip(parts[::2], parts[1::2])]
    return parts[0]


def gather_first(x, lines, between):
    grown = [[x, []], [lines, []]]

    def grow(entry, key, here, parts):
        x, axes = entry
        at = sum(1 for k in axes if k < key)
        axes.append(key)
        axes.sort()
        out = jnp.zeros(x.shape[:at] + (len(parts),) + x.shape[at:], x.dtype)
        for m, part in enumerate(parts):
            to = jnp.bitwise_xor(here, m)
            out = lax.dynamic_update_slice_in_dim(out, jnp.expand_dims(part, at), to, at)
        entry[0] = out

    for number, (axis, low, size) in enumerate(rounds()):
        here = place_in(axis, low, size)
        key = (axis == "node", -low)
        x, lines = grown[0][0], grown[1][0]
        if number == 0:
            both = jnp.concatenate([x, lines], 0)
            got = [flip(both, axis, low * m) for m in range(1, size)]
            parts = [x] + [g[: x.shape[0]] for g in got]
            others = [lines] + [g[x.shape[0] :] for g in got]
        else:
            parts = [x] + [flip(x, axis, low * m) for m in range(1, size)]
            others = [lines] + [flip(lines, axis, low * m) for m in range(1, size)] if axis == "node" else None
        parts = between(number, x, parts)
        grow(grown[0], key, here, parts)
        if others is not None:
            grow(grown[1], key, here, others)
    return [g[0] for g in grown]


def scatter_sum(x, between):
    table = rounds()
    dims = sorted(((axis == "node", -low), size) for axis, low, size in table)
    keys = [k for k, _ in dims]
    x = x.reshape(tuple(n for _, n in dims) + (-1, LANES))
    for number, (axis, low, size) in enumerate(table[::-1]):
        at = keys.index((axis == "node", -low))
        here = place_in(axis, low, size)

        def part(m, x=x, at=at, here=here):
            return lax.dynamic_slice_in_dim(x, jnp.bitwise_xor(here, m), 1, at)

        away = [flip(part(m), axis, low * m) for m in range(1, size)]
        away = between(number, x, away)
        x = tree_sum([part(0)] + list(away))
    return x.reshape(-1, LANES)


def sum_all(x):
    for axis, low, size in rounds()[::-1]:
        x = tree_sum([x] + [flip(x, axis, low * m) for m in range(1, size)])
    return x


def after(x, *others):
    return lax.optimization_barrier((x,) + others)[0]


def swap(x):
    return lax.all_to_all(x, "node", split_axis=0, concat_axis=0, tiled=True)


def to_slot(live, counts, slots):
    upper = jnp.cumsum(counts)
    shape = (-1,) + (1,) * live.ndim
    passed = live[None] >= upper.reshape(shape)
    return live + jnp.sum(jnp.where(passed, (slots - counts).reshape(shape), 0), 0)


def body(
    params,
    moment1,
    moment2,
    memory,
    mailbox,
    mail_time,
    update_time,
    node_feat,
    req_rows,
    req_count,
    root_live,
    nbr_live,
    nbr_dt,
    nbr_edge,
    ev_edge,
    ev_time,
    neg_count,
):
    shards = lax.axis_size("node")
    me = lax.axis_index("node")
    slots = req_rows.shape[3]
    wanted = req_rows[0, 0]
    counts = req_count[0, 0]
    rows = memory.shape[1]
    mem_cols = jnp.transpose(memory.reshape(rows // LANES, LANES, MEM), (2, 0, 1))
    mail_cols = mailbox[0].T
    feat_cols = node_feat.T
    edge_cols = jnp.transpose(nbr_edge[0, 0], (1, 2, 0))

    dead = jnp.arange(slots, dtype=jnp.int32)[None, :] >= counts[:, None]
    wanted_or_dead = wanted + rows * dead.astype(jnp.int32)

    near_slot = to_slot(nbr_live[0, 0].T, counts, slots)
    root_slot = to_slot(root_live[0, 0], counts, slots)
    blocks = EV // EB
    near_index = jnp.transpose(near_slot.reshape(NBR, 3, blocks, EB), (2, 0, 1, 3))
    root_index = jnp.transpose(root_slot.reshape(3, blocks, EB), (1, 0, 2))
    index = jnp.concatenate(
        [near_index.reshape(blocks, -1), root_index.reshape(blocks, -1)], 1
    ).reshape(-1)

    edge_sent = ev_edge[0, 0].T
    early = {}

    last = len(rounds()) - 1

    def between(number, x, parts):
        if number == last - 1:
            edges = after(edge_sent, x)
            early["edges"] = swap(jnp.broadcast_to(edges, (shards,) + edges.shape))
            early["codes"] = time_codes(after(mail_time - update_time, x), PAD)
            *parts, early["codes"] = lax.optimization_barrier((*parts, early["codes"]))
        return parts

    digits = jnp.stack([wanted_or_dead // 128, wanted_or_dead % 128]).astype(BF16)
    flat, asked = gather_first(
        params.astype(BF16).reshape(-1, LANES), digits.reshape(-1, LANES), between
    )
    flat = flat.reshape(-1, LANES)
    asked = asked.reshape(shards, 2, shards, slots)
    asked = lax.dynamic_slice_in_dim(asked, me, 1, 2).astype(F32).astype(jnp.int32)
    asked = (asked[:, 0] * 128 + asked[:, 1]).reshape(-1)
    alive = asked < rows
    asked = asked % rows
    codes_m = early["codes"][0]
    wts, h_sent, low, s_cols = gru_forward(asked, flat, mail_cols, codes_m, mem_cols, feat_cols, shards, slots)
    h_got = swap(h_sent)

    codes_n = time_codes(nbr_dt[0, 0].T)
    edges_all = early["edges"]
    ends = root_slot[:2].reshape(-1)
    ordered = lax.sort(ends * (2 * EV) + jnp.arange(2 * EV, dtype=jnp.int32))
    end_row, partner_slot, event = bookkeeping(ordered, ends, wanted.reshape(-1))
    first = jnp.sum(
        (ordered[None, :] < (jnp.arange(LANES, dtype=jnp.int32) * (slots * 2 * EV))[:, None]).astype(jnp.int32),
        1,
    )
    notes = jnp.concatenate([end_row, event, ev_time[0, 0], first])
    digits = jnp.concatenate([notes // 128, notes % 128]).astype(BF16)
    lines = -(-digits.shape[0] // (8 * slots)) * 8
    digits = jnp.pad(digits, (0, lines * slots - digits.shape[0])).reshape(lines, slots)
    s_sent = send_rows(s_cols, asked, digits, shards, slots)
    h_got, s_sent, codes_n, edges_all, partner_slot, index = lax.optimization_barrier(
        (h_got, s_sent, codes_n, edges_all, partner_slot, index)
    )
    s_got = swap(s_sent)
    d_sent, att_grads, losses = attention(index, h_got, edge_cols, codes_n, neg_count[0], wts)
    d_sent, s_got, low = lax.optimization_barrier((d_sent, s_got, low))
    d_got = swap(d_sent)

    upper = (jnp.arange(rows // LANES, dtype=jnp.int32)[:, None] == (asked // LANES)[None, :]) & alive[None, :]
    lower = (asked % LANES)[:, None] == jnp.arange(LANES, dtype=jnp.int32)[None, :]
    live = dot(upper.astype(BF16), lower.astype(BF16)).reshape(1, rows)
    factors, mem_new, upd_new = gru_factors(
        mail_cols, codes_m, low, mem_cols, live, mail_time, update_time, wts
    )
    partner = partner_rows(s_got, partner_slot, shards)
    digits = s_got[:, WIRE:, :].reshape(shards, -1)[:, : 2 * notes.shape[0]].astype(F32).astype(jnp.int32)
    notes = digits[:, : notes.shape[0]] * 128 + digits[:, notes.shape[0] :]
    stamps = notes[:, 4 * EV : 5 * EV].reshape(shards, 1, EV)
    events_of = notes[:, 2 * EV : 4 * EV].reshape(-1)
    rows_of = notes[:, : 2 * EV].reshape(-1)
    starts = lax.dynamic_slice_in_dim(notes[:, 5 * EV :], me, 2, 1).reshape(-1)
    mail_new, stamp_new = deliver_edges(
        starts, rows_of, events_of, edges_all, stamps, s_cols, mail_cols, mail_time
    )
    d_got, factors, partner, mail_new, starts, rows_of = lax.optimization_barrier(
        (d_got, factors, partner, mail_new, starts, rows_of)
    )
    partner_got = swap(partner)
    gru_grads, bias_grads, mem_grad = gru_backward(
        asked, d_got, factors, mail_cols, codes_m, low, feat_cols, wts
    )
    packed = pack(gru_grads, bias_grads, att_grads, losses)[:FLAT_ROWS]
    late = {}

    def during(number, x, parts):
        if number == 1:
            mail = deliver_partners(starts, rows_of, after(partner_got, x), mail_new)
            *parts, late["mail"] = lax.optimization_barrier((*parts, mail))
        return parts

    shard = scatter_sum(packed, during)
    mail_new = late["mail"]

    number = lax.axis_index("batch") * shards + me
    size = shard.shape[0] * LANES
    place = number * size + jnp.arange(size, dtype=jnp.int32).reshape(-1, LANES)
    grad = jnp.where(place < USED, shard, 0.0)
    lines = [
        jnp.sum(grad * grad, 0, keepdims=True),
        jnp.sum(jnp.where(place == USED, shard, 0.0), 0, keepdims=True),
        jnp.sum(jnp.where(place == USED + 1, shard, 0.0), 0, keepdims=True),
        jnp.zeros((5, LANES), F32),
    ]
    values = jnp.sum(sum_all(jnp.concatenate(lines, 0)), 1)
    grad_norm = jnp.sqrt(values[0])
    clipped = grad.reshape(-1) * jnp.minimum(1.0, clip_limit / (grad_norm + 1e-06))
    moment1_new = beta_first * moment1 + (1.0 - beta_first) * clipped
    moment2_new = beta_second * moment2 + (1.0 - beta_second) * clipped * clipped
    ratio = (
        moment1_new
        / (1.0 - beta_first**STEP)
        / (jnp.sqrt(moment2_new / (1.0 - beta_second**STEP)) + adam_floor)
    )
    params_new = params - learn_rate * (ratio + decay_rate * params)
    return (
        values[1],
        values[2],
        grad_norm,
        params_new,
        moment1_new,
        moment2_new,
        params_new.astype(BF16),
        jnp.transpose(mem_new, (1, 2, 0)).reshape(memory.shape),
        mail_new.T[None],
        stamp_new,
        upd_new,
        jnp.transpose(mem_grad, (1, 2, 0)).reshape(memory.shape),
    )


def solution(mesh):
    both, split = P(("batch", "node")), P("batch", "node")
    in_specs = (both, both, both, split, split, split, split, P("node")) + (split,) * 9
    out_specs = (P(), P(), P()) + (both,) * 4 + (split,) * 5
    return jax.shard_map(body, mesh=mesh, in_specs=in_specs, out_specs=out_specs, check_vma=False)
```

```python
import functools
import math

import jax
import jax.numpy as jnp
import numpy as np
from jax import lax
from jax.experimental import pallas as pl
from jax.experimental.pallas import tpu as pltpu
from jax.sharding import PartitionSpec as P

MEM = 100
TENC = 100
EDGE = 186
NFEAT = 413
NBR = 10
STEP = 5
EV = 512
MAIL = 386
FLAT = 360448

clip_limit = 1.0
learn_rate = 0.02
beta_first = 0.5
beta_second = 0.6
adam_floor = 1e-08
decay_rate = 0.01

F32 = jnp.float32
BF16 = jnp.bfloat16
LANES = 128
PAD = 112
HALF = 56
WIRE = 104
GATES = 3 * PAD
KV = 4 * HALF
EB = 128
SECT = 3 * EB
STREAMS = 8
VMEM_LIMIT = 63_000_000

ROW_HH = 1458
ROW_NF = 1758
ROW_Q = 2171
ROW_KV = 2371
ROW_O = 3143
ROW_SRC = 3343
ROW_DST = 3443
ROW_OUT = 3543
ROW_BIH = 3544
ROW_BHH = 3547
ROW_BO = 3550
ROW_GAIN = 3551
ROW_SHIFT = 3552
ROW_BPRED = 3553
ROW_BOUT = 3554
USED = 355401
FLAT_ROWS = FLAT // LANES
PERIODS = 113
WROWS = 32 * PERIODS
GRU_ROWS = 2176
ATT_BASE = 2168
ATT_ROWS = 1448

FREQS = np.float32(10.0 ** (-9.0 * np.arange(TENC) / (TENC - 1)))

VMEM = pl.BlockSpec(memory_space=pltpu.VMEM)
SMEM = pl.BlockSpec(memory_space=pltpu.SMEM)


def params_of(limit=VMEM_LIMIT):
    return pltpu.CompilerParams(vmem_limit_bytes=limit)


def dot(left, right, left_dim=1, right_dim=0):
    return lax.dot_general(
        left, right, (((left_dim,), (right_dim,)), ((), ())), preferred_element_type=F32
    )


def fit_cosine():
    u = np.cos(np.pi * (np.arange(4000) + 0.5) / 4000) * 0.5 + 0.5
    u = u * (np.pi**2 * 1.002)
    fit = np.polynomial.chebyshev.Chebyshev.fit(u, np.cos(np.sqrt(u)), 7, domain=[0, np.pi**2 * 1.002])
    return [float(np.float32(c)) for c in fit.convert(kind=np.polynomial.Polynomial).coef]


COSINE = fit_cosine()


def cosine(x):
    turns = jnp.floor(x * np.float32(0.5 / np.pi) + 0.5)
    x = x - turns * np.float32(6.28125)
    x = x - turns * np.float32(2 * np.pi - 6.28125)
    u = x * x
    total = jnp.full_like(u, COSINE[-1])
    for c in COSINE[-2::-1]:
        total = total * u + np.float32(c)
    return total


def sigmoid(x):
    return 0.5 * jnp.tanh(0.5 * x) + 0.5


GELU_C = math.sqrt(2.0 / math.pi)


def gelu(x):
    t = jnp.tanh(GELU_C * (x + 0.044715 * (x * x * x)))
    return 0.5 * x * (1.0 + t)


def gelu_slope(x):
    x2 = x * x
    t = jnp.tanh(GELU_C * (x + 0.044715 * (x2 * x)))
    return 0.5 * (1.0 + t) + 0.5 * x * (1.0 - t * t) * (GELU_C * (1.0 + 3 * 0.044715 * x2))


def lane_of(shape):
    return lax.broadcasted_iota(jnp.int32, shape, len(shape) - 1)


def row_of(shape):
    return lax.broadcasted_iota(jnp.int32, shape, len(shape) - 2)


def roll_left(x, amount):
    amount = amount % LANES
    return x if amount == 0 else pltpu.roll(x, LANES - amount, 1)


def spread_heads(x):
    lane = lane_of(x.shape)
    moved = roll_left(x, -6)
    return jnp.where(lane < 50, x, jnp.where((lane >= 56) & (lane < 106), moved, 0.0))


def join_heads(x):
    lane = lane_of(x.shape)
    return jnp.where(lane < 50, x, jnp.where(lane < 100, roll_left(x, 6), 0.0))


def codes_kernel(delta, freq, out):
    freqs = freq[...]
    extra = out.shape[1] - TENC
    if extra:
        tail = (row_of((extra, LANES)) == 0).astype(F32)
    for k in range(out.shape[0]):

        def one(i, carry, k=k):
            at = pl.ds(pl.multiple_of(i * LANES, LANES), LANES)
            value = cosine(delta[k : k + 1, at].astype(F32) * freqs)
            if extra:
                value = jnp.concatenate([value, tail], 0)
            out[k, :, at] = value.astype(BF16)
            return carry

        lax.fori_loop(0, delta.shape[1] // LANES, one, 0)


def time_codes(delta, lines=TENC):
    freq = jnp.asarray(np.tile(FREQS[:, None], (1, LANES)))
    rows, count = delta.shape
    return pl.pallas_call(
        codes_kernel,
        out_shape=jax.ShapeDtypeStruct((rows, lines, count), BF16),
        in_specs=[VMEM] * 2,
        out_specs=VMEM,
        compiler_params=params_of(16 * 2**20),
        cost_estimate=pl.CostEstimate(
            flops=rows * count * 3000, bytes_accessed=rows * count * 200, transcendentals=0
        ),
    )(delta, freq)


def unpack_weights(
    flat,
    w_mail,
    w_two,
    w_hid,
    kv_e,
    att,
    cols,
    w_feat,
    wide,
    rows,
):
    wide[0:FLAT_ROWS, :] = flat[...].astype(F32)
    wide[FLAT_ROWS:, :] = jnp.zeros((wide.shape[0] - FLAT_ROWS, LANES), F32)
    lane = lane_of((PERIODS, LANES))
    for j in range(32):
        first, shift = divmod(100 * j, LANES)
        out = roll_left(wide[pl.ds(first, PERIODS, stride=25), :], shift)
        if shift + 100 > LANES:
            after = roll_left(wide[pl.ds(first + 1, PERIODS, stride=25), :], shift)
            out = jnp.where(lane < LANES - shift, out, after)
        rows[pl.ds(j, PERIODS, stride=32), :] = jnp.where(lane < 100, out, 0.0)

    def turned(start, count, stride=1):
        size = -(-count // LANES) * LANES
        if stride == 1:
            block = rows[start : start + size, :]
        else:
            block = rows[pl.ds(start, size, stride=stride), :]
        return jnp.where(row_of((size, LANES)) < count, block, 0.0).T

    def column(r):
        return jnp.broadcast_to(rows[r : r + 1, :], (LANES, LANES)).T[:PAD, :]

    at_bias = lane_of((PAD, LANES)) == MEM
    for g in range(3):
        to = slice(PAD * g, PAD * g + PAD)
        w_mail[to, :] = turned(g, MAIL, 3)[:PAD, :MAIL].astype(BF16)
        time = jnp.where(at_bias, column(ROW_BIH + g), turned(3 * MAIL + g, TENC, 3)[:PAD])
        hid = jnp.where(at_bias, column(ROW_BHH + g), turned(ROW_HH + g, MEM, 3)[:PAD])
        time, hid = time[:, :PAD].astype(BF16), hid[:, :PAD].astype(BF16)
        none = jnp.zeros((PAD, PAD), BF16)
        if g < 2:
            w_two[to, :] = jnp.concatenate([time, hid], 1)
            w_hid[to, :] = hid
        else:
            w_two[to, :] = jnp.concatenate([time, none], 1)
            w_hid[to, :] = none
            last = slice(PAD * 3, PAD * 4)
            w_two[last, :] = jnp.concatenate([none, hid], 1)
            w_hid[last, :] = hid
    w_feat[...] = turned(ROW_NF, NFEAT)[:PAD, :NFEAT].astype(BF16)
    for part in range(2):
        to = slice(PAD * part, PAD * part + PAD)

        def heads(start, count, part=part):
            size = -(-count // LANES) * LANES
            block = spread_heads(rows[pl.ds(ROW_KV + 2 * start + part, size, stride=2), :])
            return jnp.where(row_of((size, LANES)) < count, block, 0.0).T[:PAD]

        att[to, :] = heads(0, MEM).astype(BF16)
        kv_e[to, :] = heads(MEM, EDGE)[:, :EDGE].astype(BF16)
        att[KV + PAD * part : KV + PAD * part + PAD, :] = heads(MEM + EDGE, TENC).astype(BF16)
    q_rows = spread_heads(rows[ROW_Q : ROW_Q + LANES, :])
    keep = row_of((LANES, LANES)) < 100
    q_two = spread_heads(rows[ROW_Q + 100 : ROW_Q + 100 + LANES, :])
    q_sum = jnp.sum(jnp.where(keep, q_two, 0.0), 0, keepdims=True)
    cols[6, :, :] = jnp.broadcast_to(q_sum, (LANES, LANES)).T[:PAD]
    o_att = spread_heads(turned(ROW_O, 100))
    src, dst = turned(ROW_SRC, 100), turned(ROW_DST, 100)
    blocks = (
        jnp.where(keep, q_rows, 0.0).T,
        o_att,
        o_att.T,
        turned(ROW_O + 100, 100),
        src,
        src.T,
        dst,
        dst.T,
    )
    for i, block in enumerate(blocks):
        att[2 * KV + PAD * i : 2 * KV + PAD * i + PAD, :] = block[:PAD].astype(BF16)
    for i, r in enumerate((ROW_BO, ROW_GAIN, ROW_SHIFT, ROW_BPRED, ROW_OUT)):
        cols[i, :, :] = column(r)
    first = rows[ROW_BOUT : ROW_BOUT + 1, :]
    value = jnp.sum(jnp.where(lane_of((1, LANES)) == 0, first, 0.0), 1, keepdims=True)
    cols[5, :, :] = jnp.broadcast_to(value, (PAD, LANES))


WEIGHTS = [
    ((GATES, MAIL), BF16),
    ((4 * PAD, 2 * PAD), BF16),
    ((4 * PAD, PAD), BF16),
    ((KV, EDGE), BF16),
    ((2 * KV + 8 * PAD, LANES), BF16),
    ((7, PAD, LANES), F32),
]


def gather_loop(index, table, out, count, base=0, to=0):
    group = 32

    def step(i, carry):
        for g in range(group // 16):
            at = pl.multiple_of(i * group + g * 16, 16)
            picked = [table[pl.ds(index[base + at + u], 1), :] for u in range(16)]
            out[pl.ds(to + at, 16), :] = jnp.concatenate(picked, 0).astype(out.dtype)
        return carry

    lax.fori_loop(0, count // group, step, 0)


def gather_turned(index, table, out, finished=None):
    slots = out.shape[2]
    pieces = slots // LANES

    def one(owner, carry):
        def step(j, inner):
            at = pl.ds(pl.multiple_of(j * LANES, LANES), LANES)
            base = owner * slots + j * LANES
            groups = []
            for g in range(LANES // 8):
                picked = [table[pl.ds(index[base + g * 8 + u], 1), :] for u in range(8)]
                groups.append(jnp.concatenate(picked, 0))
            out[owner, 0:WIRE, at] = jnp.concatenate(groups, 0).T[:WIRE].astype(BF16)
            return inner

        lax.fori_loop(0, pieces, step, 0, unroll=min(2, pieces))
        if finished is not None:
            finished(owner)
        return carry

    lax.fori_loop(0, out.shape[0], one, 0)


def turn_into(got, table):
    slots = got.shape[2]
    pieces = slots // LANES
    short = jnp.zeros((LANES - WIRE, LANES), F32)

    def step(j, carry):
        owner = j // pieces
        at = pl.ds(pl.multiple_of((j - owner * pieces) * LANES, LANES), LANES)
        block = jnp.concatenate([got[owner, 0:WIRE, at].astype(F32), short], 0)
        table[pl.ds(pl.multiple_of(j * LANES, LANES), LANES), :] = block.T
        return carry

    lax.fori_loop(0, got.shape[0] * pieces, step, 0, unroll=8)


def to_rows(block):
    full = jnp.concatenate([block, jnp.zeros((LANES - PAD, LANES), F32)], 0)
    return full.T


def mem_piece(mem, i):
    return mem.reshape(MEM * 8, LANES)[pl.ds(i, MEM, stride=8), :]


def gate_products(mail, two, w_mail, w_two):
    both = dot(w_two[...], two)
    first = both[:GATES] + dot(w_mail[...], mail)
    return first[:PAD], first[PAD : 2 * PAD], first[2 * PAD :], both[GATES:]


def gates_at(at, sums, low, s=None):
    gr, gz, gn, hn = (x[:, at] for x in sums)
    r = sigmoid(gr)
    z = sigmoid(gz)
    n = jnp.tanh(gn + r * hn)
    if s is None:
        s = low[:, at].astype(F32)
    return r, z, n, hn, s, (1.0 - z) * n + z * s


def gru_kernel(index, flat, mail_in, phi_in, mem_in, feat_in, *refs):
    wts, rest = refs[: len(WEIGHTS)], refs[len(WEIGHTS) :]
    sent_out, low_out, s_out = rest[:3]
    w_feat, wide, rows, mail, two, mem, feat, s_cols, table, sent, in_sems, out_sems, sent_sems = rest[3:]
    w_mail, w_two = wts[:2]
    nodes = mail.shape[1]
    half = nodes // 2
    copies = []
    for part in range(2):
        cols = slice(part * half, part * half + half)
        lines = slice(part * half // LANES, (part + 1) * half // LANES)
        pairs = [(r.at[:, cols], v.at[:, cols]) for r, v in ((mail_in, mail), (feat_in, feat))]
        pairs.append((phi_in.at[:, cols], two.at[0:PAD, cols]))
        pairs.append((mem_in.at[:, lines, :], mem.at[:, lines, :]))
        copies.append([pltpu.make_async_copy(r, v, in_sems.at[part, i]) for i, (r, v) in enumerate(pairs)])
        for copy in copies[-1]:
            copy.start()
    unpack_weights(flat, *wts, w_feat, wide, rows)
    sub = 256
    real = row_of((PAD, sub)) < MEM
    ones = (row_of((PAD, sub)) == MEM).astype(F32)
    short = jnp.zeros((PAD - MEM, sub), F32)
    for part in range(2):
        for copy in copies[part]:
            copy.wait()

        def piece(j, carry):
            start = pl.multiple_of(j * sub, sub)
            at = pl.ds(start, sub)
            lows = []
            for i in range(sub // LANES):
                line = j * (sub // LANES) + i
                lows.append(mem.reshape(MEM * (nodes // LANES), LANES)[pl.ds(line, MEM, stride=nodes // LANES), :])
            full = jnp.concatenate([jnp.concatenate(lows, 1), short], 0)
            low_now = full.astype(BF16)
            two[PAD : 2 * PAD, at] = jnp.where(real, full, ones).astype(BF16)
            sums = gate_products(mail[:, at], two[:, at], w_mail, w_two)
            nf = dot(w_feat[...], feat[:, at])
            for i in range(sub // LANES):
                here = slice(i * LANES, i * LANES + LANES)
                _, _, _, _, _, renewed = gates_at(here, sums, low_now)
                hidden = (renewed + nf[:, here]).astype(BF16).astype(F32)
                to = pl.ds(pl.multiple_of(start + i * LANES, LANES), LANES)
                table[to, :] = to_rows(hidden)
                s_cols[:, to] = renewed[:MEM].astype(BF16)
            return carry

        lax.fori_loop(part * half // sub, (part + 1) * half // sub, piece, 0, unroll=4)
    outs = [
        pltpu.make_async_copy(two.at[PAD : 2 * PAD, :], low_out, out_sems.at[0]),
        pltpu.make_async_copy(s_cols, s_out, out_sems.at[1]),
    ]
    for copy in outs:
        copy.start()

    def done(owner):
        return pltpu.make_async_copy(sent.at[owner], sent_out.at[owner], sent_sems.at[owner])

    gather_turned(index, table, sent, lambda owner: done(owner).start())

    def settle(owner, carry):
        done(owner).wait()
        return carry

    lax.fori_loop(0, sent.shape[0], settle, 0)
    for copy in outs:
        copy.wait()


BLOCK = 1024


def cols_spec(rows):
    return pl.BlockSpec((rows, BLOCK), lambda i: (0, i))


def mem_spec():
    return pl.BlockSpec((MEM, BLOCK // LANES, LANES), lambda i: (0, i, 0))


HBM = pl.BlockSpec(memory_space=pl.ANY)


def gru_forward(index, flat, mail, phi, mem, feat, shards, slots):
    rows = mail.shape[1]
    shapes = [jax.ShapeDtypeStruct(s, d) for s, d in WEIGHTS]
    shapes += [
        jax.ShapeDtypeStruct((shards, WIRE, slots), BF16),
        jax.ShapeDtypeStruct((PAD, rows), BF16),
        jax.ShapeDtypeStruct((MEM, rows), BF16),
    ]
    got = pl.pallas_call(
        gru_kernel,
        out_shape=shapes,
        in_specs=[SMEM, VMEM] + [HBM] * 4,
        out_specs=[VMEM] * len(WEIGHTS) + [HBM] * 3,
        scratch_shapes=[
            pltpu.VMEM((PAD, NFEAT), BF16),
            pltpu.VMEM((FLAT_ROWS + 16, LANES), F32),
            pltpu.VMEM((WROWS + 512, LANES), F32),
            pltpu.VMEM((MAIL, rows), BF16),
            pltpu.VMEM((2 * PAD, rows), BF16),
            pltpu.VMEM((MEM, rows // LANES, LANES), F32),
            pltpu.VMEM((NFEAT, rows), BF16),
            pltpu.VMEM((MEM, rows), BF16),
            pltpu.VMEM((rows, LANES), F32),
            pltpu.VMEM((shards, WIRE, slots), BF16),
            pltpu.SemaphoreType.DMA((2, 4)),
            pltpu.SemaphoreType.DMA((2,)),
            pltpu.SemaphoreType.DMA((shards,)),
        ],
        compiler_params=params_of(),
        cost_estimate=pl.CostEstimate(flops=4_000_000_000, bytes_accessed=24_000_000, transcendentals=3_000_000),
    )(index, flat, mail, phi, mem, feat)
    return got[: len(WEIGHTS)], *got[len(WEIGHTS) :]


def send_kernel(index, s_cols, notes, out, table):
    for owner in range(out.shape[0]):
        out[owner, WIRE:, :] = notes[...]
    short = jnp.zeros((LANES - MEM, LANES), F32)

    def step(j, carry):
        at = pl.ds(pl.multiple_of(j * LANES, LANES), LANES)
        table[at, :] = jnp.concatenate([s_cols[:, at].astype(F32), short], 0).T
        return carry

    lax.fori_loop(0, table.shape[0] // LANES, step, 0, unroll=8)
    gather_turned(index, table, out)


def send_rows(s_cols, index, notes, shards, slots):
    return pl.pallas_call(
        send_kernel,
        out_shape=jax.ShapeDtypeStruct((shards, WIRE + notes.shape[0], slots), BF16),
        in_specs=[SMEM, VMEM, VMEM],
        out_specs=VMEM,
        scratch_shapes=[pltpu.VMEM((s_cols.shape[1], LANES), F32)],
        compiler_params=params_of(24 * 2**20),
        cost_estimate=pl.CostEstimate(flops=8_000_000, bytes_accessed=6_000_000, transcendentals=0),
    )(index, s_cols, notes)


def partner_kernel(index, got, out, table, rows):
    turn_into(got, table)
    gather_loop(index, table, rows, index.shape[0])
    flag = lane_of((LANES, LANES)) == MEM
    for i in range(index.shape[0] // LANES):
        at = slice(i * LANES, i * LANES + LANES)
        block = jnp.where(flag, 1.0, rows[at, :]).T[:WIRE].astype(BF16)

        def copy(owner, carry, at=at, block=block):
            out[owner, :, at] = block
            return carry

        lax.fori_loop(0, out.shape[0], copy, 0)


def partner_rows(got, index, shards):
    return pl.pallas_call(
        partner_kernel,
        out_shape=jax.ShapeDtypeStruct((shards, WIRE, index.shape[0]), BF16),
        in_specs=[SMEM, VMEM],
        out_specs=VMEM,
        scratch_shapes=[
            pltpu.VMEM((got.shape[0] * got.shape[2], LANES), F32),
            pltpu.VMEM((index.shape[0], LANES), F32),
        ],
        compiler_params=params_of(44 * 2**20),
        cost_estimate=pl.CostEstimate(flops=2_000_000, bytes_accessed=2_000_000, transcendentals=0),
    )(index, got)


def book_kernel(ordered, ends, wanted, row, partner, event):
    count = ordered.shape[0]

    def step(i, carry):
        for u in range(8):
            at = i * 8 + u
            key = ordered[at]
            end = jnp.bitwise_and(key, count - 1)
            row[at] = wanted[lax.shift_right_logical(key, count.bit_length() - 1)]
            partner[at] = ends[jnp.bitwise_xor(end, count // 2)]
            event[at] = jnp.bitwise_and(end, count // 2 - 1)
        return carry

    lax.fori_loop(0, count // 8, step, 0)


def bookkeeping(ordered, ends, wanted):
    shape = jax.ShapeDtypeStruct(ordered.shape, jnp.int32)
    return pl.pallas_call(
        book_kernel,
        out_shape=(shape, shape, shape),
        in_specs=[SMEM] * 3,
        out_specs=(SMEM,) * 3,
        compiler_params=params_of(),
        cost_estimate=pl.CostEstimate(flops=4_000_000, bytes_accessed=60_000, transcendentals=0),
    )(ordered, ends, wanted)


def factor_kernel(
    mail, phi, low, mem, live_in, mail_time, update_time, w_mail, w_two, factors, mem_new, time_new
):
    sub = 256
    for j in range(BLOCK // sub):
        part = slice(j * sub, j * sub + sub)
        sums = gate_products(mail[:, part], jnp.concatenate([phi[:, part], low[:, part]], 0), w_mail, w_two)
        for i in range(sub // LANES):
            there = slice(i * LANES, i * LANES + LANES)
            at = slice(j * sub + i * LANES, j * sub + i * LANES + LANES)
            s_low = jnp.where(row_of((PAD, LANES)) < MEM, low[:, at].astype(F32), 0.0)
            r, z, n, hn, s, renewed = gates_at(there, sums, None, s_low)
            live = live_in[:, at] > 0.5
            an = (1.0 - z) * (1.0 - n * n)
            factors[0, :, at] = (an * hn * (r * (1.0 - r))).astype(BF16)
            factors[1, :, at] = ((s - n) * (z * (1.0 - z))).astype(BF16)
            factors[2, :, at] = an.astype(BF16)
            factors[3, :, at] = r.astype(BF16)
            factors[4, :, at] = z.astype(BF16)
            line = (j * sub) // LANES + i
            value = jnp.where(live, renewed[:MEM], mem_piece(mem, line))
            mem_new.reshape(MEM * 8, LANES)[pl.ds(line, MEM, stride=8), :] = value
            time_new[:, at] = jnp.where(live, mail_time[:, at], update_time[:, at])


def gru_factors(mail, phi, low, mem, live, mail_time, update_time, wts):
    rows = mail.shape[1]
    return pl.pallas_call(
        factor_kernel,
        grid=(rows // BLOCK,),
        out_shape=(
            jax.ShapeDtypeStruct((5, PAD, rows), BF16),
            jax.ShapeDtypeStruct((MEM, rows // LANES, LANES), F32),
            jax.ShapeDtypeStruct((1, rows), jnp.int32),
        ),
        in_specs=[cols_spec(MAIL), cols_spec(PAD), cols_spec(PAD), mem_spec()]
        + [cols_spec(1)] * 3
        + [VMEM] * 2,
        out_specs=(
            pl.BlockSpec((5, PAD, BLOCK), lambda i: (0, 0, i)),
            mem_spec(),
            cols_spec(1),
        ),
        compiler_params=params_of(),
        cost_estimate=pl.CostEstimate(flops=3_000_000_000, bytes_accessed=34_000_000, transcendentals=3_000_000),
    )(mail, phi, low, mem, live, mail_time, update_time, wts[0], wts[1])


def gru_back_kernel(
    index,
    got,
    w_hid,
    factors_in,
    mail_in,
    phi_in,
    low_in,
    feat_in,
    grads,
    biases,
    grad_out,
    factors,
    mail,
    two,
    feat,
    mem_grad,
    wide,
    placed,
    d_one,
    d_two,
    a_mail,
    a_two,
    a_feat,
    in_sems,
    out_sems,
):
    pairs = ((factors_in, factors), (mail_in, mail), (phi_in, two.at[0:PAD, :]), (low_in, two.at[PAD : 2 * PAD, :]), (feat_in, feat))
    copies = [pltpu.make_async_copy(r, v, in_sems.at[i]) for i, (r, v) in enumerate(pairs)]
    for copy in copies:
        copy.start()
    turn_into(got, wide)
    count = wide.shape[0]
    if count != placed.shape[0]:
        placed[...] = jnp.zeros_like(placed)
    group = 32

    def move(i, carry):
        for u in range(group):
            at = i * group + u
            placed[pl.ds(index[at], 1), :] = wide[pl.ds(at, 1), :]
        return carry

    lax.fori_loop(0, count // group, move, 0)
    for ref in (a_mail, a_two, a_feat):
        ref[...] = jnp.zeros_like(ref)
    for copy in copies:
        copy.wait()
    nodes = mail.shape[1]
    lines = nodes // LANES

    def out_copy(step):
        part = pl.ds(step * (BLOCK // LANES), BLOCK // LANES)
        return pltpu.make_async_copy(mem_grad.at[:, part, :], grad_out.at[:, part, :], out_sems.at[step])

    def block(step, d_all):
        start = pl.multiple_of(step * BLOCK, BLOCK)
        for i in range(BLOCK // LANES):
            at = slice(i * LANES, i * LANES + LANES)
            there = pl.ds(pl.multiple_of(start + i * LANES, LANES), LANES)
            d = placed[there, :].T[:PAD]
            dn = d * factors[2, :, there]
            for part, value in enumerate(
                (d * factors[0, :, there], d * factors[1, :, there], dn, dn * factors[3, :, there], d)
            ):
                d_all[PAD * part : PAD * part + PAD, at] = value.astype(BF16)
        gates, dlow = d_all[0 : 4 * PAD, :], d_all[4 * PAD :, :]
        there = pl.ds(start, BLOCK)
        a_mail[:, :MAIL] += dot(gates[:GATES], mail[:, there], 1, 1)
        a_two[:, : 2 * PAD] += dot(gates, two[:, there], 1, 1)
        a_feat[:, :NFEAT] += dot(dlow, feat[:, there], 1, 1)
        direct = dlow.astype(F32) * factors[4, :, there].astype(F32) + dot(w_hid[...], gates, 0, 0)
        for i in range(BLOCK // LANES):
            line = pl.ds(step * (BLOCK // LANES) + i, MEM, stride=lines)
            mem_grad.reshape(MEM * lines, LANES)[line, :] = direct[:MEM, i * LANES : i * LANES + LANES]
        out_copy(step).start()

    def two_blocks(i, carry):
        block(2 * i, d_one)
        block(2 * i + 1, d_two)
        return carry

    lax.fori_loop(0, nodes // BLOCK // 2, two_blocks, 0)

    def turned_back(block):
        return jnp.concatenate([block, jnp.zeros((LANES - PAD, block.shape[1]), F32)], 0).T

    grads[ROW_Q:GRU_ROWS, :] = jnp.zeros((GRU_ROWS - ROW_Q, LANES), F32)
    lines_of = []
    for g in range(3):
        rows = slice(PAD * g, PAD * g + PAD)
        grads[pl.ds(g, MAIL, stride=3), :] = turned_back(a_mail[rows, :])[:MAIL]
        both = turned_back(a_two[rows, :])
        grads[pl.ds(3 * MAIL + g, TENC, stride=3), :] = both[:TENC]
        lines_of.append(both[MEM : MEM + 1])
        if g == 2:
            both = turned_back(a_two[GATES:, :])
        wide[0 : 2 * LANES, :] = both
        grads[pl.ds(ROW_HH + g, MEM, stride=3), :] = wide[PAD : PAD + MEM, :]
    hidden_bias = wide[PAD + MEM : PAD + MEM + 1, :]
    grads[ROW_NF:ROW_Q, :] = turned_back(a_feat[...])[:NFEAT]
    sums = lines_of + lines_of[:2] + [hidden_bias]
    biases[...] = jnp.concatenate(sums + [jnp.zeros((2, LANES), F32)], 0)

    def settle(step, carry):
        out_copy(step).wait()
        return carry

    lax.fori_loop(0, nodes // BLOCK, settle, 0)


def gru_backward(index, got, factors, mail, phi, low, feat, wts):
    rows = mail.shape[1]
    return pl.pallas_call(
        gru_back_kernel,
        out_shape=(
            jax.ShapeDtypeStruct((GRU_ROWS, LANES), F32),
            jax.ShapeDtypeStruct((8, LANES), F32),
            jax.ShapeDtypeStruct((MEM, rows // LANES, LANES), F32),
        ),
        in_specs=[SMEM, VMEM, VMEM] + [HBM] * 5,
        out_specs=(VMEM, VMEM, HBM),
        scratch_shapes=[
            pltpu.VMEM((5, PAD, rows), BF16),
            pltpu.VMEM((MAIL, rows), BF16),
            pltpu.VMEM((2 * PAD, rows), BF16),
            pltpu.VMEM((NFEAT, rows), BF16),
            pltpu.VMEM((MEM, rows // LANES, LANES), F32),
            pltpu.VMEM((got.shape[0] * got.shape[2], LANES), F32),
            pltpu.VMEM((rows, LANES), F32),
            pltpu.VMEM((5 * PAD, BLOCK), BF16),
            pltpu.VMEM((5 * PAD, BLOCK), BF16),
            pltpu.VMEM((GATES, 512), F32),
            pltpu.VMEM((4 * PAD, 256), F32),
            pltpu.VMEM((PAD, 512), F32),
            pltpu.SemaphoreType.DMA((5,)),
            pltpu.SemaphoreType.DMA((rows // BLOCK,)),
        ],
        compiler_params=params_of(),
        cost_estimate=pl.CostEstimate(flops=5_000_000_000, bytes_accessed=36_000_000, transcendentals=0),
    )(index, got, wts[2], factors, mail, phi, low, feat)


def attention_kernel(
    index,
    got,
    e0,
    e1,
    e2,
    p0,
    p1,
    p2,
    weight,
    kv_e,
    att_wts,
    cols,
    sent,
    grads,
    losses,
    table,
    kv,
    d_rows,
    d_two,
    a_kvh,
    a_kve,
    a_kvt,
    a_qh,
    a_q1,
    a_oa,
    a_oh,
    a_src,
    a_dst,
    a_col,
    a_one,
    *rest,
):
    lanes, picks = rest[:STREAMS], rest[STREAMS:]
    step = pl.program_id(0)
    kv_h, kv_t = att_wts.at[0:KV, :], att_wts.at[KV : 2 * KV, 0:TENC]
    q_h, o_att, o_att_n, o_h, src_t, src_n, dst_t, dst_n = (
        att_wts.at[2 * KV + PAD * i : 2 * KV + PAD * i + PAD, 0 : LANES if i in (0, 3) else PAD]
        for i in range(8)
    )
    near = NBR * SECT
    total = near + SECT
    scale = 50 ** (-0.5)
    sums = (a_kvh, a_kve, a_kvt, a_qh, a_q1, a_oa, a_oh, a_src, a_dst, a_col, a_one)

    @pl.when(step == 0)
    def _():
        turn_into(got, table)
        for ref in sums + lanes:
            ref[...] = jnp.zeros_like(ref)

    at_block = step * total
    gather_loop(index, table, picks[NBR], SECT, at_block + near)
    gather_loop(index, table, picks[0], SECT, at_block)
    roots = picks[NBR][...]

    def edge_of(k):
        return jnp.concatenate([e0[k], e1[k], e2[k]], 1)

    def code_of(k):
        return jnp.concatenate([p0[k], p1[k], p2[k]], 1)

    for k in range(NBR):
        kv[k] = (
            dot(kv_h[...], picks[k][...], 1, 1)
            + dot(kv_e[...], edge_of(k))
            + dot(kv_t[...], code_of(k))
        )
        if k + 1 < NBR:
            for g in range(SECT // 16):
                first = (k + 1) * SECT + g * 16
                rows = [table[pl.ds(index[at_block + first + u], 1), :] for u in range(16)]
                picks[k + 1][g * 16 : g * 16 + 16, :] = jnp.concatenate(rows, 0).astype(BF16)
    query = dot(q_h[...], roots, 1, 1)
    o_root = dot(o_h[...], roots, 1, 1)
    bo, gain, shift, bpred, wout = (cols[i] for i in range(5))
    bout = cols[5, 0:1, :]
    real = row_of((PAD, LANES)) < MEM
    queries, probs, atts, pres, embs, norms = [], [], [], [], [], []
    for t in range(3):
        at = slice(t * EB, t * EB + EB)
        q = query[:, at] + cols[6]
        scores = [[], []]
        for k in range(NBR):
            both = q * kv[k, 0:PAD, at]
            for h in range(2):
                scores[h].append(jnp.sum(both[h * HALF : h * HALF + HALF], 0, keepdims=True) * scale)
        weights = []
        for h in range(2):
            top = functools.reduce(jnp.maximum, scores[h])
            parts = [jnp.exp(x - top) for x in scores[h]]
            whole = functools.reduce(jnp.add, parts)
            weights.append([x / whole for x in parts])
        heads = []
        for h in range(2):
            rows = slice(PAD + h * HALF, PAD + h * HALF + HALF)
            heads.append(
                functools.reduce(jnp.add, [weights[h][k] * kv[k, rows, at] for k in range(NBR)])
            )
        att = jnp.concatenate(heads, 0).astype(BF16)
        pre = dot(o_att[...], att) + o_root[:, at] + bo
        active = gelu(pre)
        mean = jnp.sum(active, 0, keepdims=True) * (1.0 / MEM)
        centre = jnp.where(real, active - mean, 0.0)
        spread = jnp.sum(centre * centre, 0, keepdims=True) * (1.0 / MEM)
        inverse = lax.rsqrt(spread + 1e-05)
        hat = centre * inverse
        queries.append(q)
        probs.append(weights)
        atts.append(att)
        pres.append(pre)
        norms.append((hat, inverse))
        embs.append((hat * gain + shift).astype(BF16))

    src_proj = dot(src_t[...], embs[0]) + bpred
    tails = [src_proj + dot(dst_t[...], embs[1]), src_proj + dot(dst_t[...], embs[2])]
    acts = [gelu(x).astype(BF16) for x in tails]
    logits = [jnp.sum(x.astype(F32) * wout, 0, keepdims=True) + bout for x in acts]
    neg_weight = weight[...].astype(F32)

    def softplus(x):
        return jnp.maximum(x, 0.0) + jnp.log1p(jnp.exp(-jnp.abs(x)))

    d_pos = -sigmoid(-logits[0])
    d_neg = neg_weight * sigmoid(logits[1])
    a_one[0:1, :] += softplus(-logits[0]) + neg_weight * softplus(logits[1])
    a_one[1:2, :] += 1.0 + neg_weight
    a_one[2:3, :] += d_pos + d_neg
    d_logits = [x.astype(BF16).astype(F32) for x in (d_pos, d_neg)]
    a_col[4] += acts[0].astype(F32) * d_logits[0] + acts[1].astype(F32) * d_logits[1]
    d_tails = [wout * d * gelu_slope(x) for d, x in zip(d_logits, tails)]
    d_src = d_tails[0] + d_tails[1]
    a_col[3] += d_src
    d_low = [x.astype(BF16) for x in (d_src, d_tails[0], d_tails[1])]
    a_src[...] += dot(embs[0], d_low[0], 1, 1)
    a_dst[...] += dot(embs[1], d_low[1], 1, 1) + dot(embs[2], d_low[2], 1, 1)
    d_embs = [dot(src_n[...], d_low[0]), dot(dst_n[...], d_low[1]), dot(dst_n[...], d_low[2])]

    d_outs, d_queries = [], []
    for t in range(3):
        at = slice(t * EB, t * EB + EB)
        hat, inverse = norms[t]
        d_emb = d_embs[t]
        a_col[1] += d_emb * hat
        a_col[2] += d_emb
        d_hat = d_emb * gain
        mean = jnp.sum(d_hat, 0, keepdims=True) * (1.0 / MEM)
        mixed = jnp.sum(d_hat * hat, 0, keepdims=True) * (1.0 / MEM)
        d_active = jnp.where(real, inverse * (d_hat - mean - hat * mixed), 0.0)
        d_out = d_active * gelu_slope(pres[t])
        a_col[0] += d_out
        d_out_low = d_out.astype(BF16)
        d_outs.append(d_out_low)
        a_oa[...] += dot(d_out_low, atts[t], 1, 1)
        d_att = dot(o_att_n[...], d_out_low)
        q = queries[t]
        d_q = jnp.zeros((PAD, EB), F32)
        slopes = [[], []]
        for h in range(2):
            rows = slice(PAD + h * HALF, PAD + h * HALF + HALF)
            d_head = d_att[h * HALF : h * HALF + HALF]
            dp = [jnp.sum(d_head * kv[k, rows, at], 0, keepdims=True) for k in range(NBR)]
            mid = functools.reduce(jnp.add, [a * b for a, b in zip(dp, probs[t][h])])
            slopes[h] = [probs[t][h][k] * (dp[k] - mid) * scale for k in range(NBR)]
        for k in range(NBR):
            keys = kv[k, 0:PAD, at]
            factor = jnp.concatenate(
                [jnp.broadcast_to(slopes[h][k], (HALF, EB)) for h in range(2)], 0
            )
            share = jnp.concatenate(
                [jnp.broadcast_to(probs[t][h][k], (HALF, EB)) for h in range(2)], 0
            )
            d_q = d_q + factor * keys
            kv[k, 0:PAD, at] = factor * q
            kv[k, PAD:KV, at] = share * d_att
        d_queries.append(d_q)
        a_q1[...] += d_q.astype(BF16).astype(F32)

    d_out_all = jnp.concatenate(d_outs, 1)
    d_q_all = jnp.concatenate(d_queries, 1).astype(BF16)
    a_oh[...] += dot(d_out_all, roots)
    a_qh[...] += dot(d_q_all, roots)
    d_rows[...] = dot(d_out_all, o_h[...], 0, 0) + dot(d_q_all, q_h[...], 0, 0)
    base = step * total
    each = SECT // STREAMS

    def add_rows(first, ref):
        for u in range(each):
            for s in range(STREAMS):
                at = s * each + u
                to = pl.ds(index[first + at], 1)
                lanes[s][to, :] += ref[at : at + 1, :]

    for k in range(NBR):
        mine, other = (d_two, d_rows) if k % 2 == 0 else (d_rows, d_two)
        d_kv = kv[k].astype(BF16)
        a_kvh[...] += dot(d_kv, picks[k][...])
        a_kve[:, :EDGE] += dot(d_kv, edge_of(k), 1, 1)
        a_kvt[:, :TENC] += dot(d_kv, code_of(k), 1, 1)
        mine[...] = dot(d_kv, kv_h[...], 0, 0)
        add_rows(base + (NBR if k == 0 else k - 1) * SECT, other)
    add_rows(base + (NBR - 1) * SECT, d_rows)

    @pl.when(step == pl.num_programs(0) - 1)
    def _():
        slots = sent.shape[2]
        pieces = slots // LANES

        def finish(j, carry):
            owner = j // pieces
            to = pl.ds(pl.multiple_of((j - owner * pieces) * LANES, LANES), LANES)
            at = pl.ds(pl.multiple_of(j * LANES, LANES), LANES)
            whole = functools.reduce(jnp.add, [ref[at, :] for ref in lanes])
            sent[owner, :, to] = jnp.where(lane_of((LANES, LANES)) < MEM, whole, 0.0).T[:WIRE].astype(BF16)
            return carry

        lax.fori_loop(0, sent.shape[0] * pieces, finish, 0, unroll=4)
        base_row = ATT_BASE

        def turned(block):
            short = -block.shape[0] % LANES
            if short:
                block = jnp.concatenate([block, jnp.zeros((short, block.shape[1]), F32)], 0)
            return block.T

        grads[...] = jnp.zeros_like(grads)
        q = ROW_Q - base_row
        grads[q : q + 100, :] = join_heads(turned(a_qh[...]))[:100]
        ones = jnp.sum(turned(a_q1[...]), 0, keepdims=True)
        grads[q + 100 : q + 200, :] = jnp.broadcast_to(join_heads(ones), (100, LANES))
        for part in range(2):
            rows = slice(PAD * part, PAD * part + PAD)
            start = ROW_KV - base_row + part
            grads[pl.ds(start, MEM, stride=2), :] = join_heads(turned(a_kvh[rows, :]))[:MEM]
            grads[pl.ds(start + 2 * MEM, EDGE, stride=2), :] = join_heads(turned(a_kve[rows, :]))[:EDGE]
            grads[pl.ds(start + 2 * (MEM + EDGE), TENC, stride=2), :] = join_heads(
                turned(a_kvt[rows, :])
            )[:TENC]
        o = ROW_O - base_row
        wide = jnp.concatenate([a_oa[...], jnp.zeros((PAD, LANES - PAD), F32)], 1)
        grads[o : o + 100, :] = turned(join_heads(wide))[:100]
        grads[o + 100 : o + 200, :] = turned(a_oh[...])[:100]
        for start, ref in ((ROW_SRC, a_src), (ROW_DST, a_dst)):
            wide = jnp.concatenate([ref[...], jnp.zeros((PAD, LANES - PAD), F32)], 1)
            grads[start - base_row : start - base_row + 100, :] = wide[:100]
        for i, r in enumerate((ROW_BO, ROW_GAIN, ROW_SHIFT, ROW_BPRED, ROW_OUT)):
            line = jnp.sum(turned(a_col[i]), 0, keepdims=True)
            grads[r - base_row : r - base_row + 1, :] = line
        line = jnp.where(
            lane_of((1, LANES)) == 0, jnp.sum(a_one[2:3, :], 1, keepdims=True), 0.0
        )
        grads[ROW_BOUT - base_row : ROW_BOUT - base_row + 1, :] = line
        losses[...] = jnp.broadcast_to(jnp.sum(a_one[...], 1, keepdims=True), (8, LANES))


def attention(index, got, edges, codes, weight, wts):
    roots = edges.shape[2]
    blocks = roots // SECT

    def section(rows, t):
        return pl.BlockSpec((NBR, rows, EB), lambda b: (0, 0, t * blocks + b))

    slots = got.shape[0] * got.shape[2]
    total = (NBR + 1) * SECT
    return pl.pallas_call(
        attention_kernel,
        grid=(blocks,),
        out_shape=(
            jax.ShapeDtypeStruct(got.shape, BF16),
            jax.ShapeDtypeStruct((ATT_ROWS, LANES), F32),
            jax.ShapeDtypeStruct((8, LANES), F32),
        ),
        in_specs=[SMEM, VMEM]
        + [section(EDGE, t) for t in range(3)]
        + [section(TENC, t) for t in range(3)]
        + [pl.BlockSpec((1, EB), lambda b: (0, b))]
        + [VMEM] * 3,
        out_specs=(VMEM, VMEM, VMEM),
        scratch_shapes=[
            pltpu.VMEM((slots, LANES), F32),
            pltpu.VMEM((NBR, KV, SECT), F32),
            pltpu.VMEM((SECT, LANES), F32),
            pltpu.VMEM((SECT, LANES), F32),
            pltpu.VMEM((KV, LANES), F32),
            pltpu.VMEM((KV, 256), F32),
            pltpu.VMEM((KV, LANES), F32),
            pltpu.VMEM((PAD, LANES), F32),
            pltpu.VMEM((PAD, LANES), F32),
            pltpu.VMEM((PAD, PAD), F32),
            pltpu.VMEM((PAD, LANES), F32),
            pltpu.VMEM((PAD, PAD), F32),
            pltpu.VMEM((PAD, PAD), F32),
            pltpu.VMEM((5, PAD, LANES), F32),
            pltpu.VMEM((8, LANES), F32),
        ]
        + [pltpu.VMEM((slots, LANES), F32) for _ in range(STREAMS)]
        + [pltpu.VMEM((SECT, LANES), BF16) for _ in range(NBR + 1)],
        compiler_params=params_of(),
        cost_estimate=pl.CostEstimate(flops=9_000_000_000, bytes_accessed=20_000_000, transcendentals=1_000_000),
    )(index, got, edges, edges, edges, codes, codes, codes, weight, *wts[3:])


def pack_kernel(gru, bias, att, losses, out, rows):
    rows[0:GRU_ROWS, :] = gru[...]
    rows[GRU_ROWS : ATT_BASE + ATT_ROWS, :] = att[8:, :]
    rows[ATT_BASE:GRU_ROWS, :] += att[0:8, :]
    rows[ROW_BIH : ROW_BIH + 8, :] += bias[...]
    rows[ATT_BASE + ATT_ROWS :, :] = jnp.zeros((rows.shape[0] - ATT_BASE - ATT_ROWS, LANES), F32)
    lane = lane_of((PERIODS, LANES))
    for m in range(25):
        first, shift = divmod(LANES * m, 100)
        value = None
        filled = 0
        source = first
        while filled < LANES:
            amount = shift if filled == 0 else -filled
            block = roll_left(rows[pl.ds(source, PERIODS, stride=32), :], amount)
            value = block if value is None else jnp.where(lane < filled, value, block)
            filled += 100 - (shift if filled == 0 else 0)
            source += 1
        out[pl.ds(m, PERIODS, stride=25), :] = value
    first, at = divmod(USED, LANES)
    tail = out.shape[0] - first
    where = row_of((tail, LANES)) * LANES + lane_of((tail, LANES))
    value = jnp.where(where < at, out[first:, :], 0.0)
    value = jnp.where(where == at, losses[0:1, :], value)
    value = jnp.where(where == at + 1, losses[1:2, :], value)
    out[first:, :] = value


def pack(gru, bias, att, losses):
    return pl.pallas_call(
        pack_kernel,
        out_shape=jax.ShapeDtypeStruct((25 * PERIODS + 7, LANES), F32),
        in_specs=[VMEM] * 4,
        out_specs=VMEM,
        scratch_shapes=[pltpu.VMEM((WROWS + 8, LANES), F32)],
        compiler_params=params_of(16 * 2**20),
        cost_estimate=pl.CostEstimate(flops=2_000_000, bytes_accessed=4_000_000, transcendentals=0),
    )(gru, bias, att, losses)


NODES = 2048


def each_message(starts, sender, body_of):
    first, end = starts[2 * sender], starts[2 * sender + 1]

    def move(i, carry):
        for u in range(8):
            body_of(jnp.minimum(first + i * 8 + u, end - 1))
        return carry

    lax.fori_loop(0, (end - first + 7) // 8, move, 0)


def after_first(count):
    return pl.BlockSpec((count, NODES), lambda i: (0, jnp.maximum(i - 1, 0)))


def edge_kernel(
    starts, rows, events, edges, stamps, own, mailbox, mail_time, mail_new, time_new, stage, far, kept, lines
):
    step = pl.program_id(0)

    @pl.when(step == 0)
    def _():
        kept[1] = jnp.zeros(kept.shape[1:], F32)
        stage[...] = jnp.zeros_like(stage)
        stage[EDGE + 1 : EDGE + 2, :] = jnp.ones((1, EV), F32)

        def sender(s, carry):
            stage[0:EDGE, :] = edges[s].astype(F32)
            stage[EDGE : EDGE + 1, :] = stamps[s].astype(F32)
            for part in range(2):
                far[part] = stage[LANES * part : LANES * part + LANES, :].T

            def one(i):
                place = s * 2 * EV + i
                to = pl.ds(rows[place], 1)
                event = pl.ds(events[place], 1)
                kept[0, to, :] = far[0, event, :]
                kept[1, to, :] = far[1, event, :]

            each_message(starts, s, one)
            return carry

        lax.fori_loop(0, edges.shape[0], sender, 0)

    @pl.when(step > 0)
    def _():
        at = pl.ds(pl.multiple_of((step - 1) * NODES, LANES), NODES)
        last = kept[1, at, :].T
        stamp = EDGE - LANES
        has = last[stamp + 1 : stamp + 2, :] > 0.5
        lines[0:MEM, :] = own[...].astype(F32)
        lines[2 * MEM : 2 * MEM + LANES, :] = kept[0, at, :].T
        lines[2 * MEM + LANES : MAIL, :] = last[0:stamp]
        mail_new[...] = jnp.where(has, lines[0:MAIL, :], mailbox[...].astype(F32)).astype(BF16)
        time_new[...] = jnp.where(has, last[stamp : stamp + 1, :].astype(jnp.int32), mail_time[...])


def deliver_edges(starts, rows, events, edges, stamps, own, mailbox, mail_time):
    nodes = mailbox.shape[1]
    return pl.pallas_call(
        edge_kernel,
        grid=(1 + nodes // NODES,),
        out_shape=(
            jax.ShapeDtypeStruct((MAIL, nodes), BF16),
            jax.ShapeDtypeStruct((1, nodes), jnp.int32),
        ),
        in_specs=[SMEM, SMEM, SMEM, VMEM, VMEM]
        + [after_first(MEM), after_first(MAIL), after_first(1)],
        out_specs=(after_first(MAIL), after_first(1)),
        scratch_shapes=[
            pltpu.VMEM((2 * LANES, EV), F32),
            pltpu.VMEM((2, EV, LANES), F32),
            pltpu.VMEM((2, nodes, LANES), F32),
            pltpu.VMEM((MAIL + 6, NODES), F32),
        ],
        compiler_params=params_of(),
        cost_estimate=pl.CostEstimate(flops=20_000_000, bytes_accessed=16_000_000, transcendentals=0),
    )(starts, rows, events, edges, stamps, own, mailbox, mail_time)


def partner_into_kernel(starts, rows, partner, mailbox, mail_new, near, kept, lines):
    step = pl.program_id(0)

    @pl.when(step == 0)
    def _():
        kept[...] = jnp.zeros_like(kept)
        short = jnp.zeros((LANES - WIRE, LANES), F32)

        def sender(s, carry):
            for i in range(2 * EV // LANES):
                at = slice(i * LANES, i * LANES + LANES)
                near[at, :] = jnp.concatenate([partner[s, :, at].astype(F32), short], 0).T

            def one(i):
                kept[pl.ds(rows[s * 2 * EV + i], 1), :] = near[pl.ds(i, 1), :]

            each_message(starts, s, one)
            return carry

        lax.fori_loop(0, partner.shape[0], sender, 0)

    @pl.when(step > 0)
    def _():
        at = pl.ds(pl.multiple_of((step - 1) * NODES, LANES), NODES)
        turned = kept[at, :].T
        has = turned[MEM : MEM + 1, :] > 0.5
        lines[...] = mailbox[...].astype(F32)
        lines[MEM : 2 * MEM, :] = jnp.where(has, turned[0:MEM], lines[MEM : 2 * MEM, :])
        mail_new[...] = lines[...].astype(BF16)


def deliver_partners(starts, rows, partner, mailbox):
    nodes = mailbox.shape[1]
    upper = 208
    return pl.pallas_call(
        partner_into_kernel,
        grid=(1 + nodes // NODES,),
        out_shape=jax.ShapeDtypeStruct((MAIL, nodes), BF16),
        in_specs=[SMEM, SMEM, VMEM, after_first(upper)],
        out_specs=after_first(upper),
        scratch_shapes=[
            pltpu.VMEM((2 * EV, LANES), F32),
            pltpu.VMEM((nodes, LANES), F32),
            pltpu.VMEM((upper, NODES), F32),
        ],
        input_output_aliases={3: 0},
        compiler_params=params_of(),
        cost_estimate=pl.CostEstimate(flops=10_000_000, bytes_accessed=8_000_000, transcendentals=0),
    )(starts, rows, partner, mailbox)


def flip(x, axis, mask):
    return lax.ppermute(x, axis, [(i, i ^ mask) for i in range(lax.axis_size(axis))])


def rounds():
    table = []
    low, count = 2, lax.axis_size("node")
    while low < count:
        size = min(4, count // low)
        table.append(("node", low, size))
        low *= size
    table.append(("batch", 1, lax.axis_size("batch")))
    table.append(("node", 1, 2))
    return table


def place_in(axis, low, size):
    return (lax.axis_index(axis) // low) % size


def tree_sum(parts):
    while len(parts) > 1:
        parts = [a + b for a, b in zip(parts[::2], parts[1::2])]
    return parts[0]


def gather_first(x, lines, between):
    grown = [[x, []], [lines, []]]

    def grow(entry, key, here, parts):
        x, axes = entry
        at = sum(1 for k in axes if k < key)
        axes.append(key)
        axes.sort()
        out = jnp.zeros(x.shape[:at] + (len(parts),) + x.shape[at:], x.dtype)
        for m, part in enumerate(parts):
            to = jnp.bitwise_xor(here, m)
            out = lax.dynamic_update_slice_in_dim(out, jnp.expand_dims(part, at), to, at)
        entry[0] = out

    for number, (axis, low, size) in enumerate(rounds()):
        here = place_in(axis, low, size)
        key = (axis == "node", -low)
        x, lines = grown[0][0], grown[1][0]
        if number == 0:
            both = jnp.concatenate([x, lines], 0)
            got = [flip(both, axis, low * m) for m in range(1, size)]
            parts = [x] + [g[: x.shape[0]] for g in got]
            others = [lines] + [g[x.shape[0] :] for g in got]
        else:
            parts = [x] + [flip(x, axis, low * m) for m in range(1, size)]
            others = [lines] + [flip(lines, axis, low * m) for m in range(1, size)] if axis == "node" else None
        parts = between(number, x, parts)
        grow(grown[0], key, here, parts)
        if others is not None:
            grow(grown[1], key, here, others)
    return [g[0] for g in grown]


def scatter_sum(x, between):
    table = rounds()
    dims = sorted(((axis == "node", -low), size) for axis, low, size in table)
    keys = [k for k, _ in dims]
    x = x.reshape(tuple(n for _, n in dims) + (-1, LANES))
    for number, (axis, low, size) in enumerate(table[::-1]):
        at = keys.index((axis == "node", -low))
        here = place_in(axis, low, size)

        def part(m, x=x, at=at, here=here):
            return lax.dynamic_slice_in_dim(x, jnp.bitwise_xor(here, m), 1, at)

        away = [flip(part(m), axis, low * m) for m in range(1, size)]
        away = between(number, x, away)
        x = tree_sum([part(0)] + list(away))
    return x.reshape(-1, LANES)


def sum_all(x):
    for axis, low, size in rounds()[::-1]:
        x = tree_sum([x] + [flip(x, axis, low * m) for m in range(1, size)])
    return x


def after(x, *others):
    return lax.optimization_barrier((x,) + others)[0]


def swap(x):
    return lax.all_to_all(x, "node", split_axis=0, concat_axis=0, tiled=True)


def to_slot(live, counts, slots):
    upper = jnp.cumsum(counts)
    shape = (-1,) + (1,) * live.ndim
    passed = live[None] >= upper.reshape(shape)
    return live + jnp.sum(jnp.where(passed, (slots - counts).reshape(shape), 0), 0)


def body(
    params,
    moment1,
    moment2,
    memory,
    mailbox,
    mail_time,
    update_time,
    node_feat,
    req_rows,
    req_count,
    root_live,
    nbr_live,
    nbr_dt,
    nbr_edge,
    ev_edge,
    ev_time,
    neg_count,
):
    shards = lax.axis_size("node")
    me = lax.axis_index("node")
    slots = req_rows.shape[3]
    wanted = req_rows[0, 0]
    counts = req_count[0, 0]
    rows = memory.shape[1]
    mem_cols = jnp.transpose(memory.reshape(rows // LANES, LANES, MEM), (2, 0, 1))
    mail_cols = mailbox[0].T
    feat_cols = node_feat.T
    edge_cols = jnp.transpose(nbr_edge[0, 0], (1, 2, 0))

    dead = jnp.arange(slots, dtype=jnp.int32)[None, :] >= counts[:, None]
    wanted_or_dead = wanted + rows * dead.astype(jnp.int32)

    near_slot = to_slot(nbr_live[0, 0].T, counts, slots)
    root_slot = to_slot(root_live[0, 0], counts, slots)
    blocks = EV // EB
    near_index = jnp.transpose(near_slot.reshape(NBR, 3, blocks, EB), (2, 0, 1, 3))
    root_index = jnp.transpose(root_slot.reshape(3, blocks, EB), (1, 0, 2))
    index = jnp.concatenate(
        [near_index.reshape(blocks, -1), root_index.reshape(blocks, -1)], 1
    ).reshape(-1)

    edge_sent = ev_edge[0, 0].T
    early = {}

    last = len(rounds()) - 1

    def between(number, x, parts):
        if number == last - 1:
            edges = after(edge_sent, x)
            early["edges"] = swap(jnp.broadcast_to(edges, (shards,) + edges.shape))
            early["codes"] = time_codes(after(mail_time - update_time, x), PAD)
            *parts, early["codes"] = lax.optimization_barrier((*parts, early["codes"]))
        return parts

    digits = jnp.stack([wanted_or_dead // 128, wanted_or_dead % 128]).astype(BF16)
    flat, asked = gather_first(
        params.astype(BF16).reshape(-1, LANES), digits.reshape(-1, LANES), between
    )
    flat = flat.reshape(-1, LANES)
    asked = asked.reshape(shards, 2, shards, slots)
    asked = lax.dynamic_slice_in_dim(asked, me, 1, 2).astype(F32).astype(jnp.int32)
    asked = (asked[:, 0] * 128 + asked[:, 1]).reshape(-1)
    alive = asked < rows
    asked = asked % rows
    codes_m = early["codes"][0]
    wts, h_sent, low, s_cols = gru_forward(asked, flat, mail_cols, codes_m, mem_cols, feat_cols, shards, slots)
    h_got = swap(h_sent)

    codes_n = time_codes(nbr_dt[0, 0].T)
    edges_all = early["edges"]
    ends = root_slot[:2].reshape(-1)
    ordered = lax.sort(ends * (2 * EV) + jnp.arange(2 * EV, dtype=jnp.int32))
    end_row, partner_slot, event = bookkeeping(ordered, ends, wanted.reshape(-1))
    first = jnp.sum(
        (ordered[None, :] < (jnp.arange(LANES, dtype=jnp.int32) * (slots * 2 * EV))[:, None]).astype(jnp.int32),
        1,
    )
    notes = jnp.concatenate([end_row, event, ev_time[0, 0], first])
    digits = jnp.concatenate([notes // 128, notes % 128]).astype(BF16)
    lines = -(-digits.shape[0] // (8 * slots)) * 8
    digits = jnp.pad(digits, (0, lines * slots - digits.shape[0])).reshape(lines, slots)
    s_sent = send_rows(s_cols, asked, digits, shards, slots)
    h_got, s_sent, codes_n, edges_all, partner_slot, index = lax.optimization_barrier(
        (h_got, s_sent, codes_n, edges_all, partner_slot, index)
    )
    s_got = swap(s_sent)
    d_sent, att_grads, losses = attention(index, h_got, edge_cols, codes_n, neg_count[0], wts)
    d_sent, s_got, low = lax.optimization_barrier((d_sent, s_got, low))
    d_got = swap(d_sent)

    upper = (jnp.arange(rows // LANES, dtype=jnp.int32)[:, None] == (asked // LANES)[None, :]) & alive[None, :]
    lower = (asked % LANES)[:, None] == jnp.arange(LANES, dtype=jnp.int32)[None, :]
    live = dot(upper.astype(BF16), lower.astype(BF16)).reshape(1, rows)
    factors, mem_new, upd_new = gru_factors(
        mail_cols, codes_m, low, mem_cols, live, mail_time, update_time, wts
    )
    partner = partner_rows(s_got, partner_slot, shards)
    digits = s_got[:, WIRE:, :].reshape(shards, -1)[:, : 2 * notes.shape[0]].astype(F32).astype(jnp.int32)
    notes = digits[:, : notes.shape[0]] * 128 + digits[:, notes.shape[0] :]
    stamps = notes[:, 4 * EV : 5 * EV].reshape(shards, 1, EV)
    events_of = notes[:, 2 * EV : 4 * EV].reshape(-1)
    rows_of = notes[:, : 2 * EV].reshape(-1)
    starts = lax.dynamic_slice_in_dim(notes[:, 5 * EV :], me, 2, 1).reshape(-1)
    mail_new, stamp_new = deliver_edges(
        starts, rows_of, events_of, edges_all, stamps, s_cols, mail_cols, mail_time
    )
    d_got, factors, partner, mail_new, starts, rows_of = lax.optimization_barrier(
        (d_got, factors, partner, mail_new, starts, rows_of)
    )
    partner_got = swap(partner)
    gru_grads, bias_grads, mem_grad = gru_backward(
        asked, d_got, factors, mail_cols, codes_m, low, feat_cols, wts
    )
    packed = pack(gru_grads, bias_grads, att_grads, losses)[:FLAT_ROWS]
    late = {}

    def during(number, x, parts):
        if number == 1:
            mail = deliver_partners(starts, rows_of, after(partner_got, x), mail_new)
            *parts, late["mail"] = lax.optimization_barrier((*parts, mail))
        return parts

    shard = scatter_sum(packed, during)
    mail_new = late["mail"]

    number = lax.axis_index("batch") * shards + me
    size = shard.shape[0] * LANES
    place = number * size + jnp.arange(size, dtype=jnp.int32).reshape(-1, LANES)
    grad = jnp.where(place < USED, shard, 0.0)
    lines = [
        jnp.sum(grad * grad, 0, keepdims=True),
        jnp.sum(jnp.where(place == USED, shard, 0.0), 0, keepdims=True),
        jnp.sum(jnp.where(place == USED + 1, shard, 0.0), 0, keepdims=True),
        jnp.zeros((5, LANES), F32),
    ]
    values = jnp.sum(sum_all(jnp.concatenate(lines, 0)), 1)
    grad_norm = jnp.sqrt(values[0])
    clipped = grad.reshape(-1) * jnp.minimum(1.0, clip_limit / (grad_norm + 1e-06))
    moment1_new = beta_first * moment1 + (1.0 - beta_first) * clipped
    moment2_new = beta_second * moment2 + (1.0 - beta_second) * clipped * clipped
    ratio = (
        moment1_new
        / (1.0 - beta_first**STEP)
        / (jnp.sqrt(moment2_new / (1.0 - beta_second**STEP)) + adam_floor)
    )
    params_new = params - learn_rate * (ratio + decay_rate * params)
    return (
        values[1],
        values[2],
        grad_norm,
        params_new,
        moment1_new,
        moment2_new,
        params_new.astype(BF16),
        jnp.transpose(mem_new, (1, 2, 0)).reshape(memory.shape),
        mail_new.T[None],
        stamp_new,
        upd_new,
        jnp.transpose(mem_grad, (1, 2, 0)).reshape(memory.shape),
    )


def solution(mesh):
    both, split = P(("batch", "node")), P("batch", "node")
    in_specs = (both, both, both, split, split, split, split, P("node")) + (split,) * 9
    out_specs = (P(), P(), P()) + (both,) * 4 + (split,) * 5
    return jax.shard_map(body, mesh=mesh, in_specs=in_specs, out_specs=out_specs, check_vma=False)
```
